32 devices in a mesh: groups: 2 (over y), gx: 4 (over z), gy: 2 (over x), gz: 2 (over core).
Axes of the slice: x: 2, y: 2, z: 4, core: 2. Of those that a mesh axis runs over, the one named last changes fastest.
Arguments:
- positions: float32 [3, 8, 2, 64], P(None, ('groups', 'gx'), 'gy'), parts along dimension 1, may hold values from 0 to 20
- species: int32 [8, 2, 64], P(('groups', 'gx'), 'gy'), parts along dimension 0, may hold values from 0 to 4
- centers: int32 [8, 2, 1024], P(('groups', 'gx'), 'gy'), parts along dimension 0, may hold values from 0 to 63
- neighbours: int32 [8, 2, 1024], P(('groups', 'gx'), 'gy'), parts along dimension 0, may hold values from 0 to 223, as said below
- masks: int32 [8, 2, 1024], P(('groups', 'gx'), 'gy'), parts along dimension 0, may hold values from 0 to 1, as said below
- skin: int32 [8, 2, 32], P(('groups', 'gx'), 'gy'), parts along dimension 0, may hold values from 0 to 63, as said below
- embed: float32 [4, 5, 32], P('gz'), may hold values from -6 to 6
- radial: float32 [4, 8, 32], P('gz'), may hold values from -2 to 2
- w_mix: float32 [4, 2, 32, 32], P('gz'), may hold values from -1 to 1
- w_latent: float32 [4, 1, 32, 32], P('gz'), may hold values from -1 to 1
- w_update: float32 [4, 2, 32, 32], P('gz'), may hold values from -1 to 1
- readout: float32 [4, 32], P('gz'), may hold values from -1 to 1
Outputs:
- forces: float32 [4, 3, 8, 2, 64], P('gz', None, ('groups', 'gx'), 'gy'), parts along dimension 2
The draws below stay inside these ranges and needn't reach their ends.
There are 2 independent parts, one for each index of `groups`. The reference program is written for one: setup_inputs(seed, part) draws one part's arguments, and reference() takes and returns one part's arrays. A program takes and returns all parts, laid end to end along the dimension named above; an argument that names none is the same for every part. Nothing has to cross between parts.
Inputs may be any that keep to these rules, and one draw needn't show every extreme that they name: `neighbours`: each value is an own atom (below 64) or an entry of a face or corner slot of the table. `masks`: in each domain the live edge slots fill whole tiles of 128 from the first tile; at least a quarter of the 8 tiles (rounded down) are live, and domain (0, 0) has all 8 live. `skin`: 32 distinct atoms of the domain; the first 8 of them are the list that corner neighbours receive.
All inputs are finite; a program needn't handle non-finite values.
Results may differ from the reference program's by a relative error of at most 0.0003.
Values sent between devices are 32-bit elements; how exact they have to be, the bound alone decides.
No kernel may reach another device: no remote copies, remote signals or barrier semaphores. Data moves between devices by JAX's collectives and lax.ppermute only.
A program may use at most 64 MiB of HBM per device.

```python
import jax
import jax.numpy as jnp
from jax import lax

C = 32
NB = 8
NEIGH = 16
LAYERS = 2
SPECIES = 5
MEMBERS = 4
ATOMS_DEV = 64
GHOSTS = 32
CORNERS = 8
EDGES = 1024
TILES = 8
SLOTS = 224
GRID_X = 4
GRID_Y = 2


def draw_neighbours(key, part):
    key = jax.random.fold_in(key, 11)
    key_own, key_slot, key_face, key_corner, key_pick = jax.random.split(key, 5)
    shape = (GRID_X, GRID_Y, EDGES)
    own_atom = jax.random.randint(key_own, shape, 0, ATOMS_DEV)
    slot_pick = jax.random.randint(key_slot, shape, 0, 20)
    face_entry = ATOMS_DEV + slot_pick // 4 * GHOSTS + jax.random.randint(key_face, shape, 0, GHOSTS)
    corner_entry = ATOMS_DEV + 4 * GHOSTS + jnp.clip(slot_pick - 16, 0, 3) * CORNERS + jax.random.randint(key_corner, shape, 0, CORNERS)
    ghost_entry = jnp.where(slot_pick < 16, face_entry, corner_entry)
    choose_ghost = jax.random.randint(key_pick, shape, 0, 10) < 3
    return jnp.where(choose_ghost, ghost_entry, own_atom).astype(jnp.int32)


def draw_masks(key, part):
    key = jax.random.fold_in(key, 7)
    live_tiles = jax.random.randint(key, (GRID_X, GRID_Y), TILES // 4, TILES + 1)
    live_tiles = live_tiles.at[0, 0].set(TILES)
    tile_of = jnp.arange(EDGES, dtype=jnp.int32) // 128
    return (tile_of[None, None, :] < live_tiles[:, :, None]).astype(jnp.int32)


def draw_skin(key, part):
    key = jax.random.fold_in(key, 5)
    domain_keys = jax.random.split(key, GRID_X * GRID_Y)
    chosen = jax.vmap(lambda domain_key: jax.random.permutation(domain_key, ATOMS_DEV)[:GHOSTS])(domain_keys)
    return chosen.reshape(GRID_X, GRID_Y, GHOSTS).astype(jnp.int32)


def set_ends(values, key, smallest, high):
    index_at = [jax.random.randint(jax.random.fold_in(key, axis), (), 0, length) for axis, length in enumerate(values.shape)]
    widest = values.shape.index(max(values.shape))
    neighbour = index_at[:widest] + [(index_at[widest] + 1) % values.shape[widest]] + index_at[widest + 1:]
    return values.at[tuple(index_at)].set(smallest).at[tuple(neighbour)].set(high)


def block_scale(rng, dims, pieces, low, largest):
    def one(axis_at, blocks):
        steps = jax.random.uniform(jax.random.fold_in(jax.random.fold_in(rng, 6), axis_at), (blocks,), jnp.float32, low / len(pieces), largest / len(pieces))
        return jnp.repeat(jnp.exp(steps), dims[axis_at] // blocks).reshape((-1,) + (1,) * (len(dims) - axis_at - 1))

    gain = one(*pieces[0])
    for cut in pieces[1:]:
        gain = gain * one(*cut)
    return gain


def normal_values(key, shape, width, bound, cuts=(), kind=jnp.bfloat16):
    factor_of = block_scale(key, shape, cuts, -0.22, 0.18) if cuts else 1.0
    entries = jax.random.normal(key, shape, jnp.float32) * width * factor_of
    return jnp.minimum(jnp.maximum(entries, -bound), bound).astype(kind)


def setup_inputs(seed: int = 0, part: int = 0) -> dict:
    splits = jax.random.split(jax.random.key(seed), 13)
    own_keys = jax.random.split(jax.random.fold_in(splits[12], part), 13)
    positions = jnp.clip(20.0 * jax.random.uniform(own_keys[0], (3, GRID_X, GRID_Y, ATOMS_DEV), jnp.float32) ** block_scale(own_keys[0], (3, GRID_X, GRID_Y, ATOMS_DEV), ((1, 4), (2, 2)), -0.2, 0.2), 0.0, 20.0)
    species = set_ends(jax.random.randint(own_keys[1], (GRID_X, GRID_Y, ATOMS_DEV), 0, SPECIES), jax.random.fold_in(own_keys[1], 1), 0, SPECIES - 1).astype(jnp.int32)
    centers = set_ends(jax.random.randint(own_keys[2], (GRID_X, GRID_Y, EDGES), 0, ATOMS_DEV), jax.random.fold_in(own_keys[2], 1), 0, ATOMS_DEV - 1).astype(jnp.int32)
    neighbours = draw_neighbours(jax.random.fold_in(jax.random.fold_in(splits[12], part), 71), part)
    masks = draw_masks(jax.random.fold_in(jax.random.fold_in(splits[12], part), 71), part)
    skin = draw_skin(jax.random.fold_in(jax.random.fold_in(splits[12], part), 71), part)
    embed = normal_values(splits[6], (MEMBERS, SPECIES, C), 1.0, 6.0, ((0, 2),), jnp.float32)
    radial = normal_values(splits[7], (MEMBERS, NB, C), NB ** -0.5, 2.0, ((0, 2),), jnp.float32)
    w_mix = normal_values(splits[8], (MEMBERS, LAYERS, C, C), C ** -0.5, 1.0, ((0, 2),), jnp.float32)
    w_latent = normal_values(splits[9], (MEMBERS, LAYERS - 1, C, C), C ** -0.5, 1.0, ((0, 2),), jnp.float32)
    w_update = normal_values(splits[10], (MEMBERS, LAYERS, C, C), C ** -0.5, 1.0, ((0, 2),), jnp.float32)
    readout = normal_values(splits[11], (MEMBERS, C), C ** -0.5, 1.0, ((0, 2),), jnp.float32)
    return {"positions": positions, "species": species, "centers": centers, "neighbours": neighbours, "masks": masks, "skin": skin, "embed": embed, "radial": radial, "w_mix": w_mix, "w_latent": w_latent, "w_update": w_update, "readout": readout}


box_edge = 20.0
energy_scale = 16.0
highest = lax.Precision.HIGHEST
face_slots = ((0, 1), (1, 0), (1, 2), (2, 1))
corner_slots = ((0, 0), (0, 2), (2, 0), (2, 2))

def slot_offsets(ghost_count, corner_count):
    first_parts = []
    second_parts = []
    for slot_pair in face_slots:
        first_parts.append(jnp.full((ghost_count,), slot_pair[0] - 1.0, jnp.float32))
        second_parts.append(jnp.full((ghost_count,), slot_pair[1] - 1.0, jnp.float32))
    for slot_pair in corner_slots:
        first_parts.append(jnp.full((corner_count,), slot_pair[0] - 1.0, jnp.float32))
        second_parts.append(jnp.full((corner_count,), slot_pair[1] - 1.0, jnp.float32))
    first_row = jnp.concatenate(first_parts)
    return jnp.stack([first_row, jnp.concatenate(second_parts), jnp.zeros_like(first_row)])

def basis_of(distance):
    freqs = jnp.arange(NB, dtype=jnp.float32) / 4.0
    return jnp.cos(freqs[:, None] * distance[None, :]) * jnp.exp(-distance / 32.0)[None, :]

def geometry_one(pos_table, center_idx, neighbour_idx, radial_m):
    offset_vec = pos_table[:, neighbour_idx] - pos_table[:, center_idx]
    distance = jnp.sqrt(lax.optimization_barrier(jnp.sum(offset_vec * offset_vec, axis=0)) + 1.0)
    basis = basis_of(distance)
    return jax.nn.silu(jnp.dot(radial_m.T, basis, precision=highest, preferred_element_type=jnp.float32))

def advance_one(feature_table, latent, center_idx, neighbour_idx, live_edges, mix_w, update_w, latent_w):
    joined = feature_table[:, center_idx] + feature_table[:, neighbour_idx]
    mixed = latent * joined
    activated = jax.nn.silu(jnp.dot(mix_w.T, mixed, precision=highest, preferred_element_type=jnp.float32)) * live_edges[None, :]
    summed = jnp.zeros((C, ATOMS_DEV), jnp.float32).at[:, center_idx].add(activated)
    features = feature_table[:, :ATOMS_DEV] + jnp.dot(update_w.T, summed, precision=highest, preferred_element_type=jnp.float32) / NEIGH
    new_latent = latent + jnp.dot(latent_w.T, activated, precision=highest, preferred_element_type=jnp.float32)
    return (features, new_latent)

def reference(positions, species, centers, neighbours, masks, skin, embed, radial, w_mix, w_latent, w_update, readout):
    domain_count = GRID_X * GRID_Y
    flat_centers = centers.reshape(domain_count, EDGES)
    flat_neighbours = neighbours.reshape(domain_count, EDGES)
    flat_masks = masks.reshape(domain_count, EDGES).astype(jnp.float32)
    offsets = slot_offsets(GHOSTS, CORNERS)

    def slot_rows(values):
        picked = jax.vmap(jax.vmap(lambda values_dom, list_dom: values_dom[:, list_dom]))(values, skin)
        slot_list = []
        for slot_pair in face_slots:
            slot_list.append(jnp.roll(picked, (1 - slot_pair[0], 1 - slot_pair[1]), axis=(0, 1)))
        for slot_pair in corner_slots:
            slot_list.append(jnp.roll(picked, (1 - slot_pair[0], 1 - slot_pair[1]), axis=(0, 1))[..., :CORNERS])
        return jnp.concatenate(slot_list, axis=3)

    def member_energy(coords, embed_m, radial_m, mix_m, latent_m, update_m, readout_m):
        pos_grid = jnp.moveaxis(coords, 0, 2)
        ghost_pos = slot_rows(pos_grid) + box_edge * offsets[None, None, :, :]
        pos_table = jnp.concatenate([pos_grid, ghost_pos], axis=3).reshape(domain_count, 3, SLOTS)
        geom_fn = jax.checkpoint(lambda items: geometry_one(items[0], items[1], items[2], radial_m))
        latent = lax.map(geom_fn, (pos_table, flat_centers, flat_neighbours))
        features = jnp.moveaxis(embed_m[species], 3, 2)
        for layer_idx in range(LAYERS):
            ghost_rows = slot_rows(features)
            feature_table = jnp.concatenate([features, ghost_rows], axis=3).reshape(domain_count, C, SLOTS)
            if layer_idx < LAYERS - 1:
                latent_w = latent_m[layer_idx]
            else:
                latent_w = jnp.zeros((C, C), jnp.float32)
            mix_w = mix_m[layer_idx]
            update_w = update_m[layer_idx]
            step_fn = jax.checkpoint(lambda items: advance_one(items[0], items[1], items[2], items[3], items[4], mix_w, update_w, latent_w))
            new_features, latent = lax.map(step_fn, (feature_table, latent, flat_centers, flat_neighbours, flat_masks))
            features = new_features.reshape(GRID_X, GRID_Y, C, ATOMS_DEV)
        return energy_scale * jnp.sum(features * readout_m[None, None, :, None])

    def member_forces(weights):
        return -jax.grad(member_energy)(positions, *weights)
    return lax.map(member_forces, (embed, radial, w_mix, w_latent, w_update, readout))
```

```python
import jax
import jax.numpy as jnp
from jax import lax
from jax.experimental import pallas as pl
from jax.experimental.pallas import tpu as pltpu
from jax.sharding import PartitionSpec as P

NEIGH = 16
box_edge = 20.0
energy_scale = 16.0
REACH = 3
LANES = 128
CHUNK = 8
PACK_ROWS = 24
f32 = jnp.float32
bf16 = jnp.bfloat16
i32 = jnp.int32


def iota(shape, dim):
    return lax.broadcasted_iota(i32, shape, dim)


def halves(x):
    hi = x.astype(bf16).astype(f32)
    return hi, x - hi


def pack_kernel(pos, species, centers, neighbours, masks, skin, out):
    tiles = centers.shape[-1] // LANES
    atoms = pos.shape[-1]
    ghosts = skin.shape[-1]
    out[...] = jnp.zeros(out.shape, f32)
    live = jnp.zeros((1, LANES), f32)
    for t in range(tiles):
        cut = slice(t * LANES, (t + 1) * LANES)
        out[t : t + 1, :] = centers[0, :, cut].astype(f32)
        out[tiles + t : tiles + t + 1, :] = neighbours[0, :, cut].astype(f32)
        live = live + masks[0, :, cut].astype(f32)
    base = 2 * tiles
    for q in range(3):
        row = pos[q, 0]
        out[base + q : base + q + 1, :] = jnp.concatenate([row, row], axis=1)
    row = species[0].astype(f32)
    out[base + 3 : base + 4, :] = jnp.concatenate([row, row], axis=1)
    out[base + 4 : base + 5, 0:ghosts] = skin[0].astype(f32)
    out[base + 5 : base + 6, :] = live


def block_diag(blocks):
    rows = []
    for at, block in enumerate(blocks):
        parts = [block if k == at else jnp.zeros((block.shape[0], other.shape[1]), f32) for k, other in enumerate(blocks)]
        rows.append(jnp.concatenate(parts, axis=1))
    return jnp.concatenate(rows, axis=0)


def split_left(matrix):
    hi, lo = halves(matrix)
    return jnp.concatenate(
        [jnp.concatenate([hi, hi], axis=1), jnp.concatenate([lo, jnp.zeros_like(lo)], axis=1)], axis=0
    ).astype(bf16)


def weights_kernel(embed, radial, w_mix, w_latent, w_update, readout, geo, dense, radial_back, columns):
    members, elements, channels = embed.shape
    width = members * channels
    embed_t = jnp.concatenate([embed[m].T for m in range(members)], axis=0)
    embed_t = jnp.concatenate([embed_t, jnp.zeros((width, 8 - elements), f32)], axis=1)
    radial_t = jnp.concatenate([radial[m].T for m in range(members)], axis=0)
    r_hi, r_lo = halves(radial_t)
    e_hi, e_lo = halves(embed_t)
    none = jnp.zeros_like(r_hi)
    geo[...] = jnp.concatenate(
        [
            jnp.concatenate([r_hi, r_hi, r_lo, none, none, none], axis=1),
            jnp.concatenate([none, none, none, e_hi, e_lo, none], axis=1),
        ],
        axis=0,
    ).astype(bf16)
    mix0 = block_diag([w_mix[m, 0] for m in range(members)])
    mix1 = block_diag([w_mix[m, 1] for m in range(members)])
    latent = block_diag([w_latent[m, 0] for m in range(members)])
    update0 = block_diag([w_update[m, 0] for m in range(members)])
    update1 = block_diag([w_update[m, 1] for m in range(members)])
    for at, matrix in enumerate((mix0.T, latent.T, mix1.T, mix1, latent, mix0, update0.T * (1.0 / NEIGH), update0 * (1.0 / NEIGH))):
        dense[at] = split_left(matrix)
    radial_back[...] = split_left(block_diag([radial[m] for m in range(members)]))
    read_row = jnp.concatenate([readout[m : m + 1, :] for m in range(members)], axis=1)
    eye = (iota((width, width), 0) == iota((width, width), 1)).astype(f32)
    read = jnp.sum(eye * read_row, axis=1, keepdims=True)
    pull = jnp.sum(update1 * read_row, axis=1, keepdims=True)
    columns[0] = jnp.broadcast_to(read * energy_scale, (width, LANES))
    columns[1] = jnp.broadcast_to(pull * (energy_scale / NEIGH), (width, LANES))


def lane_pick(table, lanes):
    return jnp.take_along_axis(table, jnp.broadcast_to(lanes, table.shape), axis=1, mode="promise_in_bounds")


def product(left, x):
    rows = left.shape[0] // 2
    hi, lo = halves(x)
    both = jnp.dot(left, jnp.concatenate([hi, lo], axis=0).astype(bf16), preferred_element_type=f32)
    return both[:rows] + both[rows:]


def sum_to(values, hot):
    hi, lo = halves(values)
    both = lax.dot_general(
        jnp.concatenate([hi, lo], axis=0).astype(bf16), hot, (((1,), (1,)), ((), ())), preferred_element_type=f32
    )
    return both[: values.shape[0]] + both[values.shape[0] :]


def silu_and_slope(x):
    s = 0.5 * jnp.tanh(0.5 * x) + 0.5
    value = x * s
    return value, s + value * (1.0 - s)


def sin_cos(x):
    turns = jnp.floor(x * 0.15915494309189535 + 0.5)
    r = (x - turns * 6.28125) - turns * 1.9353071795864769e-3
    h = 0.5 * r
    q = h * h
    s = h * (1.0 + q * (-1 / 6 + q * (1 / 120 + q * (-1 / 5040 + q * (1 / 362880 + q * (-1 / 39916800 + q * (1 / 6227020800)))))))
    c = 1.0 + q * (-1 / 2 + q * (1 / 24 + q * (-1 / 720 + q * (1 / 40320 + q * (-1 / 3628800 + q * (1 / 479001600 - q * (1 / 87178291200)))))))
    return 2.0 * s * c, 1.0 - 2.0 * s * s


def force_kernel(wx, wy, place, n_in, *refs):
    arrived = refs[:n_in]
    geo, dense, radial_back, columns, out = refs[n_in : n_in + 5]
    (raw, posb, lid_s, cl_s, spc, spn, unit, basis_s, slope_s, feats, sums, grads, pulls,
     joined_s, lat_s, dpre_s, dz_s, back_s, total, tile_list, near_list) = refs[n_in + 5 :]
    tiles = 8
    n_dom = wx * wy
    nv = (wy + 1) // 2
    n_src = 3 * nv
    n_blk = wx * nv
    width = feats.shape[1]
    members = out.shape[0]
    own_a, own_b, slots = place()

    for ref, at, slot in slots:
        raw[slot] = arrived[ref][at * PACK_ROWS : (at + 1) * PACK_ROWS, :]

    none = n_dom * tiles
    count = jnp.int32(0)
    near = jnp.int32(0)
    for d in range(n_dom):
        a, b = d // wy, d % wy
        live = jnp.max(raw[d, 2 * tiles + 5 : 2 * tiles + 6, :]).astype(i32)
        da = lax.rem(a - own_a + 1 + wx, wx)
        db = lax.rem(b - own_b + 1 + wy, wy)
        touches = jnp.logical_and(da < 3, db < 3)
        for t in range(tiles):
            tile_list[count + t] = d * tiles + t
            near_list[near + t] = d * tiles + t
        count = count + live
        near = near + jnp.where(touches, live, 0)
    for t in range(CHUNK):
        tile_list[count + t] = none
        near_list[near + t] = none

    lane = iota((8, LANES), 1)
    for a in range(wx):
        for v in range(nv):
            low = raw[a * wy + 2 * v, 2 * tiles : 2 * tiles + 8, :]
            high = raw[a * wy + min(2 * v + 1, wy - 1), 2 * tiles : 2 * tiles + 8, :]
            posb[a * nv + v] = jnp.where(lane < 64, low, high)

    lid_s[none : none + 8, :] = jnp.full((8, LANES), -1, i32)
    cl_s[none : none + 8, :] = jnp.full((8, LANES), -1, i32)
    for ref in (spc, spn):
        ref[none : none + 8, :] = jnp.zeros((8, LANES), i32)
    unit[:, none : none + 8, :] = jnp.zeros((3, 8, LANES), f32)
    basis_s[none * 8 : none * 8 + 8, :] = jnp.zeros((8, LANES), f32)
    slope_s[none * 8 : none * 8 + 8, :] = jnp.zeros((8, LANES), f32)

    row = lane[0:1]
    for d in range(n_dom):
        a, b = d // wy, d % wy

        def ids(u, v, start):
            src = ((a + u - 1) % wx) * wy + (b + v - 1) % wy
            base = u * nv * LANES + ((b + v - 1) % wy) * 64 + 8192 * v
            skin = raw[src, 2 * tiles + 4 : 2 * tiles + 5, :].astype(i32) + base
            return pltpu.roll(skin, start, 1) if start else skin

        first = row + (nv * LANES + b * 64 + 8192)
        first = jnp.where(row >= 64, ids(0, 1, 64), first)
        first = jnp.where(row >= 96, ids(1, 0, 96), first)
        second = ids(1, 2, 0)
        second = jnp.where(row >= 32, ids(2, 1, 32), second)
        for k, (u, v) in enumerate(((0, 0), (0, 2), (2, 0), (2, 2))):
            second = jnp.where(row >= 64 + 8 * k, ids(u, v, 64 + 8 * k), second)
        center = raw[d, 0:tiles, :].astype(i32)
        entry = raw[d, tiles : 2 * tiles, :].astype(i32)
        wide = (8, LANES)
        code = jnp.where(
            entry < LANES,
            lane_pick(jnp.broadcast_to(first, wide), entry & 127),
            lane_pick(jnp.broadcast_to(second, wide), entry & 127),
        )
        side_y = lax.shift_right_logical(code, 13)
        lid = code & 8191
        side_x = (lid >= nv * LANES).astype(f32) + (lid >= 2 * nv * LANES).astype(f32) - 1.0
        clid = center + b * 64
        block = lax.shift_right_logical(lid, 7)
        got_n, got_c = [], []
        for q in range(4):
            value = None
            for s in range(n_src):
                src = ((a + s // nv - 1) % wx) * nv + s % nv
                picked = lane_pick(jnp.broadcast_to(posb[src, q : q + 1, :], wide), lid & 127)
                value = picked if value is None else jnp.where(block == s, picked, value)
            got_n.append(value)
            got_c.append(lane_pick(jnp.broadcast_to(posb[a * nv + b // 2, q : q + 1, :], wide), clid & 127))
        dx = got_n[0] + box_edge * side_x - got_c[0]
        dy = got_n[1] + box_edge * (side_y.astype(f32) - 1.0) - got_c[1]
        dz = got_n[2] - got_c[2]
        distance = jnp.sqrt(dx * dx + dy * dy + dz * dz + 1.0)
        inverse = 1.0 / distance
        cut = slice(d * tiles, (d + 1) * tiles)
        for q, part in enumerate((dx, dy, dz)):
            unit[q, cut, :] = part * inverse
        spn[cut, :] = got_n[3].astype(i32)
        spc[cut, :] = got_c[3].astype(i32)
        lid_s[cut, :] = lid
        cl_s[cut, :] = clid
        s1, c1 = sin_cos(distance * 0.25)
        env = jnp.exp(distance * (-1.0 / 32.0))
        c_k, s_k = [jnp.ones_like(c1), c1], [jnp.zeros_like(s1), s1]
        for k in range(2, 8):
            c_k.append(2.0 * c1 * c_k[-1] - c_k[-2])
            s_k.append(2.0 * c1 * s_k[-1] - s_k[-2])
        for k in range(8):
            basis = c_k[k] * env
            basis_s[pl.ds(d * 64 + k, 8, stride=8), :] = basis
            slope_s[pl.ds(d * 64 + k, 8, stride=8), :] = s_k[k] * env * (-k / 4.0) - basis * (1.0 / 32.0)

    for ref in (sums, grads):
        ref[...] = jnp.zeros(ref.shape, f32)
    for ref in (joined_s, lat_s, dpre_s, dz_s, back_s):
        ref[none] = jnp.zeros((width, LANES), f32)
    total[...] = jnp.zeros(total.shape, f32)

    def spots(tau):
        d = lax.shift_right_logical(tau, 3)
        a, b = lax.div(d, wy), lax.rem(d, wy)
        sources = [lax.rem(a + (s // nv - 1 + wx), wx) * nv + s % nv for s in range(n_src)]
        home = lax.rem(a, wx) * nv + lax.div(b, 2)
        return sources, home, lax.div(b, 2)

    atom = iota((LANES, LANES), 0)

    def hot(ids_row):
        return jnp.where(atom == ids_row, 1.0, 0.0)

    def side(parts):
        return jnp.concatenate(parts, axis=1)

    def forward(chunk, carry):
        taus = [tile_list[chunk * CHUNK + j] for j in range(CHUNK)]
        rhs = []
        sub = iota((8, LANES), 0)
        for tau in taus:
            hi, lo = halves(basis_s[pl.ds(pl.multiple_of(tau * 8, 8), 8), :])
            kinds = (sub == spc[pl.ds(tau, 1), :]).astype(f32) + (sub == spn[pl.ds(tau, 1), :]).astype(f32)
            rhs.append(jnp.concatenate([hi, lo, hi, kinds, kinds, jnp.zeros_like(hi)], axis=0).astype(bf16))
        both = jnp.dot(geo[...], side(rhs), preferred_element_type=f32)
        latent, latent_slope = silu_and_slope(both[:width])
        joined = both[width:]
        active, slope = silu_and_slope(product(dense[0], latent * joined))
        latent = latent + product(dense[1], active)
        for j, tau in enumerate(taus):
            cut = slice(j * LANES, (j + 1) * LANES)
            joined_s[tau] = joined[:, cut]
            dpre_s[tau] = latent_slope[:, cut]
            dz_s[tau] = slope[:, cut]
            lat_s[tau] = latent[:, cut]
            _, home, half = spots(tau)
            ids_row = cl_s[pl.ds(tau, 1), :] - half * LANES
            sums[home] += sum_to(active[:, cut], hot(ids_row).astype(bf16))
        return carry

    chunks = lax.div(count + (CHUNK - 1), CHUNK)
    lax.fori_loop(0, chunks, forward, 0)

    sub = iota((8, LANES), 0)
    for k in range(n_blk):
        kinds = (sub == posb[k, 3:4, :].astype(i32)).astype(f32)
        empty = jnp.zeros_like(kinds)
        rhs = jnp.concatenate([empty, empty, empty, kinds, kinds, empty], axis=0).astype(bf16)
        start = jnp.dot(geo[...], rhs, preferred_element_type=f32)[width:]
        feats[k] = start + product(dense[6], sums[k])

    def middle(chunk, carry):
        taus = [tile_list[chunk * CHUNK + j] for j in range(CHUNK)]
        joined, lids, places = [], [], []
        for tau in taus:
            sources, home, half = spots(tau)
            lid = lid_s[pl.ds(tau, 1), :]
            clid = cl_s[pl.ds(tau, 1), :]
            block = jnp.broadcast_to(lax.shift_right_arithmetic(lid, 7), (width, LANES))
            value = None
            for s in range(n_src):
                picked = lane_pick(feats[sources[s]], lid & 127)
                value = picked if value is None else jnp.where(block == s, picked, value)
            joined.append(value + lane_pick(feats[home], clid & 127))
            lids.append((lid, clid - half * LANES))
            places.append((sources, home, half))
        joined = side(joined)
        latent = side([lat_s[tau] for tau in taus])
        _, slope = silu_and_slope(product(dense[2], latent * joined))
        dmix = product(dense[3], side([columns[1]] * CHUNK) * slope)
        back = dmix * joined
        spread = dmix * latent
        for j, tau in enumerate(taus):
            cut = slice(j * LANES, (j + 1) * LANES)
            back_s[tau] = back[:, cut]
            sources, home, half = places[j]
            lid, clid = lids[j]
            hots = [hot(lid - s * LANES) for s in range(n_src)]
            own = hot(clid)
            for v in range(nv):
                here = own if nv == 1 else jnp.where(half == v, own, 0.0)
                hots[nv + v] = hots[nv + v] + here
            added = sum_to(spread[:, cut], jnp.concatenate(hots, axis=0).astype(bf16))
            for s in range(n_src):
                grads[sources[s]] += added[:, s * LANES : (s + 1) * LANES]
        return carry

    lax.fori_loop(0, chunks, middle, 0)

    for k in range(n_blk):
        pulls[k] = product(dense[7], grads[k] + columns[0])

    own_block = own_a * nv + lax.div(own_b, 2)

    def backward(chunk, carry):
        taus = [near_list[chunk * CHUNK + j] for j in range(CHUNK)]
        pulled = []
        for tau in taus:
            _, home, _ = spots(tau)
            pulled.append(lane_pick(pulls[home], cl_s[pl.ds(tau, 1), :] & 127))
        back = side([back_s[tau] for tau in taus])
        active = side(pulled) + product(dense[4], back)
        dmix = product(dense[5], active * side([dz_s[tau] for tau in taus]))
        dlat = back + dmix * side([joined_s[tau] for tau in taus])
        dbasis = product(radial_back[...], dlat * side([dpre_s[tau] for tau in taus]))
        moved = total[...]
        for j, tau in enumerate(taus):
            cut = slice(j * LANES, (j + 1) * LANES)
            slope = slope_s[pl.ds(pl.multiple_of(tau * 8, 8), 8), :]
            rows = []
            for m in range(members):
                along = jnp.sum(dbasis[m * 8 : (m + 1) * 8, cut] * slope, axis=0, keepdims=True)
                rows += [along * unit[q, pl.ds(tau, 1), :] for q in range(3)]
            rows.append(jnp.zeros((8 - 3 * members, LANES), f32))
            sources, home, half = spots(tau)
            lid = lid_s[pl.ds(tau, 1), :]
            clid = cl_s[pl.ds(tau, 1), :]
            hit = jnp.full((1, LANES), -1, i32)
            for s in range(n_src):
                this = jnp.where(sources[s] == own_block, s, -2)
                hit = jnp.where(lax.shift_right_arithmetic(lid, 7) == this, lid & 127, hit)
            chit = jnp.where(home == own_block, clid - half * LANES, -1)
            many = hot(hit) - hot(chit)
            moved = moved + sum_to(jnp.concatenate(rows, axis=0), many.astype(bf16))
        total[...] = moved
        return carry

    lax.fori_loop(0, lax.div(near + (CHUNK - 1), CHUNK), backward, 0)

    result = -total[...]
    result = jnp.where(lax.rem(own_b, 2) == 1, pltpu.roll(result, 64, 1), result)
    for m in range(members):
        for q in range(3):
            out[m, q, 0] = result[m * 3 + q : m * 3 + q + 1, 0:64]


def window(size):
    return min(size, 2 * REACH + 1)


def shift(value, axis, by):
    peers = lax.axis_size(axis)
    return lax.ppermute(value, axis, [(i, (i + by) % peers) for i in range(peers)])


def swap(value, dx, dy):
    nx, ny = lax.axis_size("gx"), lax.axis_size("gy")
    pairs = [(a * ny + b, (a ^ dx) * ny + (b ^ dy)) for a in range(nx) for b in range(ny)]
    return lax.ppermute(value, ("gx", "gy"), pairs)


def gathered(own, gx, gy):
    if gx == 4 and gy == 2:
        pair = jnp.concatenate([own, swap(own, 2, 0)], axis=0)
        arrays = [pair, swap(pair, 1, 0), swap(pair, 0, 1), swap(pair, 1, 1)]

        def place():
            a, b = lax.axis_index("gx"), lax.axis_index("gy")
            slots = []
            for k in range(4):
                for at in range(2):
                    slots.append((k, at, (a ^ ((k & 1) | (2 * at))) * 2 + (b ^ (k >> 1))))
            return a, b, slots

        return arrays, place
    wx, wy = window(gx), window(gy)
    steps = list(range(wy // 2 + 1)) + list(range(wy // 2 + 1 - wy, 0))
    column = jnp.concatenate([own if s == 0 else shift(own, "gy", -s) for s in steps], axis=0)
    steps_x = list(range(wx // 2 + 1)) + list(range(wx // 2 + 1 - wx, 0))
    arrays = [column if s == 0 else shift(column, "gx", -s) for s in steps_x]

    def place():
        slots = [(k, at, k * wy + at) for k in range(wx) for at in range(wy)]
        return jnp.int32(0), jnp.int32(0), slots

    return arrays, place


def on_device(
    positions, species, centers, neighbours, masks, skin, embed, radial, w_mix, w_latent, w_update, readout
):
    gx, gy = lax.axis_size("gx"), lax.axis_size("gy")
    atoms = positions.shape[-1]
    members, _, channels = embed.shape
    width = members * channels
    own = pl.pallas_call(
        pack_kernel, out_shape=jax.ShapeDtypeStruct((PACK_ROWS, LANES), f32), name="pack"
    )(positions, species, centers, neighbours, masks, skin)
    parts = pl.pallas_call(
        weights_kernel,
        out_shape=(
            jax.ShapeDtypeStruct((2 * width, 48), bf16),
            jax.ShapeDtypeStruct((8, 2 * width, 2 * width), bf16),
            jax.ShapeDtypeStruct((2 * members * 8, 2 * width), bf16),
            jax.ShapeDtypeStruct((2, width, LANES), f32),
        ),
        name="weights",
    )(embed, radial, w_mix, w_latent, w_update, readout)
    arrays, place = gathered(own, gx, gy)
    wx, wy = window(gx), window(gy)
    n_dom = wx * wy
    n_tiles = n_dom * 8
    n_blk = wx * ((wy + 1) // 2)
    per_tile = pltpu.VMEM((n_tiles + 1, width, LANES), f32)
    per_block = pltpu.VMEM((n_blk, width, LANES), f32)
    row_ids = pltpu.VMEM((n_tiles + 8, LANES), i32)

    def body(*refs):
        force_kernel(wx, wy, place, len(arrays), *refs)

    return pl.pallas_call(
        body,
        out_shape=jax.ShapeDtypeStruct((members, 3, 1, 1, atoms), f32),
        scratch_shapes=[
            pltpu.VMEM((n_dom, PACK_ROWS, LANES), f32),
            pltpu.VMEM((n_blk, 8, LANES), f32),
            row_ids,
            row_ids,
            row_ids,
            row_ids,
            pltpu.VMEM((3, n_tiles + 8, LANES), f32),
            pltpu.VMEM((n_tiles * 8 + 8, LANES), f32),
            pltpu.VMEM((n_tiles * 8 + 8, LANES), f32),
            per_block,
            per_block,
            per_block,
            per_block,
            per_tile,
            per_tile,
            per_tile,
            per_tile,
            per_tile,
            pltpu.VMEM((8, LANES), f32),
            pltpu.SMEM((n_tiles + 2 * CHUNK,), i32),
            pltpu.SMEM((n_tiles + 2 * CHUNK,), i32),
        ],
        compiler_params=pltpu.CompilerParams(vmem_limit_bytes=56 * 1024 * 1024),
        name="forces",
    )(*arrays, *parts)


def solution(mesh):
    return jax.shard_map(
        on_device,
        mesh=mesh,
        in_specs=(
            P(None, ("groups", "gx"), "gy", None),
            P(("groups", "gx"), "gy", None),
            P(("groups", "gx"), "gy", None),
            P(("groups", "gx"), "gy", None),
            P(("groups", "gx"), "gy", None),
            P(("groups", "gx"), "gy", None),
            P("gz", None, None),
            P("gz", None, None),
            P("gz", None, None, None),
            P("gz", None, None, None),
            P("gz", None, None, None),
            P("gz", None),
        ),
        out_specs=P("gz", None, ("groups", "gx"), "gy", None),
        check_vma=False,
    )
```

```python
import jax
import jax.numpy as jnp
from jax import lax
from jax.experimental import pallas as pl
from jax.experimental.pallas import tpu as pltpu
from jax.sharding import PartitionSpec as P

NEIGH = 16
box_edge = 20.0
energy_scale = 16.0
REACH = 3
LANES = 128
CHUNK = 8
PACK_ROWS = 24
f32 = jnp.float32
bf16 = jnp.bfloat16
i32 = jnp.int32


def iota(shape, dim):
    return lax.broadcasted_iota(i32, shape, dim)


def halves(x):
    hi = x.astype(bf16).astype(f32)
    return hi, x - hi


def pack_kernel(pos, species, centers, neighbours, masks, skin, out):
    tiles = centers.shape[-1] // LANES
    atoms = pos.shape[-1]
    ghosts = skin.shape[-1]
    out[...] = jnp.zeros(out.shape, f32)
    live = jnp.zeros((1, LANES), f32)
    for t in range(tiles):
        cut = slice(t * LANES, (t + 1) * LANES)
        out[t : t + 1, :] = centers[0, :, cut].astype(f32)
        out[tiles + t : tiles + t + 1, :] = neighbours[0, :, cut].astype(f32)
        live = live + masks[0, :, cut].astype(f32)
    base = 2 * tiles
    for q in range(3):
        row = pos[q, 0]
        out[base + q : base + q + 1, :] = jnp.concatenate([row, row], axis=1)
    row = species[0].astype(f32)
    out[base + 3 : base + 4, :] = jnp.concatenate([row, row], axis=1)
    out[base + 4 : base + 5, 0:ghosts] = skin[0].astype(f32)
    out[base + 5 : base + 6, :] = live


def block_diag(blocks):
    rows = []
    for at, block in enumerate(blocks):
        parts = [block if k == at else jnp.zeros((block.shape[0], other.shape[1]), f32) for k, other in enumerate(blocks)]
        rows.append(jnp.concatenate(parts, axis=1))
    return jnp.concatenate(rows, axis=0)


def split_left(matrix):
    hi, lo = halves(matrix)
    return jnp.concatenate([hi, hi, lo], axis=1).astype(bf16)


def parts(x):
    hi = x.astype(bf16)
    return hi, (x - hi.astype(f32)).astype(bf16)


def weights_kernel(embed, radial, w_mix, w_latent, w_update, readout, geo, dense, radial_back, columns):
    members, elements, channels = embed.shape
    width = members * channels
    embed_t = jnp.concatenate([embed[m].T for m in range(members)], axis=0)
    embed_t = jnp.concatenate([embed_t, jnp.zeros((width, 8 - elements), f32)], axis=1)
    radial_t = jnp.concatenate([radial[m].T for m in range(members)], axis=0)
    r_hi, r_lo = halves(0.5 * radial_t)
    e_hi, e_lo = halves(embed_t)
    none = jnp.zeros_like(r_hi)
    geo[...] = jnp.concatenate(
        [
            jnp.concatenate([r_hi, r_hi, r_lo, none, none, none], axis=1),
            jnp.concatenate([none, none, none, e_hi, e_lo, none], axis=1),
        ],
        axis=0,
    ).astype(bf16)
    mix0 = block_diag([w_mix[m, 0] for m in range(members)])
    mix1 = block_diag([w_mix[m, 1] for m in range(members)])
    latent = block_diag([w_latent[m, 0] for m in range(members)])
    update0 = block_diag([w_update[m, 0] for m in range(members)])
    update1 = block_diag([w_update[m, 1] for m in range(members)])
    radial_back[...] = split_left(0.5 * block_diag([radial[m] for m in range(members)]))
    read_row = jnp.concatenate([readout[m : m + 1, :] for m in range(members)], axis=1)
    eye = (iota((width, width), 0) == iota((width, width), 1)).astype(f32)
    read = jnp.sum(eye * read_row, axis=1, keepdims=True)
    pull = jnp.sum(update1.T * read, axis=0, keepdims=True) * (energy_scale / NEIGH)
    columns[...] = jnp.broadcast_to(read * energy_scale, (width, LANES))
    factors = (
        0.5 * mix0.T, latent.T, 0.5 * mix1.T, 0.5 * mix1 * pull, latent, 0.5 * mix0,
        update0.T * (1.0 / NEIGH), update0 * (1.0 / NEIGH),
    )
    for at, matrix in enumerate(factors):
        dense[at] = split_left(matrix)


def lane_pick(table, lanes):
    return jnp.take_along_axis(table, jnp.broadcast_to(lanes, table.shape), axis=1, mode="promise_in_bounds")


def product(left, x):
    hi, lo = parts(x)
    return jnp.dot(left, jnp.concatenate([hi, lo, hi], axis=0), preferred_element_type=f32)


def sum_to(values, hot):
    hi, lo = parts(values)
    both = lax.dot_general(
        jnp.concatenate([hi, lo], axis=0), hot, (((1,), (1,)), ((), ())), preferred_element_type=f32
    )
    return both[: values.shape[0]] + both[values.shape[0] :]


def silu(h):
    return h + h * jnp.tanh(h)


def silu_and_slope(h):
    t = jnp.tanh(h)
    p = 1.0 + t
    return h * p, p + p * (h - h * t)


def sin_cos(x):
    turns = jnp.floor(x * 0.15915494309189535 + 0.5)
    r = (x - turns * 6.28125) - turns * 1.9353071795864769e-3
    h = 0.5 * r
    q = h * h
    s = h * (1.0 + q * (-1 / 6 + q * (1 / 120 + q * (-1 / 5040 + q * (1 / 362880 + q * (-1 / 39916800 + q * (1 / 6227020800)))))))
    c = 1.0 + q * (-1 / 2 + q * (1 / 24 + q * (-1 / 720 + q * (1 / 40320 + q * (-1 / 3628800 + q * (1 / 479001600 - q * (1 / 87178291200)))))))
    return 2.0 * s * c, 1.0 - 2.0 * s * s


def force_kernel(wx, wy, place, n_in, *refs):
    arrived = refs[:n_in]
    geo_in, dense_in, radial_back_in, columns_in, out = refs[n_in : n_in + 5]
    (raw, posb, lid_s, cl_s, spc, spn, unit, basis_s, slope_s, feats2, sums, grads, pulls,
     joined_s, lat_s, dpre_s, dz_s, back_s, total, tile_list, near_list,
     geo, dense, radial_back, columns, sems) = refs[n_in + 5 :]
    tiles = 8
    n_dom = wx * wy
    nv = (wy + 1) // 2
    n_src = 3 * nv
    n_blk = wx * nv
    width = feats2.shape[1] // 2
    members = out.shape[0]
    own_a, own_b, slots = place()

    copies = [
        pltpu.make_async_copy(arrived[ref].at[pl.ds(at * PACK_ROWS, PACK_ROWS), :], raw.at[slot], sems.at[k])
        for k, (ref, at, slot) in enumerate(slots)
    ]
    loads = ((geo_in, geo), (dense_in, dense), (radial_back_in, radial_back), (columns_in, columns))
    later = [pltpu.make_async_copy(src, dst, sems.at[n_dom + k]) for k, (src, dst) in enumerate(loads)]
    for copy in copies + later:
        copy.start()
    for copy in copies:
        copy.wait()

    none = n_dom * tiles
    count = jnp.int32(0)
    near = jnp.int32(0)
    for d in range(n_dom):
        a, b = d // wy, d % wy
        live = jnp.max(raw[d, 2 * tiles + 5 : 2 * tiles + 6, :]).astype(i32)
        da = lax.rem(a - own_a + 1 + wx, wx)
        db = lax.rem(b - own_b + 1 + wy, wy)
        touches = jnp.logical_and(da < 3, db < 3)
        for t in range(tiles):
            tile_list[count + t] = d * tiles + t
            near_list[near + t] = d * tiles + t
        count = count + live
        near = near + jnp.where(touches, live, 0)
    for t in range(CHUNK):
        tile_list[count + t] = none
        near_list[near + t] = none

    lane = iota((8, LANES), 1)
    for a in range(wx):
        for v in range(nv):
            low = raw[a * wy + 2 * v, 2 * tiles : 2 * tiles + 8, :]
            high = raw[a * wy + min(2 * v + 1, wy - 1), 2 * tiles : 2 * tiles + 8, :]
            posb[a * nv + v] = jnp.where(lane < 64, low, high)

    lid_s[none : none + 8, :] = jnp.full((8, LANES), -1, i32)
    cl_s[none : none + 8, :] = jnp.full((8, LANES), -1, i32)
    for ref in (spc, spn):
        ref[none : none + 8, :] = jnp.zeros((8, LANES), i32)
    unit[:, none : none + 8, :] = jnp.zeros((3, 8, LANES), f32)
    basis_s[none * 8 : none * 8 + 8, :] = jnp.zeros((8, LANES), f32)
    slope_s[none * 8 : none * 8 + 8, :] = jnp.zeros((8, LANES), f32)

    row = lane[0:1]
    for d in range(n_dom):
        a, b = d // wy, d % wy

        def ids(u, v, start):
            src = ((a + u - 1) % wx) * wy + (b + v - 1) % wy
            base = u * nv * LANES + ((b + v - 1) % wy) * 64 + 8192 * v
            skin = raw[src, 2 * tiles + 4 : 2 * tiles + 5, :].astype(i32) + base
            return pltpu.roll(skin, start, 1) if start else skin

        first = row + (nv * LANES + b * 64 + 8192)
        first = jnp.where(row >= 64, ids(0, 1, 64), first)
        first = jnp.where(row >= 96, ids(1, 0, 96), first)
        second = ids(1, 2, 0)
        second = jnp.where(row >= 32, ids(2, 1, 32), second)
        for k, (u, v) in enumerate(((0, 0), (0, 2), (2, 0), (2, 2))):
            second = jnp.where(row >= 64 + 8 * k, ids(u, v, 64 + 8 * k), second)
        center = raw[d, 0:tiles, :].astype(i32)
        entry = raw[d, tiles : 2 * tiles, :].astype(i32)
        wide = (8, LANES)
        code = jnp.where(
            entry < LANES,
            lane_pick(jnp.broadcast_to(first, wide), entry & 127),
            lane_pick(jnp.broadcast_to(second, wide), entry & 127),
        )
        side_y = lax.shift_right_logical(code, 13)
        lid = code & 8191
        side_x = (lid >= nv * LANES).astype(f32) + (lid >= 2 * nv * LANES).astype(f32) - 1.0
        clid = center + b * 64
        block = lax.shift_right_logical(lid, 7)
        got_n, got_c = [], []
        for q in range(4):
            value = None
            for s in range(n_src):
                src = ((a + s // nv - 1) % wx) * nv + s % nv
                picked = lane_pick(jnp.broadcast_to(posb[src, q : q + 1, :], wide), lid & 127)
                value = picked if value is None else jnp.where(block == s, picked, value)
            got_n.append(value)
            got_c.append(lane_pick(jnp.broadcast_to(posb[a * nv + b // 2, q : q + 1, :], wide), clid & 127))
        dx = got_n[0] + box_edge * side_x - got_c[0]
        dy = got_n[1] + box_edge * (side_y.astype(f32) - 1.0) - got_c[1]
        dz = got_n[2] - got_c[2]
        distance = jnp.sqrt(dx * dx + dy * dy + dz * dz + 1.0)
        inverse = 1.0 / distance
        cut = slice(d * tiles, (d + 1) * tiles)
        for q, part in enumerate((dx, dy, dz)):
            unit[q, cut, :] = part * inverse
        spn[cut, :] = got_n[3].astype(i32)
        spc[cut, :] = got_c[3].astype(i32)
        lid_s[cut, :] = lid
        cl_s[cut, :] = clid
        s1, c1 = sin_cos(distance * 0.25)
        env = jnp.exp(distance * (-1.0 / 32.0))
        c_k, s_k = [jnp.ones_like(c1), c1], [jnp.zeros_like(s1), s1]
        for k in range(2, 8):
            c_k.append(2.0 * c1 * c_k[-1] - c_k[-2])
            s_k.append(2.0 * c1 * s_k[-1] - s_k[-2])
        for k in range(8):
            basis = c_k[k] * env
            basis_s[pl.ds(d * 64 + k, 8, stride=8), :] = basis
            slope_s[pl.ds(d * 64 + k, 8, stride=8), :] = s_k[k] * env * (-k / 4.0) - basis * (1.0 / 32.0)

    for ref in (sums, grads):
        ref[...] = jnp.zeros(ref.shape, f32)
    for ref in (joined_s, lat_s, dpre_s, dz_s, back_s):
        ref[none] = jnp.zeros((width, LANES), f32)
    total[...] = jnp.zeros(total.shape, f32)

    def spots(tau):
        d = lax.shift_right_logical(tau, 3)
        a, b = lax.div(d, wy), lax.rem(d, wy)
        sources = [lax.rem(a + (s // nv - 1 + wx), wx) * nv + s % nv for s in range(n_src)]
        home = lax.rem(a, wx) * nv + lax.div(b, 2)
        return sources, home, lax.div(b, 2)

    atom = iota((LANES, LANES), 0)

    def hot(ids_row):
        return jnp.where(atom == ids_row, 1.0, 0.0)

    def side(parts):
        return jnp.concatenate(parts, axis=1)

    def forward(chunk, carry):
        taus = [tile_list[chunk * CHUNK + j] for j in range(CHUNK)]
        rhs = []
        sub = iota((8, LANES), 0)
        for tau in taus:
            hi, lo = halves(basis_s[pl.ds(pl.multiple_of(tau * 8, 8), 8), :])
            kinds = (sub == spc[pl.ds(tau, 1), :]).astype(f32) + (sub == spn[pl.ds(tau, 1), :]).astype(f32)
            rhs.append(jnp.concatenate([hi, lo, hi, kinds, kinds, jnp.zeros_like(hi)], axis=0).astype(bf16))
        both = jnp.dot(geo[...], side(rhs), preferred_element_type=f32)
        latent, latent_slope = silu_and_slope(both[:width])
        joined = both[width:]
        active, slope = silu_and_slope(product(dense[0], latent * joined))
        latent = latent + product(dense[1], active)
        for j, tau in enumerate(taus):
            cut = slice(j * LANES, (j + 1) * LANES)
            joined_s[tau] = joined[:, cut]
            dpre_s[tau] = latent_slope[:, cut]
            dz_s[tau] = slope[:, cut]
            lat_s[tau] = latent[:, cut]
            _, home, half = spots(tau)
            ids_row = cl_s[pl.ds(tau, 1), :] - half * LANES
            sums[home] += sum_to(active[:, cut], hot(ids_row).astype(bf16))
        return carry

    chunks = lax.div(count + (CHUNK - 1), CHUNK)
    for copy in later:
        copy.wait()
    lax.fori_loop(0, chunks, forward, 0)

    sub = iota((8, LANES), 0)
    for k in range(n_blk):
        kinds = (sub == posb[k, 3:4, :].astype(i32)).astype(f32)
        empty = jnp.zeros_like(kinds)
        rhs = jnp.concatenate([empty, empty, empty, kinds, kinds, empty], axis=0).astype(bf16)
        start = jnp.dot(geo[...], rhs, preferred_element_type=f32)[width:]
        feats2[k] = jnp.concatenate(parts(start + product(dense[6], sums[k])), axis=0)

    def middle(chunk, carry):
        taus = [tile_list[chunk * CHUNK + j] for j in range(CHUNK)]
        joined, lids, places = [], [], []
        for tau in taus:
            sources, home, half = spots(tau)
            lid = lid_s[pl.ds(tau, 1), :]
            clid = cl_s[pl.ds(tau, 1), :]
            lids.append((lid, clid - half * LANES))
            places.append((sources, home, half))
        hot_rows = []
        for j, tau in enumerate(taus):
            sources, home, half = places[j]
            lid, clid = lids[j]
            hots = [hot(lid - s * LANES) for s in range(n_src)]
            own = hot(clid)
            for v in range(nv):
                here = own if nv == 1 else jnp.where(half == v, own, 0.0)
                hots[nv + v] = hots[nv + v] + here
            hot_rows.append(jnp.concatenate(hots, axis=0).astype(bf16))
            both = jnp.dot(side([feats2[s] for s in sources]), hot_rows[-1], preferred_element_type=f32)
            joined.append(both[:width] + both[width:])
        joined = side(joined)
        latent = side([lat_s[tau] for tau in taus])
        _, slope = silu_and_slope(product(dense[2], latent * joined))
        dmix = product(dense[3], slope)
        back = dmix * joined
        spread = dmix * latent
        for j, tau in enumerate(taus):
            cut = slice(j * LANES, (j + 1) * LANES)
            back_s[tau] = back[:, cut]
            sources, home, half = places[j]
            added = sum_to(spread[:, cut], hot_rows[j])
            for s in range(n_src):
                grads[sources[s]] += added[:, s * LANES : (s + 1) * LANES]
        return carry

    lax.fori_loop(0, chunks, middle, 0)

    for k in range(n_blk):
        pulls[k] = product(dense[7], grads[k] + columns[...])

    own_block = own_a * nv + lax.div(own_b, 2)

    def backward(chunk, carry):
        taus = [near_list[chunk * CHUNK + j] for j in range(CHUNK)]
        pulled = []
        for tau in taus:
            _, home, _ = spots(tau)
            pulled.append(lane_pick(pulls[home], cl_s[pl.ds(tau, 1), :] & 127))
        back = side([back_s[tau] for tau in taus])
        active = side(pulled) + product(dense[4], back)
        dmix = product(dense[5], active * side([dz_s[tau] for tau in taus]))
        dlat = back + dmix * side([joined_s[tau] for tau in taus])
        dbasis = product(radial_back[...], dlat * side([dpre_s[tau] for tau in taus]))
        moved = total[...]
        for j, tau in enumerate(taus):
            cut = slice(j * LANES, (j + 1) * LANES)
            slope = slope_s[pl.ds(pl.multiple_of(tau * 8, 8), 8), :]
            rows = []
            for m in range(members):
                along = jnp.sum(dbasis[m * 8 : (m + 1) * 8, cut] * slope, axis=0, keepdims=True)
                rows += [along * unit[q, pl.ds(tau, 1), :] for q in range(3)]
            rows.append(jnp.zeros((8 - 3 * members, LANES), f32))
            sources, home, half = spots(tau)
            lid = lid_s[pl.ds(tau, 1), :]
            clid = cl_s[pl.ds(tau, 1), :]
            hit = jnp.full((1, LANES), -1, i32)
            for s in range(n_src):
                this = jnp.where(sources[s] == own_block, s, -2)
                hit = jnp.where(lax.shift_right_arithmetic(lid, 7) == this, lid & 127, hit)
            chit = jnp.where(home == own_block, clid - half * LANES, -1)
            many = hot(hit) - hot(chit)
            moved = moved + sum_to(jnp.concatenate(rows, axis=0), many.astype(bf16))
        total[...] = moved
        return carry

    lax.fori_loop(0, lax.div(near + (CHUNK - 1), CHUNK), backward, 0)

    result = -total[...]
    result = jnp.where(lax.rem(own_b, 2) == 1, pltpu.roll(result, 64, 1), result)
    for m in range(members):
        for q in range(3):
            out[m, q, 0] = result[m * 3 + q : m * 3 + q + 1, 0:64]


def window(size):
    return min(size, 2 * REACH + 1)


def shift(value, axis, by):
    peers = lax.axis_size(axis)
    return lax.ppermute(value, axis, [(i, (i + by) % peers) for i in range(peers)])


def swap(value, by_core):
    sizes = [lax.axis_size(axis) for axis in ("gx", "gy", "gz")]
    pairs = []
    for a in range(sizes[0]):
        for b in range(sizes[1]):
            for c in range(sizes[2]):
                dx, dy, dz = by_core[c]
                pairs.append(((a * sizes[1] + b) * sizes[2] + c, ((a ^ dx) * sizes[1] + (b ^ dy)) * sizes[2] + (c ^ dz)))
    return lax.ppermute(value, ("gx", "gy", "gz"), pairs)


def gathered(own, gx, gy):
    if gx == 4 and gy == 2 and lax.axis_size("gz") == 2:
        fetch = (((0, 1), (2, 1)), ((1, 0), (3, 0)), ((1, 1), (3, 1)))
        far = swap(own, ((2, 0, 0), (2, 0, 0)))
        fetched = [swap(own, (low + (0,), high + (0,))) for low, high in fetch]
        handed = [swap(value, ((0, 0, 1), (0, 0, 1))) for value in fetched]

        def place():
            a, b, c = lax.axis_index("gx"), lax.axis_index("gy"), lax.axis_index("gz")
            slots = [(0, 0, a * 2 + b), (1, 0, (a ^ 2) * 2 + b)]
            for k, (low, high) in enumerate(fetch):
                mine = [jnp.where(c == 0, low[q], high[q]) for q in range(2)]
                other = [jnp.where(c == 0, high[q], low[q]) for q in range(2)]
                slots.append((2 + k, 0, (a ^ mine[0]) * 2 + (b ^ mine[1])))
                slots.append((5 + k, 0, (a ^ other[0]) * 2 + (b ^ other[1])))
            return a, b, slots

        return [own, far] + fetched + handed, place
    wx, wy = window(gx), window(gy)
    steps = list(range(wy // 2 + 1)) + list(range(wy // 2 + 1 - wy, 0))
    column = jnp.concatenate([own if s == 0 else shift(own, "gy", -s) for s in steps], axis=0)
    steps_x = list(range(wx // 2 + 1)) + list(range(wx // 2 + 1 - wx, 0))
    arrays = [column if s == 0 else shift(column, "gx", -s) for s in steps_x]

    def place():
        slots = [(k, at, k * wy + at) for k in range(wx) for at in range(wy)]
        return jnp.int32(0), jnp.int32(0), slots

    return arrays, place


def on_device(
    positions, species, centers, neighbours, masks, skin, embed, radial, w_mix, w_latent, w_update, readout
):
    gx, gy = lax.axis_size("gx"), lax.axis_size("gy")
    atoms = positions.shape[-1]
    members, _, channels = embed.shape
    width = members * channels
    own = pl.pallas_call(
        pack_kernel, out_shape=jax.ShapeDtypeStruct((PACK_ROWS, LANES), f32), name="pack"
    )(positions, species, centers, neighbours, masks, skin)
    parts = pl.pallas_call(
        weights_kernel,
        out_shape=(
            jax.ShapeDtypeStruct((2 * width, 48), bf16),
            jax.ShapeDtypeStruct((8, width, 3 * width), bf16),
            jax.ShapeDtypeStruct((members * 8, 3 * width), bf16),
            jax.ShapeDtypeStruct((width, LANES), f32),
        ),
        name="weights",
    )(embed, radial, w_mix, w_latent, w_update, readout)
    arrays, place = gathered(own, gx, gy)
    wx, wy = window(gx), window(gy)
    n_dom = wx * wy
    n_tiles = n_dom * 8
    n_blk = wx * ((wy + 1) // 2)
    held = 5 * (n_tiles + 1) * width * LANES * 4 + 8 * 1024 * 1024
    per_tile = pltpu.VMEM((n_tiles + 1, width, LANES), f32)
    per_block = pltpu.VMEM((n_blk, width, LANES), f32)
    row_ids = pltpu.VMEM((n_tiles + 8, LANES), i32)

    def body(*refs):
        force_kernel(wx, wy, place, len(arrays), *refs)

    return pl.pallas_call(
        body,
        out_shape=jax.ShapeDtypeStruct((members, 3, 1, 1, atoms), f32),
        scratch_shapes=[
            pltpu.VMEM((n_dom, PACK_ROWS, LANES), f32),
            pltpu.VMEM((n_blk, 8, LANES), f32),
            row_ids,
            row_ids,
            row_ids,
            row_ids,
            pltpu.VMEM((3, n_tiles + 8, LANES), f32),
            pltpu.VMEM((n_tiles * 8 + 8, LANES), f32),
            pltpu.VMEM((n_tiles * 8 + 8, LANES), f32),
            pltpu.VMEM((n_blk, 2 * width, LANES), bf16),
            per_block,
            per_block,
            per_block,
            per_tile,
            per_tile,
            per_tile,
            per_tile,
            per_tile,
            pltpu.VMEM((8, LANES), f32),
            pltpu.SMEM((n_tiles + 2 * CHUNK,), i32),
            pltpu.SMEM((n_tiles + 2 * CHUNK,), i32),
        ]
        + [pltpu.VMEM(part.shape, part.dtype) for part in parts]
        + [pltpu.SemaphoreType.DMA((n_dom + len(parts),))],
        in_specs=[pl.BlockSpec(memory_space=pl.ANY)] * (len(arrays) + len(parts)),
        compiler_params=pltpu.CompilerParams(vmem_limit_bytes=held),
        name="forces",
    )(*arrays, *parts)


def solution(mesh):
    return jax.shard_map(
        on_device,
        mesh=mesh,
        in_specs=(
            P(None, ("groups", "gx"), "gy", None),
            P(("groups", "gx"), "gy", None),
            P(("groups", "gx"), "gy", None),
            P(("groups", "gx"), "gy", None),
            P(("groups", "gx"), "gy", None),
            P(("groups", "gx"), "gy", None),
            P("gz", None, None),
            P("gz", None, None),
            P("gz", None, None, None),
            P("gz", None, None, None),
            P("gz", None, None, None),
            P("gz", None),
        ),
        out_specs=P("gz", None, ("groups", "gx"), "gy", None),
        check_vma=False,
    )
```

```python
import jax
import jax.numpy as jnp
from jax import lax
from jax.experimental import pallas as pl
from jax.experimental.pallas import tpu as pltpu
from jax.sharding import PartitionSpec as P

NEIGH = 16
box_edge = 20.0
energy_scale = 16.0
REACH = 3
LANES = 128
CHUNK = 8
PACK_ROWS = 24
f32 = jnp.float32
bf16 = jnp.bfloat16
i32 = jnp.int32


def iota(shape, dim):
    return lax.broadcasted_iota(i32, shape, dim)


def halves(x):
    hi = x.astype(bf16).astype(f32)
    return hi, x - hi


def pack_kernel(pos, species, centers, neighbours, masks, skin, out):
    tiles = centers.shape[-1] // LANES
    atoms = pos.shape[-1]
    ghosts = skin.shape[-1]
    out[...] = jnp.zeros(out.shape, f32)
    live = jnp.zeros((1, LANES), f32)
    for t in range(tiles):
        cut = slice(t * LANES, (t + 1) * LANES)
        out[t : t + 1, :] = centers[0, :, cut].astype(f32)
        out[tiles + t : tiles + t + 1, :] = neighbours[0, :, cut].astype(f32)
        live = live + masks[0, :, cut].astype(f32)
    base = 2 * tiles
    for q in range(3):
        row = pos[q, 0]
        out[base + q : base + q + 1, :] = jnp.concatenate([row, row], axis=1)
    row = species[0].astype(f32)
    out[base + 3 : base + 4, :] = jnp.concatenate([row, row], axis=1)
    out[base + 4 : base + 5, 0:ghosts] = skin[0].astype(f32)
    out[base + 5 : base + 6, :] = live


def block_diag(blocks):
    rows = []
    for at, block in enumerate(blocks):
        parts = [block if k == at else jnp.zeros((block.shape[0], other.shape[1]), f32) for k, other in enumerate(blocks)]
        rows.append(jnp.concatenate(parts, axis=1))
    return jnp.concatenate(rows, axis=0)


def split_left(matrix):
    hi, lo = halves(matrix)
    return jnp.concatenate([hi, hi, lo], axis=1).astype(bf16)


def parts(x):
    hi = x.astype(bf16)
    return hi, (x - hi.astype(f32)).astype(bf16)


def weight_factors(embed, radial, w_mix, w_latent, w_update, readout, geo, dense, radial_back, columns):
    elements, members, channels = embed.shape
    width = members * channels
    embed_t = jnp.concatenate([embed[:, m, :].T for m in range(members)], axis=0)
    embed_t = jnp.concatenate([embed_t, jnp.zeros((width, 8 - elements), f32)], axis=1)
    radial_t = jnp.concatenate([radial[m].T for m in range(members)], axis=0)
    r_hi, r_lo = halves(0.5 * radial_t)
    e_hi, e_lo = halves(embed_t)
    none = jnp.zeros_like(r_hi)
    geo[...] = jnp.concatenate(
        [
            jnp.concatenate([r_hi, r_hi, r_lo, none, none, none], axis=1),
            jnp.concatenate([none, none, none, e_hi, e_lo, none], axis=1),
        ],
        axis=0,
    ).astype(bf16)
    mix0 = block_diag([w_mix[m, 0] for m in range(members)])
    mix1 = block_diag([w_mix[m, 1] for m in range(members)])
    latent = block_diag([w_latent[m, 0] for m in range(members)])
    update0 = block_diag([w_update[m, 0] for m in range(members)])
    update1 = block_diag([w_update[m, 1] for m in range(members)])
    radial_back[...] = split_left(0.5 * block_diag([radial[m] for m in range(members)]))
    read_row = jnp.concatenate([readout[m : m + 1, :] for m in range(members)], axis=1)
    eye = (iota((width, width), 0) == iota((width, width), 1)).astype(f32)
    read = jnp.sum(eye * read_row, axis=1, keepdims=True)
    pull = jnp.sum(update1.T * read, axis=0, keepdims=True) * (energy_scale / NEIGH)
    columns[...] = jnp.broadcast_to(read * energy_scale, (width, LANES))
    factors = (
        0.5 * mix0.T, latent.T, 0.5 * mix1.T, 0.5 * mix1 * pull, latent, 0.5 * mix0,
        update0.T * (1.0 / NEIGH), update0 * (1.0 / NEIGH),
    )
    for at, matrix in enumerate(factors):
        dense[at] = split_left(matrix)


def lane_pick(table, lanes):
    return jnp.take_along_axis(table, jnp.broadcast_to(lanes, table.shape), axis=1, mode="promise_in_bounds")


def product(left, x):
    hi, lo = parts(x)
    return jnp.dot(left, jnp.concatenate([hi, lo, hi], axis=0), preferred_element_type=f32)


def sum_to(values, hot):
    hi, lo = parts(values)
    both = lax.dot_general(
        jnp.concatenate([hi, lo], axis=0), hot, (((1,), (1,)), ((), ())), preferred_element_type=f32
    )
    return both[: values.shape[0]] + both[values.shape[0] :]


def silu(h):
    return h + h * jnp.tanh(h)


def silu_and_slope(h):
    t = jnp.tanh(h)
    p = 1.0 + t
    return h * p, p + p * (h - h * t)


def sin_cos(x):
    turns = jnp.floor(x * 0.15915494309189535 + 0.5)
    r = (x - turns * 6.28125) - turns * 1.9353071795864769e-3
    h = 0.5 * r
    q = h * h
    s = h * (1.0 + q * (-1 / 6 + q * (1 / 120 + q * (-1 / 5040 + q * (1 / 362880 + q * (-1 / 39916800 + q * (1 / 6227020800)))))))
    c = 1.0 + q * (-1 / 2 + q * (1 / 24 + q * (-1 / 720 + q * (1 / 40320 + q * (-1 / 3628800 + q * (1 / 479001600 - q * (1 / 87178291200)))))))
    return 2.0 * s * c, 1.0 - 2.0 * s * s


def force_kernel(wx, wy, place, n_in, *refs):
    arrived = refs[:n_in]
    model_in, out = refs[n_in : n_in + 6], refs[n_in + 6]
    (raw, posb, lid_s, cl_s, spc, spn, unit, basis_s, slope_s, feats2, sums, grads, pulls,
     joined_s, lat_s, dpre_s, dz_s, back_s, total, tile_list, near_list,
     geo, dense, radial_back, columns, *model, sems) = refs[n_in + 7 :]
    tiles = 8
    n_dom = wx * wy
    nv = (wy + 1) // 2
    n_src = 3 * nv
    n_blk = wx * nv
    width = feats2.shape[1] // 2
    members = out.shape[0]
    own_a, own_b, slots = place()

    copies = [
        pltpu.make_async_copy(arrived[ref].at[pl.ds(at * PACK_ROWS, PACK_ROWS), :], raw.at[slot], sems.at[k])
        for k, (ref, at, slot) in enumerate(slots)
    ]
    later = [pltpu.make_async_copy(src, dst, sems.at[n_dom + k]) for k, (src, dst) in enumerate(zip(model_in, model))]
    for copy in copies + later:
        copy.start()
    for copy in copies:
        copy.wait()

    none = n_dom * tiles
    count = jnp.int32(0)
    near = jnp.int32(0)
    for d in range(n_dom):
        a, b = d // wy, d % wy
        live = jnp.max(raw[d, 2 * tiles + 5 : 2 * tiles + 6, :]).astype(i32)
        da = lax.rem(a - own_a + 1 + wx, wx)
        db = lax.rem(b - own_b + 1 + wy, wy)
        touches = jnp.logical_and(da < 3, db < 3)
        for t in range(tiles):
            tile_list[count + t] = d * tiles + t
            near_list[near + t] = d * tiles + t
        count = count + live
        near = near + jnp.where(touches, live, 0)
    for t in range(CHUNK):
        tile_list[count + t] = none
        near_list[near + t] = none

    lane = iota((8, LANES), 1)
    for a in range(wx):
        for v in range(nv):
            low = raw[a * wy + 2 * v, 2 * tiles : 2 * tiles + 8, :]
            high = raw[a * wy + min(2 * v + 1, wy - 1), 2 * tiles : 2 * tiles + 8, :]
            posb[a * nv + v] = jnp.where(lane < 64, low, high)

    lid_s[none : none + 8, :] = jnp.full((8, LANES), -1, i32)
    cl_s[none : none + 8, :] = jnp.full((8, LANES), -1, i32)
    for ref in (spc, spn):
        ref[none : none + 8, :] = jnp.zeros((8, LANES), i32)
    unit[:, none : none + 8, :] = jnp.zeros((3, 8, LANES), f32)
    basis_s[none * 8 : none * 8 + 8, :] = jnp.zeros((8, LANES), f32)
    slope_s[none * 8 : none * 8 + 8, :] = jnp.zeros((8, LANES), f32)

    row = lane[0:1]
    for d in range(n_dom):
        a, b = d // wy, d % wy

        def ids(u, v, start):
            src = ((a + u - 1) % wx) * wy + (b + v - 1) % wy
            base = u * nv * LANES + ((b + v - 1) % wy) * 64 + 8192 * v
            skin = raw[src, 2 * tiles + 4 : 2 * tiles + 5, :].astype(i32) + base
            return pltpu.roll(skin, start, 1) if start else skin

        first = row + (nv * LANES + b * 64 + 8192)
        first = jnp.where(row >= 64, ids(0, 1, 64), first)
        first = jnp.where(row >= 96, ids(1, 0, 96), first)
        second = ids(1, 2, 0)
        second = jnp.where(row >= 32, ids(2, 1, 32), second)
        for k, (u, v) in enumerate(((0, 0), (0, 2), (2, 0), (2, 2))):
            second = jnp.where(row >= 64 + 8 * k, ids(u, v, 64 + 8 * k), second)
        center = raw[d, 0:tiles, :].astype(i32)
        entry = raw[d, tiles : 2 * tiles, :].astype(i32)
        wide = (8, LANES)
        code = jnp.where(
            entry < LANES,
            lane_pick(jnp.broadcast_to(first, wide), entry & 127),
            lane_pick(jnp.broadcast_to(second, wide), entry & 127),
        )
        side_y = lax.shift_right_logical(code, 13)
        lid = code & 8191
        side_x = (lid >= nv * LANES).astype(f32) + (lid >= 2 * nv * LANES).astype(f32) - 1.0
        clid = center + b * 64
        block = lax.shift_right_logical(lid, 7)
        got_n, got_c = [], []
        for q in range(4):
            value = None
            for s in range(n_src):
                src = ((a + s // nv - 1) % wx) * nv + s % nv
                picked = lane_pick(jnp.broadcast_to(posb[src, q : q + 1, :], wide), lid & 127)
                value = picked if value is None else jnp.where(block == s, picked, value)
            got_n.append(value)
            got_c.append(lane_pick(jnp.broadcast_to(posb[a * nv + b // 2, q : q + 1, :], wide), clid & 127))
        dx = got_n[0] + box_edge * side_x - got_c[0]
        dy = got_n[1] + box_edge * (side_y.astype(f32) - 1.0) - got_c[1]
        dz = got_n[2] - got_c[2]
        distance = jnp.sqrt(dx * dx + dy * dy + dz * dz + 1.0)
        inverse = 1.0 / distance
        cut = slice(d * tiles, (d + 1) * tiles)
        for q, part in enumerate((dx, dy, dz)):
            unit[q, cut, :] = part * inverse
        spn[cut, :] = got_n[3].astype(i32)
        spc[cut, :] = got_c[3].astype(i32)
        lid_s[cut, :] = lid
        cl_s[cut, :] = clid
        s1, c1 = sin_cos(distance * 0.25)
        env = jnp.exp(distance * (-1.0 / 32.0))
        c_k, s_k = [jnp.ones_like(c1), c1], [jnp.zeros_like(s1), s1]
        for k in range(2, 8):
            c_k.append(2.0 * c1 * c_k[-1] - c_k[-2])
            s_k.append(2.0 * c1 * s_k[-1] - s_k[-2])
        for k in range(8):
            basis = c_k[k] * env
            basis_s[pl.ds(d * 64 + k, 8, stride=8), :] = basis
            slope_s[pl.ds(d * 64 + k, 8, stride=8), :] = s_k[k] * env * (-k / 4.0) - basis * (1.0 / 32.0)

    for ref in (sums, grads):
        ref[...] = jnp.zeros(ref.shape, f32)
    for ref in (joined_s, lat_s, dpre_s, dz_s, back_s):
        ref[none] = jnp.zeros((width, LANES), f32)
    total[...] = jnp.zeros(total.shape, f32)

    def spots(tau):
        d = lax.shift_right_logical(tau, 3)
        a, b = lax.div(d, wy), lax.rem(d, wy)
        sources = [lax.rem(a + (s // nv - 1 + wx), wx) * nv + s % nv for s in range(n_src)]
        home = lax.rem(a, wx) * nv + lax.div(b, 2)
        return sources, home, lax.div(b, 2)

    atom = iota((LANES, LANES), 0)

    def hot(ids_row):
        return jnp.where(atom == ids_row, 1.0, 0.0)

    def side(parts):
        return jnp.concatenate(parts, axis=1)

    def forward(chunk, carry):
        taus = [tile_list[chunk * CHUNK + j] for j in range(CHUNK)]
        rhs = []
        sub = iota((8, LANES), 0)
        for tau in taus:
            hi, lo = halves(basis_s[pl.ds(pl.multiple_of(tau * 8, 8), 8), :])
            kinds = (sub == spc[pl.ds(tau, 1), :]).astype(f32) + (sub == spn[pl.ds(tau, 1), :]).astype(f32)
            rhs.append(jnp.concatenate([hi, lo, hi, kinds, kinds, jnp.zeros_like(hi)], axis=0).astype(bf16))
        both = jnp.dot(geo[...], side(rhs), preferred_element_type=f32)
        latent, latent_slope = silu_and_slope(both[:width])
        joined = both[width:]
        active, slope = silu_and_slope(product(dense[0], latent * joined))
        latent = latent + product(dense[1], active)
        for j, tau in enumerate(taus):
            cut = slice(j * LANES, (j + 1) * LANES)
            joined_s[tau] = joined[:, cut]
            dpre_s[tau] = latent_slope[:, cut]
            dz_s[tau] = slope[:, cut]
            lat_s[tau] = latent[:, cut]
            _, home, half = spots(tau)
            ids_row = cl_s[pl.ds(tau, 1), :] - half * LANES
            sums[home] += sum_to(active[:, cut], hot(ids_row).astype(bf16))
        return carry

    chunks = lax.div(count + (CHUNK - 1), CHUNK)
    for copy in later:
        copy.wait()
    weight_factors(*model, geo, dense, radial_back, columns)
    lax.fori_loop(0, chunks, forward, 0)

    sub = iota((8, LANES), 0)
    for k in range(n_blk):
        kinds = (sub == posb[k, 3:4, :].astype(i32)).astype(f32)
        empty = jnp.zeros_like(kinds)
        rhs = jnp.concatenate([empty, empty, empty, kinds, kinds, empty], axis=0).astype(bf16)
        start = jnp.dot(geo[...], rhs, preferred_element_type=f32)[width:]
        feats2[k] = jnp.concatenate(parts(start + product(dense[6], sums[k])), axis=0)

    def middle(chunk, carry):
        taus = [tile_list[chunk * CHUNK + j] for j in range(CHUNK)]
        joined, lids, places = [], [], []
        for tau in taus:
            sources, home, half = spots(tau)
            lid = lid_s[pl.ds(tau, 1), :]
            clid = cl_s[pl.ds(tau, 1), :]
            lids.append((lid, clid - half * LANES))
            places.append((sources, home, half))
        hot_rows = []
        for j, tau in enumerate(taus):
            sources, home, half = places[j]
            lid, clid = lids[j]
            hots = [hot(lid - s * LANES) for s in range(n_src)]
            own = hot(clid)
            for v in range(nv):
                here = own if nv == 1 else jnp.where(half == v, own, 0.0)
                hots[nv + v] = hots[nv + v] + here
            hot_rows.append(jnp.concatenate(hots, axis=0).astype(bf16))
            both = jnp.dot(side([feats2[s] for s in sources]), hot_rows[-1], preferred_element_type=f32)
            joined.append(both[:width] + both[width:])
        joined = side(joined)
        latent = side([lat_s[tau] for tau in taus])
        _, slope = silu_and_slope(product(dense[2], latent * joined))
        dmix = product(dense[3], slope)
        back = dmix * joined
        spread = dmix * latent
        for j, tau in enumerate(taus):
            cut = slice(j * LANES, (j + 1) * LANES)
            back_s[tau] = back[:, cut]
            sources, home, half = places[j]
            added = sum_to(spread[:, cut], hot_rows[j])
            for s in range(n_src):
                grads[sources[s]] += added[:, s * LANES : (s + 1) * LANES]
        return carry

    lax.fori_loop(0, chunks, middle, 0)

    for k in range(n_blk):
        pulls[k] = product(dense[7], grads[k] + columns[...])

    own_block = own_a * nv + lax.div(own_b, 2)

    def backward(chunk, carry):
        taus = [near_list[chunk * CHUNK + j] for j in range(CHUNK)]
        pulled = []
        for tau in taus:
            _, home, _ = spots(tau)
            pulled.append(lane_pick(pulls[home], cl_s[pl.ds(tau, 1), :] & 127))
        back = side([back_s[tau] for tau in taus])
        active = side(pulled) + product(dense[4], back)
        dmix = product(dense[5], active * side([dz_s[tau] for tau in taus]))
        dlat = back + dmix * side([joined_s[tau] for tau in taus])
        dbasis = product(radial_back[...], dlat * side([dpre_s[tau] for tau in taus]))
        moved = total[...]
        for j, tau in enumerate(taus):
            cut = slice(j * LANES, (j + 1) * LANES)
            slope = slope_s[pl.ds(pl.multiple_of(tau * 8, 8), 8), :]
            rows = []
            for m in range(members):
                along = jnp.sum(dbasis[m * 8 : (m + 1) * 8, cut] * slope, axis=0, keepdims=True)
                rows += [along * unit[q, pl.ds(tau, 1), :] for q in range(3)]
            rows.append(jnp.zeros((8 - 3 * members, LANES), f32))
            sources, home, half = spots(tau)
            lid = lid_s[pl.ds(tau, 1), :]
            clid = cl_s[pl.ds(tau, 1), :]
            hit = jnp.full((1, LANES), -1, i32)
            for s in range(n_src):
                this = jnp.where(sources[s] == own_block, s, -2)
                hit = jnp.where(lax.shift_right_arithmetic(lid, 7) == this, lid & 127, hit)
            chit = jnp.where(home == own_block, clid - half * LANES, -1)
            many = hot(hit) - hot(chit)
            moved = moved + sum_to(jnp.concatenate(rows, axis=0), many.astype(bf16))
        total[...] = moved
        return carry

    lax.fori_loop(0, lax.div(near + (CHUNK - 1), CHUNK), backward, 0)

    result = -total[...]
    result = jnp.where(lax.rem(own_b, 2) == 1, pltpu.roll(result, 64, 1), result)
    for m in range(members):
        for q in range(3):
            out[m, q, 0] = result[m * 3 + q : m * 3 + q + 1, 0:64]


def window(size):
    return min(size, 2 * REACH + 1)


def shift(value, axis, by):
    peers = lax.axis_size(axis)
    return lax.ppermute(value, axis, [(i, (i + by) % peers) for i in range(peers)])


def swap(value, by_core):
    sizes = [lax.axis_size(axis) for axis in ("gx", "gy", "gz")]
    pairs = []
    for a in range(sizes[0]):
        for b in range(sizes[1]):
            for c in range(sizes[2]):
                dx, dy, dz = by_core[c]
                pairs.append(((a * sizes[1] + b) * sizes[2] + c, ((a ^ dx) * sizes[1] + (b ^ dy)) * sizes[2] + (c ^ dz)))
    return lax.ppermute(value, ("gx", "gy", "gz"), pairs)


def gathered(own, gx, gy):
    if gx == 4 and gy == 2 and lax.axis_size("gz") == 2:
        fetch = (((0, 1), (2, 1)), ((1, 0), (3, 0)), ((1, 1), (3, 1)))
        far = swap(own, ((2, 0, 0), (2, 0, 0)))
        fetched = [swap(own, (low + (0,), high + (0,))) for low, high in fetch]
        handed = [swap(value, ((0, 0, 1), (0, 0, 1))) for value in fetched]

        def place():
            a, b, c = lax.axis_index("gx"), lax.axis_index("gy"), lax.axis_index("gz")
            slots = [(0, 0, a * 2 + b), (1, 0, (a ^ 2) * 2 + b)]
            for k, (low, high) in enumerate(fetch):
                mine = [jnp.where(c == 0, low[q], high[q]) for q in range(2)]
                other = [jnp.where(c == 0, high[q], low[q]) for q in range(2)]
                slots.append((2 + k, 0, (a ^ mine[0]) * 2 + (b ^ mine[1])))
                slots.append((5 + k, 0, (a ^ other[0]) * 2 + (b ^ other[1])))
            return a, b, slots

        return [own, far] + fetched + handed, place
    wx, wy = window(gx), window(gy)
    steps = list(range(wy // 2 + 1)) + list(range(wy // 2 + 1 - wy, 0))
    column = jnp.concatenate([own if s == 0 else shift(own, "gy", -s) for s in steps], axis=0)
    steps_x = list(range(wx // 2 + 1)) + list(range(wx // 2 + 1 - wx, 0))
    arrays = [column if s == 0 else shift(column, "gx", -s) for s in steps_x]

    def place():
        slots = [(k, at, k * wy + at) for k in range(wx) for at in range(wy)]
        return jnp.int32(0), jnp.int32(0), slots

    return arrays, place


def on_device(
    positions, species, centers, neighbours, masks, skin, embed, radial, w_mix, w_latent, w_update, readout
):
    gx, gy = lax.axis_size("gx"), lax.axis_size("gy")
    atoms = positions.shape[-1]
    members, _, channels = embed.shape
    width = members * channels
    own = pl.pallas_call(
        pack_kernel, out_shape=jax.ShapeDtypeStruct((PACK_ROWS, LANES), f32), name="pack"
    )(positions, species, centers, neighbours, masks, skin)
    model = (jnp.transpose(embed, (1, 0, 2)), radial, w_mix, w_latent, w_update, readout)
    arrays, place = gathered(own, gx, gy)
    wx, wy = window(gx), window(gy)
    n_dom = wx * wy
    n_tiles = n_dom * 8
    n_blk = wx * ((wy + 1) // 2)
    held = 5 * (n_tiles + 1) * width * LANES * 4 + 8 * 1024 * 1024
    per_tile = pltpu.VMEM((n_tiles + 1, width, LANES), f32)
    per_block = pltpu.VMEM((n_blk, width, LANES), f32)
    row_ids = pltpu.VMEM((n_tiles + 8, LANES), i32)

    def body(*refs):
        force_kernel(wx, wy, place, len(arrays), *refs)

    return pl.pallas_call(
        body,
        out_shape=jax.ShapeDtypeStruct((members, 3, 1, 1, atoms), f32),
        scratch_shapes=[
            pltpu.VMEM((n_dom, PACK_ROWS, LANES), f32),
            pltpu.VMEM((n_blk, 8, LANES), f32),
            row_ids,
            row_ids,
            row_ids,
            row_ids,
            pltpu.VMEM((3, n_tiles + 8, LANES), f32),
            pltpu.VMEM((n_tiles * 8 + 8, LANES), f32),
            pltpu.VMEM((n_tiles * 8 + 8, LANES), f32),
            pltpu.VMEM((n_blk, 2 * width, LANES), bf16),
            per_block,
            per_block,
            per_block,
            per_tile,
            per_tile,
            per_tile,
            per_tile,
            per_tile,
            pltpu.VMEM((8, LANES), f32),
            pltpu.SMEM((n_tiles + 2 * CHUNK,), i32),
            pltpu.SMEM((n_tiles + 2 * CHUNK,), i32),
        ]
        + [
            pltpu.VMEM((2 * width, 48), bf16),
            pltpu.VMEM((8, width, 3 * width), bf16),
            pltpu.VMEM((members * 8, 3 * width), bf16),
            pltpu.VMEM((width, LANES), f32),
        ]
        + [pltpu.VMEM(part.shape, part.dtype) for part in model]
        + [pltpu.SemaphoreType.DMA((n_dom + len(model),))],
        in_specs=[pl.BlockSpec(memory_space=pl.ANY)] * len(arrays) + [pl.BlockSpec(memory_space=pltpu.HBM)] * len(model),
        compiler_params=pltpu.CompilerParams(vmem_limit_bytes=held),
        name="forces",
    )(*arrays, *model)


def solution(mesh):
    return jax.shard_map(
        on_device,
        mesh=mesh,
        in_specs=(
            P(None, ("groups", "gx"), "gy", None),
            P(("groups", "gx"), "gy", None),
            P(("groups", "gx"), "gy", None),
            P(("groups", "gx"), "gy", None),
            P(("groups", "gx"), "gy", None),
            P(("groups", "gx"), "gy", None),
            P("gz", None, None),
            P("gz", None, None),
            P("gz", None, None, None),
            P("gz", None, None, None),
            P("gz", None, None, None),
            P("gz", None),
        ),
        out_specs=P("gz", None, ("groups", "gx"), "gy", None),
        check_vma=False,
    )
```

```python
import jax
import jax.numpy as jnp
from jax import lax
from jax.experimental import pallas as pl
from jax.experimental.pallas import tpu as pltpu
from jax.sharding import PartitionSpec as P

NEIGH = 16
box_edge = 20.0
energy_scale = 16.0
REACH = 3
LANES = 128
CHUNK = 8
PACK_ROWS = 24
f32 = jnp.float32
bf16 = jnp.bfloat16
i32 = jnp.int32


def iota(shape, dim):
    return lax.broadcasted_iota(i32, shape, dim)


def halves(x):
    hi = x.astype(bf16).astype(f32)
    return hi, x - hi


def pack_kernel(pos, species, centers, neighbours, masks, skin, out):
    tiles = centers.shape[-1] // LANES
    atoms = pos.shape[-1]
    ghosts = skin.shape[-1]
    out[...] = jnp.zeros(out.shape, f32)
    live = jnp.zeros((1, LANES), f32)
    for t in range(tiles):
        cut = slice(t * LANES, (t + 1) * LANES)
        out[t : t + 1, :] = centers[0, :, cut].astype(f32)
        out[tiles + t : tiles + t + 1, :] = neighbours[0, :, cut].astype(f32)
        live = live + masks[0, :, cut].astype(f32)
    base = 2 * tiles
    for q in range(3):
        row = pos[q, 0]
        out[base + q : base + q + 1, :] = jnp.concatenate([row, row], axis=1)
    row = species[0].astype(f32)
    out[base + 3 : base + 4, :] = jnp.concatenate([row, row], axis=1)
    out[base + 4 : base + 5, 0:ghosts] = skin[0].astype(f32)
    out[base + 5 : base + 6, :] = live


def block_diag(blocks):
    rows = []
    for at, block in enumerate(blocks):
        parts = [block if k == at else jnp.zeros((block.shape[0], other.shape[1]), f32) for k, other in enumerate(blocks)]
        rows.append(jnp.concatenate(parts, axis=1))
    return jnp.concatenate(rows, axis=0)


def split_left(matrix):
    hi, lo = halves(matrix)
    return jnp.concatenate([hi, hi, lo], axis=1).astype(bf16)


def parts(x):
    hi = x.astype(bf16)
    return hi, (x - hi.astype(f32)).astype(bf16)


def weight_factors(embed, radial, w_mix, w_latent, w_update, readout, geo, dense, radial_back, columns):
    elements, members, channels = embed.shape
    width = members * channels
    embed_t = jnp.concatenate([embed[:, m, :].T for m in range(members)], axis=0)
    embed_t = jnp.concatenate([embed_t, jnp.zeros((width, 8 - elements), f32)], axis=1)
    radial_t = jnp.concatenate([radial[m].T for m in range(members)], axis=0)
    r_hi, r_lo = halves(0.5 * radial_t)
    e_hi, e_lo = halves(embed_t)
    none = jnp.zeros_like(r_hi)
    geo[...] = jnp.concatenate(
        [
            jnp.concatenate([r_hi, r_hi, r_lo, none, none, none], axis=1),
            jnp.concatenate([none, none, none, e_hi, e_lo, none], axis=1),
        ],
        axis=0,
    ).astype(bf16)
    mix0 = block_diag([w_mix[m, 0] for m in range(members)])
    mix1 = block_diag([w_mix[m, 1] for m in range(members)])
    latent = block_diag([w_latent[m, 0] for m in range(members)])
    update0 = block_diag([w_update[m, 0] for m in range(members)])
    update1 = block_diag([w_update[m, 1] for m in range(members)])
    radial_back[...] = split_left(0.5 * block_diag([radial[m] for m in range(members)]))
    read_row = jnp.concatenate([readout[m : m + 1, :] for m in range(members)], axis=1)
    eye = (iota((width, width), 0) == iota((width, width), 1)).astype(f32)
    read = jnp.sum(eye * read_row, axis=1, keepdims=True)
    pull = jnp.sum(update1.T * read, axis=0, keepdims=True) * (energy_scale / NEIGH)
    columns[...] = jnp.broadcast_to(read * energy_scale, (width, LANES))
    factors = (
        0.5 * mix0.T, latent.T, 0.5 * mix1.T, 0.5 * mix1 * pull, latent, 0.5 * mix0,
        update0.T * (1.0 / NEIGH), update0 * (1.0 / NEIGH),
    )
    for at, matrix in enumerate(factors):
        dense[at] = split_left(matrix)


def lane_pick(table, lanes):
    return jnp.take_along_axis(table, jnp.broadcast_to(lanes, table.shape), axis=1, mode="promise_in_bounds")


def product(left, x):
    hi, lo = parts(x)
    return jnp.dot(left, jnp.concatenate([hi, lo, hi], axis=0), preferred_element_type=f32)


def sum_to(values, hot):
    hi, lo = parts(values)
    both = lax.dot_general(
        jnp.concatenate([hi, lo], axis=0), hot, (((1,), (1,)), ((), ())), preferred_element_type=f32
    )
    return both[: values.shape[0]] + both[values.shape[0] :]


def silu(h):
    return h + h * jnp.tanh(h)


def silu_and_slope(h):
    t = jnp.tanh(h)
    p = 1.0 + t
    return h * p, p + p * (h - h * t)


def sin_cos(x):
    turns = jnp.floor(x * 0.15915494309189535 + 0.5)
    r = (x - turns * 6.28125) - turns * 1.9353071795864769e-3
    h = 0.5 * r
    q = h * h
    s = h * (1.0 + q * (-1 / 6 + q * (1 / 120 + q * (-1 / 5040 + q * (1 / 362880 + q * (-1 / 39916800 + q * (1 / 6227020800)))))))
    c = 1.0 + q * (-1 / 2 + q * (1 / 24 + q * (-1 / 720 + q * (1 / 40320 + q * (-1 / 3628800 + q * (1 / 479001600 - q * (1 / 87178291200)))))))
    return 2.0 * s * c, 1.0 - 2.0 * s * s


def force_kernel(wx, wy, place, n_in, *refs):
    arrived = refs[:n_in]
    model_in, out = refs[n_in : n_in + 6], refs[n_in + 6]
    (raw, posb, lid_s, cl_s, spc, spn, unit, basis_s, slope_s, feats2, sums, grads, pulls,
     joined_s, lat_s, dpre_s, dz_s, back_s, total, tile_list, near_list,
     hold_a, hold_b, hold_hot, geo, dense, radial_back, columns, *model, sems) = refs[n_in + 7 :]
    tiles = 8
    n_dom = wx * wy
    nv = (wy + 1) // 2
    n_src = 3 * nv
    n_blk = wx * nv
    width = feats2.shape[1] // 2
    members = out.shape[0]
    own_a, own_b, slots = place()

    copies = [
        pltpu.make_async_copy(arrived[ref].at[pl.ds(at * PACK_ROWS, PACK_ROWS), :], raw.at[slot], sems.at[k])
        for k, (ref, at, slot) in enumerate(slots)
    ]
    later = [pltpu.make_async_copy(src, dst, sems.at[n_dom + k]) for k, (src, dst) in enumerate(zip(model_in, model))]
    for copy in copies + later:
        copy.start()
    for copy in copies:
        copy.wait()

    none = n_dom * tiles
    count = jnp.int32(0)
    near = jnp.int32(0)
    for t in range(CHUNK):
        tile_list[t] = none
        near_list[t] = none
    for d in range(n_dom):
        a, b = d // wy, d % wy
        live = jnp.max(raw[d, 2 * tiles + 5 : 2 * tiles + 6, :]).astype(i32)
        da = lax.rem(a - own_a + 1 + wx, wx)
        db = lax.rem(b - own_b + 1 + wy, wy)
        touches = jnp.logical_and(da < 3, db < 3)
        for t in range(tiles):
            tile_list[CHUNK + count + t] = d * tiles + t
            near_list[CHUNK + near + t] = d * tiles + t
        count = count + live
        near = near + jnp.where(touches, live, 0)
    for t in range(2 * CHUNK):
        tile_list[CHUNK + count + t] = none
        near_list[CHUNK + near + t] = none
    chunks = lax.div(count + (CHUNK - 1), CHUNK)
    near_chunks = lax.div(near + (CHUNK - 1), CHUNK)

    def tiles_of(tile_ids, chunk):
        return [tile_ids[chunk * CHUNK + j] for j in range(CHUNK)]

    def cut(j):
        return slice(j * LANES, (j + 1) * LANES)

    lane = iota((8, LANES), 1)
    for a in range(wx):
        for v in range(nv):
            low = raw[a * wy + 2 * v, 2 * tiles : 2 * tiles + 8, :]
            high = raw[a * wy + min(2 * v + 1, wy - 1), 2 * tiles : 2 * tiles + 8, :]
            posb[a * nv + v] = jnp.where(lane < 64, low, high)

    lid_s[none : none + 8, :] = jnp.full((8, LANES), -1, i32)
    cl_s[none : none + 8, :] = jnp.full((8, LANES), -1, i32)
    for ref in (spc, spn):
        ref[none : none + 8, :] = jnp.zeros((8, LANES), i32)
    unit[:, none : none + 8, :] = jnp.zeros((3, 8, LANES), f32)
    basis_s[none * 8 : none * 8 + 8, :] = jnp.zeros((8, LANES), f32)
    slope_s[none * 8 : none * 8 + 8, :] = jnp.zeros((8, LANES), f32)

    row = lane[0:1]
    for d in range(n_dom):
        a, b = d // wy, d % wy

        def ids(u, v, start):
            src = ((a + u - 1) % wx) * wy + (b + v - 1) % wy
            base = u * nv * LANES + ((b + v - 1) % wy) * 64 + 8192 * v
            skin = raw[src, 2 * tiles + 4 : 2 * tiles + 5, :].astype(i32) + base
            return pltpu.roll(skin, start, 1) if start else skin

        first = row + (nv * LANES + b * 64 + 8192)
        first = jnp.where(row >= 64, ids(0, 1, 64), first)
        first = jnp.where(row >= 96, ids(1, 0, 96), first)
        second = ids(1, 2, 0)
        second = jnp.where(row >= 32, ids(2, 1, 32), second)
        for k, (u, v) in enumerate(((0, 0), (0, 2), (2, 0), (2, 2))):
            second = jnp.where(row >= 64 + 8 * k, ids(u, v, 64 + 8 * k), second)
        center = raw[d, 0:tiles, :].astype(i32)
        entry = raw[d, tiles : 2 * tiles, :].astype(i32)
        wide = (8, LANES)
        code = jnp.where(
            entry < LANES,
            lane_pick(jnp.broadcast_to(first, wide), entry & 127),
            lane_pick(jnp.broadcast_to(second, wide), entry & 127),
        )
        side_y = lax.shift_right_logical(code, 13)
        lid = code & 8191
        side_x = (lid >= nv * LANES).astype(f32) + (lid >= 2 * nv * LANES).astype(f32) - 1.0
        clid = center + b * 64
        block = lax.shift_right_logical(lid, 7)
        got_n, got_c = [], []
        for q in range(4):
            value = None
            for s in range(n_src):
                src = ((a + s // nv - 1) % wx) * nv + s % nv
                picked = lane_pick(jnp.broadcast_to(posb[src, q : q + 1, :], wide), lid & 127)
                value = picked if value is None else jnp.where(block == s, picked, value)
            got_n.append(value)
            got_c.append(lane_pick(jnp.broadcast_to(posb[a * nv + b // 2, q : q + 1, :], wide), clid & 127))
        dx = got_n[0] + box_edge * side_x - got_c[0]
        dy = got_n[1] + box_edge * (side_y.astype(f32) - 1.0) - got_c[1]
        dz = got_n[2] - got_c[2]
        distance = jnp.sqrt(dx * dx + dy * dy + dz * dz + 1.0)
        inverse = 1.0 / distance
        rows = slice(d * tiles, (d + 1) * tiles)
        for q, part in enumerate((dx, dy, dz)):
            unit[q, rows, :] = part * inverse
        spn[rows, :] = got_n[3].astype(i32)
        spc[rows, :] = got_c[3].astype(i32)
        lid_s[rows, :] = lid
        cl_s[rows, :] = clid
        s1, c1 = sin_cos(distance * 0.25)
        env = jnp.exp(distance * (-1.0 / 32.0))
        c_k, s_k = [jnp.ones_like(c1), c1], [jnp.zeros_like(s1), s1]
        for k in range(2, 8):
            c_k.append(2.0 * c1 * c_k[-1] - c_k[-2])
            s_k.append(2.0 * c1 * s_k[-1] - s_k[-2])
        for k in range(8):
            basis = c_k[k] * env
            basis_s[pl.ds(d * 64 + k, 8, stride=8), :] = basis
            slope_s[pl.ds(d * 64 + k, 8, stride=8), :] = s_k[k] * env * (-k / 4.0) - basis * (1.0 / 32.0)

    for ref in (sums, grads):
        ref[...] = jnp.zeros(ref.shape, f32)
    for ref in (joined_s, lat_s, dpre_s, dz_s, back_s):
        ref[none] = jnp.zeros((width, LANES), f32)
    total[...] = jnp.zeros(total.shape, f32)

    def spots(tau):
        d = lax.shift_right_logical(tau, 3)
        a, b = lax.div(d, wy), lax.rem(d, wy)
        sources = [lax.rem(a + (s // nv - 1 + wx), wx) * nv + s % nv for s in range(n_src)]
        home = lax.rem(a, wx) * nv + lax.div(b, 2)
        return sources, home, lax.div(b, 2)

    atom = iota((LANES, LANES), 0).astype(bf16)
    one = jnp.ones((LANES, LANES), bf16)
    zero = jnp.zeros((LANES, LANES), bf16)

    def hot(ids_row):
        return jnp.where(atom == ids_row.astype(f32).astype(bf16), one, zero)

    def side(parts):
        return jnp.concatenate(parts, axis=1)

    def forward(chunk, carry):
        old = tiles_of(tile_list, chunk)
        new = tiles_of(tile_list, chunk + 1)
        old_latent = side([lat_s[tau] for tau in old])
        mixed = old_latent * side([joined_s[tau] for tau in old])
        sub = iota((8, LANES), 0)
        rhs = []
        for tau in new:
            hi, lo = halves(basis_s[pl.ds(pl.multiple_of(tau * 8, 8), 8), :])
            kinds = (sub == spc[pl.ds(tau, 1), :]).astype(f32) + (sub == spn[pl.ds(tau, 1), :]).astype(f32)
            rhs.append(jnp.concatenate([hi, lo, hi, kinds, kinds, jnp.zeros_like(hi)], axis=0).astype(bf16))
        homes, hots = [], []
        for tau in old:
            _, home, half = spots(tau)
            homes.append(home)
            hots.append(hot(cl_s[pl.ds(tau, 1), :] - half * LANES))
        z = product(dense[0], mixed)
        both = jnp.dot(geo[...], side(rhs), preferred_element_type=f32)
        active, slope = silu_and_slope(z)
        latent, latent_slope = silu_and_slope(both[:width])
        added = [sum_to(active[:, cut(j)], hots[j]) for j in range(CHUNK)]
        old_latent = old_latent + product(dense[1], active)
        for j, tau in enumerate(new):
            joined_s[tau] = both[width:, cut(j)]
            dpre_s[tau] = latent_slope[:, cut(j)]
            lat_s[tau] = latent[:, cut(j)]
        for j, tau in enumerate(old):
            dz_s[tau] = slope[:, cut(j)]
            lat_s[tau] = old_latent[:, cut(j)]
            sums[homes[j]] += added[j]
        return carry

    for copy in later:
        copy.wait()
    weight_factors(*model, geo, dense, radial_back, columns)
    lax.fori_loop(0, chunks + 1, forward, 0)

    sub = iota((8, LANES), 0)
    for k in range(n_blk):
        kinds = (sub == posb[k, 3:4, :].astype(i32)).astype(f32)
        empty = jnp.zeros_like(kinds)
        rhs = jnp.concatenate([empty, empty, empty, kinds, kinds, empty], axis=0).astype(bf16)
        start = jnp.dot(geo[...], rhs, preferred_element_type=f32)[width:]
        feats2[k] = jnp.concatenate(parts(start + product(dense[6], sums[k])), axis=0)

    def middle(chunk, carry):
        old = tiles_of(tile_list, chunk)
        new = tiles_of(tile_list, chunk + 1)
        old_joined, old_slope = hold_a[...], hold_b[...]
        old_hots = [hold_hot[j] for j in range(CHUNK)]
        old_latent = side([lat_s[tau] for tau in old])
        old_sources = [spots(tau)[0] for tau in old]
        latent = side([lat_s[tau] for tau in new])
        joined, hots = [], []
        for tau in new:
            sources, _, half = spots(tau)
            lid = lid_s[pl.ds(tau, 1), :]
            own = hot(cl_s[pl.ds(tau, 1), :] - half * LANES)
            rows = [hot(lid - s * LANES) for s in range(n_src)]
            for v in range(nv):
                rows[nv + v] = rows[nv + v] + (own if nv == 1 else jnp.where(half == v, own, zero))
            hots.append(jnp.concatenate(rows, axis=0))
            both = jnp.dot(side([feats2[s] for s in sources]), hots[-1], preferred_element_type=f32)
            joined.append(both[:width] + both[width:])
        dmix = product(dense[3], old_slope)
        joined = side(joined)
        z = product(dense[2], latent * joined)
        spread = dmix * old_latent
        added = [sum_to(spread[:, cut(j)], old_hots[j]) for j in range(CHUNK)]
        back = dmix * old_joined
        _, slope = silu_and_slope(z)
        hold_a[...] = joined
        hold_b[...] = slope
        for j in range(CHUNK):
            hold_hot[j] = hots[j]
        for j, tau in enumerate(old):
            back_s[tau] = back[:, cut(j)]
            for s in range(n_src):
                grads[old_sources[j][s]] += added[j][:, s * LANES : (s + 1) * LANES]
        return carry

    hold_b[...] = jnp.zeros(hold_b.shape, f32)
    hold_a[...] = jnp.zeros(hold_a.shape, f32)
    hold_hot[...] = jnp.zeros(hold_hot.shape, bf16)
    lax.fori_loop(0, chunks + 1, middle, 0)

    for k in range(n_blk):
        pulls[k] = product(dense[7], grads[k] + columns[...])

    own_block = own_a * nv + lax.div(own_b, 2)

    def backward(chunk, carry):
        old = tiles_of(near_list, chunk)
        new = tiles_of(near_list, chunk + 1)
        old_pre = hold_a[...]
        slopes = [slope_s[pl.ds(pl.multiple_of(tau * 8, 8), 8), :] for tau in old]
        units = [[unit[q, pl.ds(tau, 1), :] for q in range(3)] for tau in old]
        back = side([back_s[tau] for tau in new])
        dz = side([dz_s[tau] for tau in new])
        joined = side([joined_s[tau] for tau in new])
        dpre = side([dpre_s[tau] for tau in new])
        pulled = []
        for tau in new:
            _, home, _ = spots(tau)
            pulled.append(lane_pick(pulls[home], cl_s[pl.ds(tau, 1), :] & 127))
        manys = []
        for tau in old:
            sources, home, half = spots(tau)
            lid = lid_s[pl.ds(tau, 1), :]
            hit = jnp.full((1, LANES), -1, i32)
            for s in range(n_src):
                this = jnp.where(sources[s] == own_block, s, -2)
                hit = jnp.where(lax.shift_right_arithmetic(lid, 7) == this, lid & 127, hit)
            chit = jnp.where(home == own_block, cl_s[pl.ds(tau, 1), :] - half * LANES, -1)
            manys.append(hot(hit) - hot(chit))
        dbasis = product(radial_back[...], old_pre)
        active = side(pulled) + product(dense[4], back)
        moved = total[...]
        for j in range(CHUNK):
            rows = []
            for m in range(members):
                along = jnp.sum(dbasis[m * 8 : (m + 1) * 8, cut(j)] * slopes[j], axis=0, keepdims=True)
                rows += [along * units[j][q] for q in range(3)]
            rows.append(jnp.zeros((8 - 3 * members, LANES), f32))
            moved = moved + sum_to(jnp.concatenate(rows, axis=0), manys[j])
        dmix = product(dense[5], active * dz)
        hold_a[...] = (back + dmix * joined) * dpre
        total[...] = moved
        return carry

    hold_a[...] = jnp.zeros(hold_a.shape, f32)
    lax.fori_loop(0, near_chunks + 1, backward, 0)

    result = -total[...]
    result = jnp.where(lax.rem(own_b, 2) == 1, pltpu.roll(result, 64, 1), result)
    for m in range(members):
        for q in range(3):
            out[m, q, 0] = result[m * 3 + q : m * 3 + q + 1, 0:64]


def window(size):
    return min(size, 2 * REACH + 1)


def shift(value, axis, by):
    peers = lax.axis_size(axis)
    return lax.ppermute(value, axis, [(i, (i + by) % peers) for i in range(peers)])


def swap(value, by_core):
    sizes = [lax.axis_size(axis) for axis in ("gx", "gy", "gz")]
    pairs = []
    for a in range(sizes[0]):
        for b in range(sizes[1]):
            for c in range(sizes[2]):
                dx, dy, dz = by_core[c]
                pairs.append(((a * sizes[1] + b) * sizes[2] + c, ((a ^ dx) * sizes[1] + (b ^ dy)) * sizes[2] + (c ^ dz)))
    return lax.ppermute(value, ("gx", "gy", "gz"), pairs)


def gathered(own, gx, gy):
    if gx == 4 and gy == 2 and lax.axis_size("gz") == 2:
        fetch = (((0, 1), (2, 1)), ((1, 0), (3, 0)), ((1, 1), (3, 1)))
        far = swap(own, ((2, 0, 0), (2, 0, 0)))
        fetched = [swap(own, (low + (0,), high + (0,))) for low, high in fetch]
        handed = [swap(value, ((0, 0, 1), (0, 0, 1))) for value in fetched]

        def place():
            a, b, c = lax.axis_index("gx"), lax.axis_index("gy"), lax.axis_index("gz")
            slots = [(0, 0, a * 2 + b), (1, 0, (a ^ 2) * 2 + b)]
            for k, (low, high) in enumerate(fetch):
                mine = [jnp.where(c == 0, low[q], high[q]) for q in range(2)]
                other = [jnp.where(c == 0, high[q], low[q]) for q in range(2)]
                slots.append((2 + k, 0, (a ^ mine[0]) * 2 + (b ^ mine[1])))
                slots.append((5 + k, 0, (a ^ other[0]) * 2 + (b ^ other[1])))
            return a, b, slots

        return [own, far] + fetched + handed, place
    wx, wy = window(gx), window(gy)
    steps = list(range(wy // 2 + 1)) + list(range(wy // 2 + 1 - wy, 0))
    column = jnp.concatenate([own if s == 0 else shift(own, "gy", -s) for s in steps], axis=0)
    steps_x = list(range(wx // 2 + 1)) + list(range(wx // 2 + 1 - wx, 0))
    arrays = [column if s == 0 else shift(column, "gx", -s) for s in steps_x]

    def place():
        slots = [(k, at, k * wy + at) for k in range(wx) for at in range(wy)]
        return jnp.int32(0), jnp.int32(0), slots

    return arrays, place


def on_device(
    positions, species, centers, neighbours, masks, skin, embed, radial, w_mix, w_latent, w_update, readout
):
    gx, gy = lax.axis_size("gx"), lax.axis_size("gy")
    atoms = positions.shape[-1]
    members, _, channels = embed.shape
    width = members * channels
    own = pl.pallas_call(
        pack_kernel, out_shape=jax.ShapeDtypeStruct((PACK_ROWS, LANES), f32), name="pack"
    )(positions, species, centers, neighbours, masks, skin)
    model = (jnp.transpose(embed, (1, 0, 2)), radial, w_mix, w_latent, w_update, readout)
    arrays, place = gathered(own, gx, gy)
    wx, wy = window(gx), window(gy)
    n_dom = wx * wy
    n_tiles = n_dom * 8
    n_blk = wx * ((wy + 1) // 2)
    per_tile = pltpu.VMEM((n_tiles + 1, width, LANES), f32)
    per_block = pltpu.VMEM((n_blk, width, LANES), f32)
    row_ids = pltpu.VMEM((n_tiles + 8, LANES), i32)

    def body(*refs):
        force_kernel(wx, wy, place, len(arrays), *refs)

    return pl.pallas_call(
        body,
        out_shape=jax.ShapeDtypeStruct((members, 3, 1, 1, atoms), f32),
        scratch_shapes=[
            pltpu.VMEM((n_dom, PACK_ROWS, LANES), f32),
            pltpu.VMEM((n_blk, 8, LANES), f32),
            row_ids,
            row_ids,
            row_ids,
            row_ids,
            pltpu.VMEM((3, n_tiles + 8, LANES), f32),
            pltpu.VMEM((n_tiles * 8 + 8, LANES), f32),
            pltpu.VMEM((n_tiles * 8 + 8, LANES), f32),
            pltpu.VMEM((n_blk, 2 * width, LANES), bf16),
            per_block,
            per_block,
            per_block,
            per_tile,
            per_tile,
            per_tile,
            per_tile,
            per_tile,
            pltpu.VMEM((8, LANES), f32),
            pltpu.SMEM((n_tiles + 3 * CHUNK,), i32),
            pltpu.SMEM((n_tiles + 3 * CHUNK,), i32),
            pltpu.VMEM((width, CHUNK * LANES), f32),
            pltpu.VMEM((width, CHUNK * LANES), f32),
            pltpu.VMEM((CHUNK, 3 * n_blk // wx * LANES, LANES), bf16),
        ]
        + [
            pltpu.VMEM((2 * width, 48), bf16),
            pltpu.VMEM((8, width, 3 * width), bf16),
            pltpu.VMEM((members * 8, 3 * width), bf16),
            pltpu.VMEM((width, LANES), f32),
        ]
        + [pltpu.VMEM(part.shape, part.dtype) for part in model]
        + [pltpu.SemaphoreType.DMA((n_dom + len(model),))],
        in_specs=[pl.BlockSpec(memory_space=pl.ANY)] * len(arrays) + [pl.BlockSpec(memory_space=pltpu.HBM)] * len(model),
        compiler_params=pltpu.CompilerParams(vmem_limit_bytes=60 * 1024 * 1024),
        name="forces",
    )(*arrays, *model)


def solution(mesh):
    return jax.shard_map(
        on_device,
        mesh=mesh,
        in_specs=(
            P(None, ("groups", "gx"), "gy", None),
            P(("groups", "gx"), "gy", None),
            P(("groups", "gx"), "gy", None),
            P(("groups", "gx"), "gy", None),
            P(("groups", "gx"), "gy", None),
            P(("groups", "gx"), "gy", None),
            P("gz", None, None),
            P("gz", None, None),
            P("gz", None, None, None),
            P("gz", None, None, None),
            P("gz", None, None, None),
            P("gz", None),
        ),
        out_specs=P("gz", None, ("groups", "gx"), "gy", None),
        check_vma=False,
    )
```

```python
import jax
import jax.numpy as jnp
from jax import lax
from jax.experimental import pallas as pl
from jax.experimental.pallas import tpu as pltpu
from jax.sharding import PartitionSpec as P

NEIGH = 16
box_edge = 20.0
energy_scale = 16.0
REACH = 3
LANES = 128
CHUNK = 8
PACK_ROWS = 24
f32 = jnp.float32
bf16 = jnp.bfloat16
i32 = jnp.int32


def iota(shape, dim):
    return lax.broadcasted_iota(i32, shape, dim)


def halves(x):
    hi = x.astype(bf16).astype(f32)
    return hi, x - hi


def pack_kernel(pos, species, centers, neighbours, masks, skin, out):
    tiles = centers.shape[-1] // LANES
    atoms = pos.shape[-1]
    ghosts = skin.shape[-1]
    out[...] = jnp.zeros(out.shape, f32)
    live = jnp.zeros((1, LANES), f32)
    for t in range(tiles):
        cut = slice(t * LANES, (t + 1) * LANES)
        out[t : t + 1, :] = centers[0, :, cut].astype(f32)
        out[tiles + t : tiles + t + 1, :] = neighbours[0, :, cut].astype(f32)
        live = live + masks[0, :, cut].astype(f32)
    base = 2 * tiles
    for q in range(3):
        row = pos[q, 0]
        out[base + q : base + q + 1, :] = jnp.concatenate([row, row], axis=1)
    row = species[0].astype(f32)
    out[base + 3 : base + 4, :] = jnp.concatenate([row, row], axis=1)
    out[base + 4 : base + 5, 0:ghosts] = skin[0].astype(f32)
    out[base + 5 : base + 6, :] = live


def block_diag(blocks):
    rows = []
    for at, block in enumerate(blocks):
        parts = [block if k == at else jnp.zeros((block.shape[0], other.shape[1]), f32) for k, other in enumerate(blocks)]
        rows.append(jnp.concatenate(parts, axis=1))
    return jnp.concatenate(rows, axis=0)


def split_left(matrix):
    hi, lo = halves(matrix)
    return jnp.concatenate([hi, hi, lo], axis=1).astype(bf16)


def parts(x):
    hi = x.astype(bf16)
    return hi, (x - hi.astype(f32)).astype(bf16)


def weight_factors(embed, radial, w_mix, w_latent, w_update, readout, geo, dense, radial_back, columns):
    elements, members, channels = embed.shape
    width = members * channels
    embed_t = jnp.concatenate([embed[:, m, :].T for m in range(members)], axis=0)
    embed_t = jnp.concatenate([embed_t, jnp.zeros((width, 8 - elements), f32)], axis=1)
    radial_t = jnp.concatenate([radial[m].T for m in range(members)], axis=0)
    r_hi, r_lo = halves(0.5 * radial_t)
    e_hi, e_lo = halves(embed_t)
    none = jnp.zeros_like(r_hi)
    geo[...] = jnp.concatenate(
        [
            jnp.concatenate([r_hi, r_hi, r_lo, none, none, none], axis=1),
            jnp.concatenate([none, none, none, e_hi, e_lo, none], axis=1),
        ],
        axis=0,
    ).astype(bf16)
    mix0 = block_diag([w_mix[m, 0] for m in range(members)])
    mix1 = block_diag([w_mix[m, 1] for m in range(members)])
    latent = block_diag([w_latent[m, 0] for m in range(members)])
    update0 = block_diag([w_update[m, 0] for m in range(members)])
    update1 = block_diag([w_update[m, 1] for m in range(members)])
    radial_back[...] = split_left(0.5 * block_diag([radial[m] for m in range(members)]))
    read_row = jnp.concatenate([readout[m : m + 1, :] for m in range(members)], axis=1)
    eye = (iota((width, width), 0) == iota((width, width), 1)).astype(f32)
    read = jnp.sum(eye * read_row, axis=1, keepdims=True)
    pull = jnp.sum(update1.T * read, axis=0, keepdims=True) * (energy_scale / NEIGH)
    columns[...] = jnp.broadcast_to(read * energy_scale, (width, LANES))
    factors = (
        0.5 * mix0.T, latent.T, 0.5 * mix1.T, 0.5 * mix1 * pull, latent, 0.5 * mix0,
        update0.T * (1.0 / NEIGH), update0 * (1.0 / NEIGH),
    )
    for at, matrix in enumerate(factors):
        dense[at] = split_left(matrix)


def lane_pick(table, lanes):
    return jnp.take_along_axis(table, jnp.broadcast_to(lanes, table.shape), axis=1, mode="promise_in_bounds")


def product(left, x):
    hi, lo = parts(x)
    return jnp.dot(left, jnp.concatenate([hi, lo, hi], axis=0), preferred_element_type=f32)


def sum_to(values, hot):
    hi, lo = parts(values)
    both = lax.dot_general(
        jnp.concatenate([hi, lo], axis=0), hot, (((1,), (1,)), ((), ())), preferred_element_type=f32
    )
    return both[: values.shape[0]] + both[values.shape[0] :]


def silu(h):
    return h + h * jnp.tanh(h)


def silu_and_slope(h):
    t = jnp.tanh(h)
    p = 1.0 + t
    return h * p, p + p * (h - h * t)


def sin_cos(x):
    turns = jnp.floor(x * 0.15915494309189535 + 0.5)
    r = (x - turns * 6.28125) - turns * 1.9353071795864769e-3
    h = 0.5 * r
    q = h * h
    s = h * (1.0 + q * (-1 / 6 + q * (1 / 120 + q * (-1 / 5040 + q * (1 / 362880 + q * (-1 / 39916800 + q * (1 / 6227020800)))))))
    c = 1.0 + q * (-1 / 2 + q * (1 / 24 + q * (-1 / 720 + q * (1 / 40320 + q * (-1 / 3628800 + q * (1 / 479001600 - q * (1 / 87178291200)))))))
    return 2.0 * s * c, 1.0 - 2.0 * s * s


def force_kernel(wx, wy, place, n_in, *refs):
    arrived = refs[:n_in]
    model_in, out = refs[n_in : n_in + 6], refs[n_in + 6]
    (raw, posb, lid_s, cl_s, spc, spn, unit, basis_s, slope_s, feats2, sums, grads, pulls,
     joined_s, lat_s, dpre_s, dz_s, back_s, total, tile_list, near_list,
     hold_a, hold_b, hold_hot, geo, dense, radial_back, columns, *model, sems) = refs[n_in + 7 :]
    tiles = 8
    n_dom = wx * wy
    nv = (wy + 1) // 2
    n_src = 3 * nv
    n_blk = wx * nv
    width = feats2.shape[1] // 2
    members = out.shape[0]
    own_a, own_b, slots = place()

    copies = [
        pltpu.make_async_copy(arrived[ref].at[pl.ds(at * PACK_ROWS, PACK_ROWS), :], raw.at[slot], sems.at[k])
        for k, (ref, at, slot) in enumerate(slots)
    ]
    later = [pltpu.make_async_copy(src, dst, sems.at[n_dom + k]) for k, (src, dst) in enumerate(zip(model_in, model))]
    for copy in copies + later:
        copy.start()
    for copy in copies:
        copy.wait()

    none = n_dom * tiles
    pairs = CHUNK // 2
    count = jnp.int32(0)
    near = jnp.int32(0)
    for t in range(pairs):
        tile_list[t] = none // 2
        near_list[t] = none // 2
    for d in range(n_dom):
        a, b = d // wy, d % wy
        live = jnp.max(raw[d, 2 * tiles + 5 : 2 * tiles + 6, :]).astype(i32)
        live = lax.shift_right_logical(live + 1, 1)
        da = lax.rem(a - own_a + 1 + wx, wx)
        db = lax.rem(b - own_b + 1 + wy, wy)
        touches = jnp.logical_and(da < 3, db < 3)
        for t in range(tiles // 2):
            tile_list[pairs + count + t] = d * (tiles // 2) + t
            near_list[pairs + near + t] = d * (tiles // 2) + t
        count = count + live
        near = near + jnp.where(touches, live, 0)
    for t in range(2 * pairs):
        tile_list[pairs + count + t] = none // 2
        near_list[pairs + near + t] = none // 2
    chunks = lax.div(count + (pairs - 1), pairs)
    near_chunks = lax.div(near + (pairs - 1), pairs)

    def tiles_of(ids, chunk):
        firsts = [ids[chunk * pairs + j] * 2 for j in range(pairs)]
        return [first + k for first in firsts for k in range(2)]

    def wide(p):
        return slice(p * 2 * LANES, (p + 1) * 2 * LANES)

    def cut(j):
        return slice(j * LANES, (j + 1) * LANES)

    lane = iota((8, LANES), 1)
    for a in range(wx):
        for v in range(nv):
            low = raw[a * wy + 2 * v, 2 * tiles : 2 * tiles + 8, :]
            high = raw[a * wy + min(2 * v + 1, wy - 1), 2 * tiles : 2 * tiles + 8, :]
            posb[a * nv + v] = jnp.where(lane < 64, low, high)

    lid_s[none : none + 8, :] = jnp.full((8, LANES), -1, i32)
    cl_s[none : none + 8, :] = jnp.full((8, LANES), -1, i32)
    for ref in (spc, spn):
        ref[none : none + 8, :] = jnp.zeros((8, LANES), i32)
    unit[:, none : none + 8, :] = jnp.zeros((3, 8, LANES), f32)
    basis_s[none * 8 : none * 8 + 16, :] = jnp.zeros((16, LANES), f32)
    slope_s[none * 8 : none * 8 + 16, :] = jnp.zeros((16, LANES), f32)

    row = lane[0:1]
    for d in range(n_dom):
        a, b = d // wy, d % wy

        def ids(u, v, start):
            src = ((a + u - 1) % wx) * wy + (b + v - 1) % wy
            base = u * nv * LANES + ((b + v - 1) % wy) * 64 + 8192 * v
            skin = raw[src, 2 * tiles + 4 : 2 * tiles + 5, :].astype(i32) + base
            return pltpu.roll(skin, start, 1) if start else skin

        first = row + (nv * LANES + b * 64 + 8192)
        first = jnp.where(row >= 64, ids(0, 1, 64), first)
        first = jnp.where(row >= 96, ids(1, 0, 96), first)
        second = ids(1, 2, 0)
        second = jnp.where(row >= 32, ids(2, 1, 32), second)
        for k, (u, v) in enumerate(((0, 0), (0, 2), (2, 0), (2, 2))):
            second = jnp.where(row >= 64 + 8 * k, ids(u, v, 64 + 8 * k), second)
        center = raw[d, 0:tiles, :].astype(i32)
        entry = raw[d, tiles : 2 * tiles, :].astype(i32)
        shape = (8, LANES)
        code = jnp.where(
            entry < LANES,
            lane_pick(jnp.broadcast_to(first, shape), entry & 127),
            lane_pick(jnp.broadcast_to(second, shape), entry & 127),
        )
        side_y = lax.shift_right_logical(code, 13)
        lid = code & 8191
        side_x = (lid >= nv * LANES).astype(f32) + (lid >= 2 * nv * LANES).astype(f32) - 1.0
        clid = center + b * 64
        block = lax.shift_right_logical(lid, 7)
        got_n, got_c = [], []
        for q in range(4):
            value = None
            for s in range(n_src):
                src = ((a + s // nv - 1) % wx) * nv + s % nv
                picked = lane_pick(jnp.broadcast_to(posb[src, q : q + 1, :], shape), lid & 127)
                value = picked if value is None else jnp.where(block == s, picked, value)
            got_n.append(value)
            got_c.append(lane_pick(jnp.broadcast_to(posb[a * nv + b // 2, q : q + 1, :], shape), clid & 127))
        dx = got_n[0] + box_edge * side_x - got_c[0]
        dy = got_n[1] + box_edge * (side_y.astype(f32) - 1.0) - got_c[1]
        dz = got_n[2] - got_c[2]
        distance = jnp.sqrt(dx * dx + dy * dy + dz * dz + 1.0)
        inverse = 1.0 / distance
        rows = slice(d * tiles, (d + 1) * tiles)
        for q, part in enumerate((dx, dy, dz)):
            unit[q, rows, :] = part * inverse
        spn[rows, :] = got_n[3].astype(i32)
        spc[rows, :] = got_c[3].astype(i32)
        live = iota(shape, 0).astype(f32) < raw[d, 2 * tiles + 5 : 2 * tiles + 6, :]
        lid_s[rows, :] = jnp.where(live, lid, -1)
        cl_s[rows, :] = jnp.where(live, clid, -1)
        s1, c1 = sin_cos(distance * 0.25)
        env = jnp.exp(distance * (-1.0 / 32.0))
        c_k, s_k = [jnp.ones_like(c1), c1], [jnp.zeros_like(s1), s1]
        for k in range(2, 8):
            c_k.append(2.0 * c1 * c_k[-1] - c_k[-2])
            s_k.append(2.0 * c1 * s_k[-1] - s_k[-2])
        for k in range(8):
            basis = c_k[k] * env
            basis_s[pl.ds(d * 64 + k, 8, stride=8), :] = basis
            slope_s[pl.ds(d * 64 + k, 8, stride=8), :] = s_k[k] * env * (-k / 4.0) - basis * (1.0 / 32.0)

    for ref in (sums, grads):
        ref[...] = jnp.zeros(ref.shape, f32)
    for ref in (joined_s, lat_s, dpre_s, dz_s, back_s):
        ref[none : none + 2] = jnp.zeros((2, width, LANES), f32)
    total[...] = jnp.zeros(total.shape, f32)

    def spots(tau):
        d = lax.shift_right_logical(tau, 3)
        a, b = lax.div(d, wy), lax.rem(d, wy)
        sources = [lax.rem(a + (s // nv - 1 + wx), wx) * nv + s % nv for s in range(n_src)]
        home = lax.rem(a, wx) * nv + lax.div(b, 2)
        return sources, home, lax.div(b, 2)

    def ones_and_zeros(lanes):
        return iota((LANES, lanes), 0).astype(bf16), jnp.ones((LANES, lanes), bf16), jnp.zeros((LANES, lanes), bf16)

    def ids_of(ref, taus):
        return jnp.concatenate([ref[pl.ds(tau, 1), :] for tau in taus], axis=1)

    def hot(ids_row):
        atom, one, zero = ones_and_zeros(ids_row.shape[1])
        return jnp.where(atom == ids_row.astype(f32).astype(bf16), one, zero)

    def side(parts):
        return jnp.concatenate(parts, axis=1)

    def forward(chunk, carry):
        old = tiles_of(tile_list, chunk)
        new = tiles_of(tile_list, chunk + 1)
        old_latent = side([lat_s[tau] for tau in old])
        mixed = old_latent * side([joined_s[tau] for tau in old])
        sub = iota((8, LANES), 0)
        rhs = []
        for tau in new:
            hi, lo = halves(basis_s[pl.ds(pl.multiple_of(tau * 8, 8), 8), :])
            kinds = (sub == spc[pl.ds(tau, 1), :]).astype(f32) + (sub == spn[pl.ds(tau, 1), :]).astype(f32)
            rhs.append(jnp.concatenate([hi, lo, hi, kinds, kinds, jnp.zeros_like(hi)], axis=0).astype(bf16))
        homes, hots = [], []
        for p in range(pairs):
            _, home, half = spots(old[2 * p])
            homes.append(home)
            hots.append(hot(ids_of(cl_s, old[2 * p : 2 * p + 2]) - half * LANES))
        z = product(dense[0], mixed)
        both = jnp.dot(geo[...], side(rhs), preferred_element_type=f32)
        active, slope = silu_and_slope(z)
        latent, latent_slope = silu_and_slope(both[:width])
        added = [sum_to(active[:, wide(p)], hots[p]) for p in range(pairs)]
        old_latent = old_latent + product(dense[1], active)
        for j, tau in enumerate(new):
            joined_s[tau] = both[width:, cut(j)]
            dpre_s[tau] = latent_slope[:, cut(j)]
            lat_s[tau] = latent[:, cut(j)]
        for j, tau in enumerate(old):
            dz_s[tau] = slope[:, cut(j)]
            lat_s[tau] = old_latent[:, cut(j)]
        for p in range(pairs):
            sums[homes[p]] += added[p]
        return carry

    for copy in later:
        copy.wait()
    weight_factors(*model, geo, dense, radial_back, columns)
    lax.fori_loop(0, chunks + 1, forward, 0)

    sub = iota((8, LANES), 0)
    for k in range(n_blk):
        kinds = (sub == posb[k, 3:4, :].astype(i32)).astype(f32)
        empty = jnp.zeros_like(kinds)
        rhs = jnp.concatenate([empty, empty, empty, kinds, kinds, empty], axis=0).astype(bf16)
        start = jnp.dot(geo[...], rhs, preferred_element_type=f32)[width:]
        feats2[k] = jnp.concatenate(parts(start + product(dense[6], sums[k])), axis=0)

    def middle(chunk, carry):
        old = tiles_of(tile_list, chunk)
        new = tiles_of(tile_list, chunk + 1)
        old_joined, old_slope = hold_a[...], hold_b[...]
        old_hots = [hold_hot[p] for p in range(pairs)]
        old_latent = side([lat_s[tau] for tau in old])
        old_sources = [spots(old[2 * p])[0] for p in range(pairs)]
        latent = side([lat_s[tau] for tau in new])
        joined, hots = [], []
        for p in range(pairs):
            sources, _, half = spots(new[2 * p])
            lid = ids_of(lid_s, new[2 * p : 2 * p + 2])
            own = hot(ids_of(cl_s, new[2 * p : 2 * p + 2]) - half * LANES)
            rows = [hot(lid - s * LANES) for s in range(n_src)]
            for v in range(nv):
                rows[nv + v] = rows[nv + v] + (own if nv == 1 else jnp.where(half == v, own, jnp.zeros_like(own)))
            hots.append(jnp.concatenate(rows, axis=0))
            both = jnp.dot(side([feats2[s] for s in sources]), hots[-1], preferred_element_type=f32)
            joined.append(both[:width] + both[width:])
        dmix = product(dense[3], old_slope)
        joined = side(joined)
        z = product(dense[2], latent * joined)
        spread = dmix * old_latent
        added = [sum_to(spread[:, wide(p)], old_hots[p]) for p in range(pairs)]
        back = dmix * old_joined
        _, slope = silu_and_slope(z)
        hold_a[...] = joined
        hold_b[...] = slope
        for p in range(pairs):
            hold_hot[p] = hots[p]
        for j, tau in enumerate(old):
            back_s[tau] = back[:, cut(j)]
        for p in range(pairs):
            for s in range(n_src):
                grads[old_sources[p][s]] += added[p][:, cut(s)]
        return carry

    hold_b[...] = jnp.zeros(hold_b.shape, f32)
    hold_a[...] = jnp.zeros(hold_a.shape, f32)
    hold_hot[...] = jnp.zeros(hold_hot.shape, bf16)
    lax.fori_loop(0, chunks + 1, middle, 0)

    for k in range(n_blk):
        pulls[k] = product(dense[7], grads[k] + columns[...])

    own_block = own_a * nv + lax.div(own_b, 2)

    def backward(chunk, carry):
        old = tiles_of(near_list, chunk)
        new = tiles_of(near_list, chunk + 1)
        old_pre = hold_a[...]
        slopes = [slope_s[pl.ds(pl.multiple_of(tau * 8, 8), 8), :] for tau in old]
        units = [[unit[q, pl.ds(tau, 1), :] for q in range(3)] for tau in old]
        back = side([back_s[tau] for tau in new])
        dz = side([dz_s[tau] for tau in new])
        joined = side([joined_s[tau] for tau in new])
        dpre = side([dpre_s[tau] for tau in new])
        pulled = []
        for tau in new:
            _, home, _ = spots(tau)
            pulled.append(lane_pick(pulls[home], cl_s[pl.ds(tau, 1), :] & 127))
        hits, chits = [], []
        for p in range(pairs):
            sources, home, half = spots(old[2 * p])
            lid = ids_of(lid_s, old[2 * p : 2 * p + 2])
            hit = jnp.full(lid.shape, -1, i32)
            for s in range(n_src):
                this = jnp.where(sources[s] == own_block, s, -2)
                hit = jnp.where(lax.shift_right_arithmetic(lid, 7) == this, lid & 127, hit)
            hits.append(hit)
            chits.append(jnp.where(home == own_block, ids_of(cl_s, old[2 * p : 2 * p + 2]) - half * LANES, -1))
        many = hot(side(hits)) - hot(side(chits))
        dbasis = product(radial_back[...], old_pre)
        active = side(pulled) + product(dense[4], back)
        moves = []
        for j in range(CHUNK):
            rows = []
            for m in range(members):
                along = jnp.sum(dbasis[m * 8 : (m + 1) * 8, cut(j)] * slopes[j], axis=0, keepdims=True)
                rows += [along * units[j][q] for q in range(3)]
            rows.append(jnp.zeros((8 - 3 * members, LANES), f32))
            moves.append(jnp.concatenate(rows, axis=0))
        added = sum_to(side(moves), many)
        dmix = product(dense[5], active * dz)
        hold_a[...] = (back + dmix * joined) * dpre
        total[...] += added
        return carry

    hold_a[...] = jnp.zeros(hold_a.shape, f32)
    lax.fori_loop(0, near_chunks + 1, backward, 0)

    result = -total[...]
    result = jnp.where(lax.rem(own_b, 2) == 1, pltpu.roll(result, 64, 1), result)
    for m in range(members):
        for q in range(3):
            out[m, q, 0] = result[m * 3 + q : m * 3 + q + 1, 0:64]


def window(size):
    return min(size, 2 * REACH + 1)


def shift(value, axis, by):
    peers = lax.axis_size(axis)
    return lax.ppermute(value, axis, [(i, (i + by) % peers) for i in range(peers)])


def swap(value, by_core):
    sizes = [lax.axis_size(axis) for axis in ("gx", "gy", "gz")]
    pairs = []
    for a in range(sizes[0]):
        for b in range(sizes[1]):
            for c in range(sizes[2]):
                dx, dy, dz = by_core[c]
                pairs.append(((a * sizes[1] + b) * sizes[2] + c, ((a ^ dx) * sizes[1] + (b ^ dy)) * sizes[2] + (c ^ dz)))
    return lax.ppermute(value, ("gx", "gy", "gz"), pairs)


def gathered(own, gx, gy):
    if gx == 4 and gy == 2 and lax.axis_size("gz") == 2:
        fetch = (((0, 1), (2, 1)), ((1, 0), (3, 0)), ((1, 1), (3, 1)))
        far = swap(own, ((2, 0, 0), (2, 0, 0)))
        fetched = [swap(own, (low + (0,), high + (0,))) for low, high in fetch]
        handed = [swap(value, ((0, 0, 1), (0, 0, 1))) for value in fetched]

        def place():
            a, b, c = lax.axis_index("gx"), lax.axis_index("gy"), lax.axis_index("gz")
            slots = [(0, 0, a * 2 + b), (1, 0, (a ^ 2) * 2 + b)]
            for k, (low, high) in enumerate(fetch):
                mine = [jnp.where(c == 0, low[q], high[q]) for q in range(2)]
                other = [jnp.where(c == 0, high[q], low[q]) for q in range(2)]
                slots.append((2 + k, 0, (a ^ mine[0]) * 2 + (b ^ mine[1])))
                slots.append((5 + k, 0, (a ^ other[0]) * 2 + (b ^ other[1])))
            return a, b, slots

        return [own, far] + fetched + handed, place
    wx, wy = window(gx), window(gy)
    steps = list(range(wy // 2 + 1)) + list(range(wy // 2 + 1 - wy, 0))
    column = jnp.concatenate([own if s == 0 else shift(own, "gy", -s) for s in steps], axis=0)
    steps_x = list(range(wx // 2 + 1)) + list(range(wx // 2 + 1 - wx, 0))
    arrays = [column if s == 0 else shift(column, "gx", -s) for s in steps_x]

    def place():
        slots = [(k, at, k * wy + at) for k in range(wx) for at in range(wy)]
        return jnp.int32(0), jnp.int32(0), slots

    return arrays, place


def on_device(
    positions, species, centers, neighbours, masks, skin, embed, radial, w_mix, w_latent, w_update, readout
):
    gx, gy = lax.axis_size("gx"), lax.axis_size("gy")
    atoms = positions.shape[-1]
    members, _, channels = embed.shape
    width = members * channels
    own = pl.pallas_call(
        pack_kernel, out_shape=jax.ShapeDtypeStruct((PACK_ROWS, LANES), f32), name="pack"
    )(positions, species, centers, neighbours, masks, skin)
    model = (jnp.transpose(embed, (1, 0, 2)), radial, w_mix, w_latent, w_update, readout)
    arrays, place = gathered(own, gx, gy)
    wx, wy = window(gx), window(gy)
    n_dom = wx * wy
    n_tiles = n_dom * 8
    n_blk = wx * ((wy + 1) // 2)
    per_tile = pltpu.VMEM((n_tiles + 2, width, LANES), f32)
    per_block = pltpu.VMEM((n_blk, width, LANES), f32)
    row_ids = pltpu.VMEM((n_tiles + 8, LANES), i32)

    def body(*refs):
        force_kernel(wx, wy, place, len(arrays), *refs)

    return pl.pallas_call(
        body,
        out_shape=jax.ShapeDtypeStruct((members, 3, 1, 1, atoms), f32),
        scratch_shapes=[
            pltpu.VMEM((n_dom, PACK_ROWS, LANES), f32),
            pltpu.VMEM((n_blk, 8, LANES), f32),
            row_ids,
            row_ids,
            row_ids,
            row_ids,
            pltpu.VMEM((3, n_tiles + 8, LANES), f32),
            pltpu.VMEM((n_tiles * 8 + 16, LANES), f32),
            pltpu.VMEM((n_tiles * 8 + 16, LANES), f32),
            pltpu.VMEM((n_blk, 2 * width, LANES), bf16),
            per_block,
            per_block,
            per_block,
            per_tile,
            per_tile,
            per_tile,
            per_tile,
            per_tile,
            pltpu.VMEM((8, LANES), f32),
            pltpu.SMEM((n_tiles + 3 * CHUNK,), i32),
            pltpu.SMEM((n_tiles + 3 * CHUNK,), i32),
            pltpu.VMEM((width, CHUNK * LANES), f32),
            pltpu.VMEM((width, CHUNK * LANES), f32),
            pltpu.VMEM((CHUNK // 2, 3 * n_blk // wx * LANES, 2 * LANES), bf16),
        ]
        + [
            pltpu.VMEM((2 * width, 48), bf16),
            pltpu.VMEM((8, width, 3 * width), bf16),
            pltpu.VMEM((members * 8, 3 * width), bf16),
            pltpu.VMEM((width, LANES), f32),
        ]
        + [pltpu.VMEM(part.shape, part.dtype) for part in model]
        + [pltpu.SemaphoreType.DMA((n_dom + len(model),))],
        in_specs=[pl.BlockSpec(memory_space=pl.ANY)] * len(arrays) + [pl.BlockSpec(memory_space=pltpu.HBM)] * len(model),
        compiler_params=pltpu.CompilerParams(vmem_limit_bytes=60 * 1024 * 1024),
        name="forces",
    )(*arrays, *model)


def solution(mesh):
    return jax.shard_map(
        on_device,
        mesh=mesh,
        in_specs=(
            P(None, ("groups", "gx"), "gy", None),
            P(("groups", "gx"), "gy", None),
            P(("groups", "gx"), "gy", None),
            P(("groups", "gx"), "gy", None),
            P(("groups", "gx"), "gy", None),
            P(("groups", "gx"), "gy", None),
            P("gz", None, None),
            P("gz", None, None),
            P("gz", None, None, None),
            P("gz", None, None, None),
            P("gz", None, None, None),
            P("gz", None),
        ),
        out_specs=P("gz", None, ("groups", "gx"), "gy", None),
        check_vma=False,
    )
```

```python
import jax
import jax.numpy as jnp
from jax import lax
from jax.experimental import pallas as pl
from jax.experimental.pallas import tpu as pltpu
from jax.sharding import PartitionSpec as P

NEIGH = 16
box_edge = 20.0
energy_scale = 16.0
REACH = 3
LANES = 128
CHUNK = 12
PACK_ROWS = 24
f32 = jnp.float32
bf16 = jnp.bfloat16
i32 = jnp.int32


def iota(shape, dim):
    return lax.broadcasted_iota(i32, shape, dim)


def halves(x):
    hi = x.astype(bf16).astype(f32)
    return hi, x - hi


def pack_kernel(pos, species, centers, neighbours, masks, skin, out):
    tiles = centers.shape[-1] // LANES
    atoms = pos.shape[-1]
    ghosts = skin.shape[-1]
    out[...] = jnp.zeros(out.shape, f32)
    live = jnp.zeros((1, LANES), f32)
    for t in range(tiles):
        cut = slice(t * LANES, (t + 1) * LANES)
        out[t : t + 1, :] = centers[0, :, cut].astype(f32)
        out[tiles + t : tiles + t + 1, :] = neighbours[0, :, cut].astype(f32)
        live = live + masks[0, :, cut].astype(f32)
    base = 2 * tiles
    for q in range(3):
        row = pos[q, 0]
        out[base + q : base + q + 1, :] = jnp.concatenate([row, row], axis=1)
    row = species[0].astype(f32)
    out[base + 3 : base + 4, :] = jnp.concatenate([row, row], axis=1)
    out[base + 4 : base + 5, 0:ghosts] = skin[0].astype(f32)
    out[base + 5 : base + 6, :] = live


def block_diag(blocks):
    rows = []
    for at, block in enumerate(blocks):
        parts = [block if k == at else jnp.zeros((block.shape[0], other.shape[1]), f32) for k, other in enumerate(blocks)]
        rows.append(jnp.concatenate(parts, axis=1))
    return jnp.concatenate(rows, axis=0)


def split_left(matrix):
    hi, lo = halves(matrix)
    return jnp.concatenate([hi, hi, lo], axis=1).astype(bf16)


def parts(x):
    hi = x.astype(bf16)
    return hi, (x - hi.astype(f32)).astype(bf16)


def weight_factors(embed, radial, w_mix, w_latent, w_update, readout, geo, dense, radial_back, columns):
    elements, members, channels = embed.shape
    width = members * channels
    embed_t = jnp.concatenate([embed[:, m, :].T for m in range(members)], axis=0)
    embed_t = jnp.concatenate([embed_t, jnp.zeros((width, 8 - elements), f32)], axis=1)
    radial_t = jnp.concatenate([radial[m].T for m in range(members)], axis=0)
    r_hi, r_lo = halves(0.5 * radial_t)
    e_hi, e_lo = halves(embed_t)
    none = jnp.zeros_like(r_hi)
    geo[...] = jnp.concatenate(
        [
            jnp.concatenate([r_hi, r_hi, r_lo, none, none, none], axis=1),
            jnp.concatenate([none, none, none, e_hi, e_lo, none], axis=1),
        ],
        axis=0,
    ).astype(bf16)
    mix0 = block_diag([w_mix[m, 0] for m in range(members)])
    mix1 = block_diag([w_mix[m, 1] for m in range(members)])
    latent = block_diag([w_latent[m, 0] for m in range(members)])
    update0 = block_diag([w_update[m, 0] for m in range(members)])
    update1 = block_diag([w_update[m, 1] for m in range(members)])
    radial_back[...] = split_left(0.5 * block_diag([radial[m] for m in range(members)]))
    read_row = jnp.concatenate([readout[m : m + 1, :] for m in range(members)], axis=1)
    eye = (iota((width, width), 0) == iota((width, width), 1)).astype(f32)
    read = jnp.sum(eye * read_row, axis=1, keepdims=True)
    pull = jnp.sum(update1.T * read, axis=0, keepdims=True) * (energy_scale / NEIGH)
    columns[...] = jnp.broadcast_to(read * energy_scale, (width, LANES))
    factors = (
        0.5 * mix0.T, latent.T, 0.5 * mix1.T, 0.5 * mix1 * pull, latent, 0.5 * mix0,
        update0.T * (1.0 / NEIGH), update0 * (1.0 / NEIGH),
    )
    for at, matrix in enumerate(factors):
        dense[at] = split_left(matrix)


def lane_pick(table, lanes):
    return jnp.take_along_axis(table, jnp.broadcast_to(lanes, table.shape), axis=1, mode="promise_in_bounds")


def product(left, x):
    hi, lo = parts(x)
    return jnp.dot(left, jnp.concatenate([hi, lo, hi], axis=0), preferred_element_type=f32)


def sum_to(values, hot):
    hi, lo = parts(values)
    both = lax.dot_general(
        jnp.concatenate([hi, lo], axis=0), hot, (((1,), (1,)), ((), ())), preferred_element_type=f32
    )
    return both[: values.shape[0]] + both[values.shape[0] :]


def silu(h):
    return h + h * jnp.tanh(h)


def silu_and_slope(h):
    t = jnp.tanh(h)
    p = 1.0 + t
    return h * p, p + p * (h - h * t)


def sin_cos(x):
    turns = jnp.floor(x * 0.15915494309189535 + 0.5)
    r = (x - turns * 6.28125) - turns * 1.9353071795864769e-3
    h = 0.5 * r
    q = h * h
    s = h * (1.0 + q * (-1 / 6 + q * (1 / 120 + q * (-1 / 5040 + q * (1 / 362880 + q * (-1 / 39916800 + q * (1 / 6227020800)))))))
    c = 1.0 + q * (-1 / 2 + q * (1 / 24 + q * (-1 / 720 + q * (1 / 40320 + q * (-1 / 3628800 + q * (1 / 479001600 - q * (1 / 87178291200)))))))
    return 2.0 * s * c, 1.0 - 2.0 * s * s


def force_kernel(wx, wy, place, n_in, *refs):
    arrived = refs[:n_in]
    model_in, out = refs[n_in : n_in + 6], refs[n_in + 6]
    (raw, posb, lid_s, cl_s, spc, spn, unit, basis_s, slope_s, feats2, sums, grads, pulls,
     joined_s, lat_s, dpre_s, dz_s, back_s, total, tile_list, near_list,
     hold_a, hold_b, hold_hot, geo, dense, radial_back, columns, *model, sems) = refs[n_in + 7 :]
    tiles = 8
    n_dom = wx * wy
    nv = (wy + 1) // 2
    n_src = 3 * nv
    n_blk = wx * nv
    width = feats2.shape[1] // 2
    members = out.shape[0]
    own_a, own_b, slots = place()

    copies = [
        pltpu.make_async_copy(arrived[ref].at[pl.ds(at * PACK_ROWS, PACK_ROWS), :], raw.at[slot], sems.at[k])
        for k, (ref, at, slot) in enumerate(slots)
    ]
    later = [pltpu.make_async_copy(src, dst, sems.at[n_dom + k]) for k, (src, dst) in enumerate(zip(model_in, model))]
    for copy in copies + later:
        copy.start()
    for copy in copies:
        copy.wait()

    none = n_dom * tiles
    pairs = CHUNK // 2
    count = jnp.int32(0)
    near = jnp.int32(0)
    for d in range(n_dom):
        a, b = d // wy, d % wy
        live = jnp.max(raw[d, 2 * tiles + 5 : 2 * tiles + 6, :]).astype(i32)
        live = lax.shift_right_logical(live + 1, 1)
        da = lax.rem(a - own_a + 1 + wx, wx)
        db = lax.rem(b - own_b + 1 + wy, wy)
        touches = jnp.logical_and(da < 3, db < 3)
        for t in range(tiles // 2):
            tile_list[count + t] = d * (tiles // 2) + t
            near_list[near + t] = d * (tiles // 2) + t
        count = count + live
        near = near + jnp.where(touches, live, 0)
    for t in range(pairs):
        tile_list[count + t] = none // 2
        near_list[near + t] = none // 2
    chunks = lax.div(count + (pairs - 1), pairs)
    near_chunks = lax.div(near + (pairs - 1), pairs)

    def tiles_of(ids, chunk):
        firsts = [ids[chunk * pairs + j] * 2 for j in range(pairs)]
        return [first + k for first in firsts for k in range(2)]

    def wide(p):
        return slice(p * 2 * LANES, (p + 1) * 2 * LANES)

    def cut(j):
        return slice(j * LANES, (j + 1) * LANES)

    lane = iota((8, LANES), 1)
    for a in range(wx):
        for v in range(nv):
            low = raw[a * wy + 2 * v, 2 * tiles : 2 * tiles + 8, :]
            high = raw[a * wy + min(2 * v + 1, wy - 1), 2 * tiles : 2 * tiles + 8, :]
            posb[a * nv + v] = jnp.where(lane < 64, low, high)

    lid_s[none : none + 8, :] = jnp.full((8, LANES), -1, i32)
    cl_s[none : none + 8, :] = jnp.full((8, LANES), -1, i32)
    for ref in (spc, spn):
        ref[none : none + 8, :] = jnp.zeros((8, LANES), i32)
    unit[:, none : none + 8, :] = jnp.zeros((3, 8, LANES), f32)
    basis_s[none * 8 : none * 8 + 16, :] = jnp.zeros((16, LANES), f32)
    slope_s[none * 8 : none * 8 + 16, :] = jnp.zeros((16, LANES), f32)

    row = lane[0:1]
    for d in range(n_dom):
        a, b = d // wy, d % wy

        def ids(u, v, start):
            src = ((a + u - 1) % wx) * wy + (b + v - 1) % wy
            base = u * nv * LANES + ((b + v - 1) % wy) * 64 + 8192 * v
            skin = raw[src, 2 * tiles + 4 : 2 * tiles + 5, :].astype(i32) + base
            return pltpu.roll(skin, start, 1) if start else skin

        first = row + (nv * LANES + b * 64 + 8192)
        first = jnp.where(row >= 64, ids(0, 1, 64), first)
        first = jnp.where(row >= 96, ids(1, 0, 96), first)
        second = ids(1, 2, 0)
        second = jnp.where(row >= 32, ids(2, 1, 32), second)
        for k, (u, v) in enumerate(((0, 0), (0, 2), (2, 0), (2, 2))):
            second = jnp.where(row >= 64 + 8 * k, ids(u, v, 64 + 8 * k), second)
        center = raw[d, 0:tiles, :].astype(i32)
        entry = raw[d, tiles : 2 * tiles, :].astype(i32)
        shape = (8, LANES)
        code = jnp.where(
            entry < LANES,
            lane_pick(jnp.broadcast_to(first, shape), entry & 127),
            lane_pick(jnp.broadcast_to(second, shape), entry & 127),
        )
        side_y = lax.shift_right_logical(code, 13)
        lid = code & 8191
        side_x = (lid >= nv * LANES).astype(f32) + (lid >= 2 * nv * LANES).astype(f32) - 1.0
        clid = center + b * 64
        block = lax.shift_right_logical(lid, 7)
        got_n, got_c = [], []
        for q in range(4):
            value = None
            for s in range(n_src):
                src = ((a + s // nv - 1) % wx) * nv + s % nv
                picked = lane_pick(jnp.broadcast_to(posb[src, q : q + 1, :], shape), lid & 127)
                value = picked if value is None else jnp.where(block == s, picked, value)
            got_n.append(value)
            got_c.append(lane_pick(jnp.broadcast_to(posb[a * nv + b // 2, q : q + 1, :], shape), clid & 127))
        dx = got_n[0] + box_edge * side_x - got_c[0]
        dy = got_n[1] + box_edge * (side_y.astype(f32) - 1.0) - got_c[1]
        dz = got_n[2] - got_c[2]
        distance = jnp.sqrt(dx * dx + dy * dy + dz * dz + 1.0)
        inverse = 1.0 / distance
        rows = slice(d * tiles, (d + 1) * tiles)
        for q, part in enumerate((dx, dy, dz)):
            unit[q, rows, :] = part * inverse
        spn[rows, :] = got_n[3].astype(i32)
        spc[rows, :] = got_c[3].astype(i32)
        live = iota(shape, 0).astype(f32) < raw[d, 2 * tiles + 5 : 2 * tiles + 6, :]
        lid_s[rows, :] = jnp.where(live, lid, -1)
        cl_s[rows, :] = jnp.where(live, clid, -1)
        s1, c1 = sin_cos(distance * 0.25)
        env = jnp.exp(distance * (-1.0 / 32.0))
        c_k, s_k = [jnp.ones_like(c1), c1], [jnp.zeros_like(s1), s1]
        for k in range(2, 8):
            c_k.append(2.0 * c1 * c_k[-1] - c_k[-2])
            s_k.append(2.0 * c1 * s_k[-1] - s_k[-2])
        for k in range(8):
            basis = c_k[k] * env
            basis_s[pl.ds(d * 64 + k, 8, stride=8), :] = basis
            slope_s[pl.ds(d * 64 + k, 8, stride=8), :] = s_k[k] * env * (-k / 4.0) - basis * (1.0 / 32.0)

    for ref in (sums, grads):
        ref[...] = jnp.zeros(ref.shape, f32)
    for ref in (joined_s, lat_s, dpre_s, dz_s, back_s):
        ref[none : none + 2] = jnp.zeros((2, width, LANES), f32)
    total[...] = jnp.zeros(total.shape, f32)

    def spots(tau):
        d = lax.shift_right_logical(tau, 3)
        a, b = lax.div(d, wy), lax.rem(d, wy)
        sources = [lax.rem(a + (s // nv - 1 + wx), wx) * nv + s % nv for s in range(n_src)]
        home = lax.rem(a, wx) * nv + lax.div(b, 2)
        return sources, home, lax.div(b, 2)

    def ones_and_zeros(lanes):
        return iota((LANES, lanes), 0).astype(bf16), jnp.ones((LANES, lanes), bf16), jnp.zeros((LANES, lanes), bf16)

    def ids_of(ref, taus):
        return jnp.concatenate([ref[pl.ds(tau, 1), :] for tau in taus], axis=1)

    def hot(ids_row):
        atom, one, zero = ones_and_zeros(ids_row.shape[1])
        return jnp.where(atom == ids_row.astype(f32).astype(bf16), one, zero)

    def side(parts):
        return jnp.concatenate(parts, axis=1)

    def pipelined(step, ids, chunks):
        step(tiles_of(ids, 0), None)

        def both(chunk, carry):
            step(tiles_of(ids, chunk), tiles_of(ids, chunk - 1))
            return carry

        lax.fori_loop(1, chunks, both, 0)
        step(None, tiles_of(ids, chunks - 1))

    def forward(new, old):
        if old:
            old_latent = side([lat_s[tau] for tau in old])
            mixed = old_latent * side([joined_s[tau] for tau in old])
        if new:
            sub = iota((8, LANES), 0)
            rhs = []
            for tau in new:
                hi, lo = halves(basis_s[pl.ds(pl.multiple_of(tau * 8, 8), 8), :])
                kinds = (sub == spc[pl.ds(tau, 1), :]).astype(f32) + (sub == spn[pl.ds(tau, 1), :]).astype(f32)
                rhs.append(jnp.concatenate([hi, lo, hi, kinds, kinds, jnp.zeros_like(hi)], axis=0).astype(bf16))
        if old:
            homes, hots = [], []
            for p in range(pairs):
                _, home, half = spots(old[2 * p])
                homes.append(home)
                hots.append(hot(ids_of(cl_s, old[2 * p : 2 * p + 2]) - half * LANES))
            z = product(dense[0], mixed)
        if new:
            both = jnp.dot(geo[...], side(rhs), preferred_element_type=f32)
        if old:
            active, slope = silu_and_slope(z)
        if new:
            latent, latent_slope = silu_and_slope(both[:width])
        if old:
            added = [sum_to(active[:, wide(p)], hots[p]) for p in range(pairs)]
            old_latent = old_latent + product(dense[1], active)
        if new:
            for j, tau in enumerate(new):
                joined_s[tau] = both[width:, cut(j)]
                dpre_s[tau] = latent_slope[:, cut(j)]
                lat_s[tau] = latent[:, cut(j)]
        if old:
            for j, tau in enumerate(old):
                dz_s[tau] = slope[:, cut(j)]
                lat_s[tau] = old_latent[:, cut(j)]
            for p in range(pairs):
                sums[homes[p]] += added[p]

    for copy in later:
        copy.wait()
    weight_factors(*model, geo, dense, radial_back, columns)
    pipelined(forward, tile_list, chunks)

    sub = iota((8, n_blk * LANES), 0)
    kinds = (sub == side([posb[k, 3:4, :] for k in range(n_blk)]).astype(i32)).astype(f32)
    empty = jnp.zeros_like(kinds)
    rhs = jnp.concatenate([empty, empty, empty, kinds, kinds, empty], axis=0).astype(bf16)
    start = jnp.dot(geo[...], rhs, preferred_element_type=f32)[width:]
    features = start + product(dense[6], side([sums[k] for k in range(n_blk)]))
    features = jnp.concatenate(parts(features), axis=0)
    for k in range(n_blk):
        feats2[k] = features[:, cut(k)]

    def middle(new, old):
        if old:
            old_joined, old_slope = hold_a[...], hold_b[...]
            old_hots = [hold_hot[p] for p in range(pairs)]
            old_latent = side([lat_s[tau] for tau in old])
            old_sources = [spots(old[2 * p])[0] for p in range(pairs)]
        if new:
            latent = side([lat_s[tau] for tau in new])
            joined, hots = [], []
            for p in range(pairs):
                sources, _, half = spots(new[2 * p])
                lid = ids_of(lid_s, new[2 * p : 2 * p + 2])
                own = hot(ids_of(cl_s, new[2 * p : 2 * p + 2]) - half * LANES)
                rows = [hot(lid - s * LANES) for s in range(n_src)]
                for v in range(nv):
                    rows[nv + v] = rows[nv + v] + (own if nv == 1 else jnp.where(half == v, own, jnp.zeros_like(own)))
                hots.append(jnp.concatenate(rows, axis=0))
                both = jnp.dot(side([feats2[s] for s in sources]), hots[-1], preferred_element_type=f32)
                joined.append(both[:width] + both[width:])
        if old:
            dmix = product(dense[3], old_slope)
        if new:
            joined = side(joined)
            z = product(dense[2], latent * joined)
        if old:
            spread = dmix * old_latent
            added = [sum_to(spread[:, wide(p)], old_hots[p]) for p in range(pairs)]
            back = dmix * old_joined
        if new:
            _, slope = silu_and_slope(z)
            hold_a[...] = joined
            hold_b[...] = slope
            for p in range(pairs):
                hold_hot[p] = hots[p]
        if old:
            for j, tau in enumerate(old):
                back_s[tau] = back[:, cut(j)]
            for p in range(pairs):
                for s in range(n_src):
                    grads[old_sources[p][s]] += added[p][:, cut(s)]

    pipelined(middle, tile_list, chunks)

    pulled_all = product(dense[7], side([grads[k] + columns[...] for k in range(n_blk)]))
    for k in range(n_blk):
        pulls[k] = pulled_all[:, cut(k)]

    own_block = own_a * nv + lax.div(own_b, 2)

    def backward(new, old):
        if old:
            old_pre = hold_a[...]
            slopes = [slope_s[pl.ds(pl.multiple_of(tau * 8, 8), 8), :] for tau in old]
            units = [[unit[q, pl.ds(tau, 1), :] for q in range(3)] for tau in old]
        if new:
            back = side([back_s[tau] for tau in new])
            dz = side([dz_s[tau] for tau in new])
            joined = side([joined_s[tau] for tau in new])
            dpre = side([dpre_s[tau] for tau in new])
            pulled = []
            for tau in new:
                _, home, _ = spots(tau)
                pulled.append(lane_pick(pulls[home], cl_s[pl.ds(tau, 1), :] & 127))
        if old:
            hits, chits = [], []
            for p in range(pairs):
                sources, home, half = spots(old[2 * p])
                lid = ids_of(lid_s, old[2 * p : 2 * p + 2])
                hit = jnp.full(lid.shape, -1, i32)
                for s in range(n_src):
                    this = jnp.where(sources[s] == own_block, s, -2)
                    hit = jnp.where(lax.shift_right_arithmetic(lid, 7) == this, lid & 127, hit)
                hits.append(hit)
                chits.append(jnp.where(home == own_block, ids_of(cl_s, old[2 * p : 2 * p + 2]) - half * LANES, -1))
            many = hot(side(hits)) - hot(side(chits))
            dbasis = product(radial_back[...], old_pre)
        if new:
            active = side(pulled) + product(dense[4], back)
        if old:
            moves = []
            for j in range(CHUNK):
                rows = []
                for m in range(members):
                    along = jnp.sum(dbasis[m * 8 : (m + 1) * 8, cut(j)] * slopes[j], axis=0, keepdims=True)
                    rows += [along * units[j][q] for q in range(3)]
                rows.append(jnp.zeros((8 - 3 * members, LANES), f32))
                moves.append(jnp.concatenate(rows, axis=0))
            added = sum_to(side(moves), many)
        if new:
            dmix = product(dense[5], active * dz)
            hold_a[...] = (back + dmix * joined) * dpre
        if old:
            total[...] += added

    pipelined(backward, near_list, near_chunks)

    result = -total[...]
    result = jnp.where(lax.rem(own_b, 2) == 1, pltpu.roll(result, 64, 1), result)
    for m in range(members):
        for q in range(3):
            out[m, q, 0] = result[m * 3 + q : m * 3 + q + 1, 0:64]


def window(size):
    return min(size, 2 * REACH + 1)


def shift(value, axis, by):
    peers = lax.axis_size(axis)
    return lax.ppermute(value, axis, [(i, (i + by) % peers) for i in range(peers)])


def swap(value, by_core):
    sizes = [lax.axis_size(axis) for axis in ("gx", "gy", "gz")]
    pairs = []
    for a in range(sizes[0]):
        for b in range(sizes[1]):
            for c in range(sizes[2]):
                dx, dy, dz = by_core[c]
                pairs.append(((a * sizes[1] + b) * sizes[2] + c, ((a ^ dx) * sizes[1] + (b ^ dy)) * sizes[2] + (c ^ dz)))
    return lax.ppermute(value, ("gx", "gy", "gz"), pairs)


def gathered(own, gx, gy):
    if gx == 4 and gy == 2 and lax.axis_size("gz") == 2:
        fetch = (((0, 1), (2, 1)), ((1, 0), (3, 0)), ((1, 1), (3, 1)))
        far = swap(own, ((2, 0, 0), (2, 0, 0)))
        fetched = [swap(own, (low + (0,), high + (0,))) for low, high in fetch]
        handed = [swap(value, ((0, 0, 1), (0, 0, 1))) for value in fetched]

        def place():
            a, b, c = lax.axis_index("gx"), lax.axis_index("gy"), lax.axis_index("gz")
            slots = [(0, 0, a * 2 + b), (1, 0, (a ^ 2) * 2 + b)]
            for k, (low, high) in enumerate(fetch):
                mine = [jnp.where(c == 0, low[q], high[q]) for q in range(2)]
                other = [jnp.where(c == 0, high[q], low[q]) for q in range(2)]
                slots.append((2 + k, 0, (a ^ mine[0]) * 2 + (b ^ mine[1])))
                slots.append((5 + k, 0, (a ^ other[0]) * 2 + (b ^ other[1])))
            return a, b, slots

        return [own, far] + fetched + handed, place
    wx, wy = window(gx), window(gy)
    steps = list(range(wy // 2 + 1)) + list(range(wy // 2 + 1 - wy, 0))
    column = jnp.concatenate([own if s == 0 else shift(own, "gy", -s) for s in steps], axis=0)
    steps_x = list(range(wx // 2 + 1)) + list(range(wx // 2 + 1 - wx, 0))
    arrays = [column if s == 0 else shift(column, "gx", -s) for s in steps_x]

    def place():
        slots = [(k, at, k * wy + at) for k in range(wx) for at in range(wy)]
        return jnp.int32(0), jnp.int32(0), slots

    return arrays, place


def on_device(
    positions, species, centers, neighbours, masks, skin, embed, radial, w_mix, w_latent, w_update, readout
):
    gx, gy = lax.axis_size("gx"), lax.axis_size("gy")
    atoms = positions.shape[-1]
    members, _, channels = embed.shape
    width = members * channels
    own = pl.pallas_call(
        pack_kernel, out_shape=jax.ShapeDtypeStruct((PACK_ROWS, LANES), f32), name="pack"
    )(positions, species, centers, neighbours, masks, skin)
    model = (jnp.transpose(embed, (1, 0, 2)), radial, w_mix, w_latent, w_update, readout)
    arrays, place = gathered(own, gx, gy)
    wx, wy = window(gx), window(gy)
    n_dom = wx * wy
    n_tiles = n_dom * 8
    n_blk = wx * ((wy + 1) // 2)
    per_tile = pltpu.VMEM((n_tiles + 2, width, LANES), f32)
    per_block = pltpu.VMEM((n_blk, width, LANES), f32)
    row_ids = pltpu.VMEM((n_tiles + 8, LANES), i32)

    def body(*refs):
        force_kernel(wx, wy, place, len(arrays), *refs)

    return pl.pallas_call(
        body,
        out_shape=jax.ShapeDtypeStruct((members, 3, 1, 1, atoms), f32),
        scratch_shapes=[
            pltpu.VMEM((n_dom, PACK_ROWS, LANES), f32),
            pltpu.VMEM((n_blk, 8, LANES), f32),
            row_ids,
            row_ids,
            row_ids,
            row_ids,
            pltpu.VMEM((3, n_tiles + 8, LANES), f32),
            pltpu.VMEM((n_tiles * 8 + 16, LANES), f32),
            pltpu.VMEM((n_tiles * 8 + 16, LANES), f32),
            pltpu.VMEM((n_blk, 2 * width, LANES), bf16),
            per_block,
            per_block,
            per_block,
            per_tile,
            per_tile,
            per_tile,
            per_tile,
            per_tile,
            pltpu.VMEM((8, LANES), f32),
            pltpu.SMEM((n_tiles // 2 + CHUNK // 2 + 4,), i32),
            pltpu.SMEM((n_tiles // 2 + CHUNK // 2 + 4,), i32),
            pltpu.VMEM((width, CHUNK * LANES), f32),
            pltpu.VMEM((width, CHUNK * LANES), f32),
            pltpu.VMEM((CHUNK // 2, 3 * n_blk // wx * LANES, 2 * LANES), bf16),
        ]
        + [
            pltpu.VMEM((2 * width, 48), bf16),
            pltpu.VMEM((8, width, 3 * width), bf16),
            pltpu.VMEM((members * 8, 3 * width), bf16),
            pltpu.VMEM((width, LANES), f32),
        ]
        + [pltpu.VMEM(part.shape, part.dtype) for part in model]
        + [pltpu.SemaphoreType.DMA((n_dom + len(model),))],
        in_specs=[pl.BlockSpec(memory_space=pl.ANY)] * len(arrays) + [pl.BlockSpec(memory_space=pltpu.HBM)] * len(model),
        compiler_params=pltpu.CompilerParams(vmem_limit_bytes=60 * 1024 * 1024),
        name="forces",
    )(*arrays, *model)


def solution(mesh):
    return jax.shard_map(
        on_device,
        mesh=mesh,
        in_specs=(
            P(None, ("groups", "gx"), "gy", None),
            P(("groups", "gx"), "gy", None),
            P(("groups", "gx"), "gy", None),
            P(("groups", "gx"), "gy", None),
            P(("groups", "gx"), "gy", None),
            P(("groups", "gx"), "gy", None),
            P("gz", None, None),
            P("gz", None, None),
            P("gz", None, None, None),
            P("gz", None, None, None),
            P("gz", None, None, None),
            P("gz", None),
        ),
        out_specs=P("gz", None, ("groups", "gx"), "gy", None),
        check_vma=False,
    )
```

```python
import jax
import jax.numpy as jnp
from jax import lax
from jax.experimental import pallas as pl
from jax.experimental.pallas import tpu as pltpu
from jax.sharding import PartitionSpec as P

NEIGH = 16
box_edge = 20.0
energy_scale = 16.0
REACH = 3
LANES = 128
CHUNK = 12
PACK_ROWS = 24
f32 = jnp.float32
bf16 = jnp.bfloat16
i32 = jnp.int32


def iota(shape, dim):
    return lax.broadcasted_iota(i32, shape, dim)


def halves(x):
    hi = x.astype(bf16).astype(f32)
    return hi, x - hi


def pack_kernel(pos, species, centers, neighbours, masks, skin, packed, out, sem):
    tiles = centers.shape[-1] // LANES
    atoms = pos.shape[-1]
    ghosts = skin.shape[-1]
    out[...] = jnp.zeros(out.shape, f32)
    live = jnp.zeros((1, LANES), f32)
    for t in range(tiles):
        cut = slice(t * LANES, (t + 1) * LANES)
        out[t : t + 1, :] = centers[0, :, cut].astype(f32)
        out[tiles + t : tiles + t + 1, :] = neighbours[0, :, cut].astype(f32)
        live = live + masks[0, :, cut].astype(f32)
    base = 2 * tiles
    for q in range(3):
        row = pos[q, 0]
        out[base + q : base + q + 1, :] = jnp.concatenate([row, row], axis=1)
    row = species[0].astype(f32)
    out[base + 3 : base + 4, :] = jnp.concatenate([row, row], axis=1)
    out[base + 4 : base + 5, 0:ghosts] = skin[0].astype(f32)
    out[base + 5 : base + 6, :] = live
    copy = pltpu.make_async_copy(out, packed, sem)
    copy.start()
    copy.wait()


def block_diag(blocks):
    rows = []
    for at, block in enumerate(blocks):
        parts = [block if k == at else jnp.zeros((block.shape[0], other.shape[1]), f32) for k, other in enumerate(blocks)]
        rows.append(jnp.concatenate(parts, axis=1))
    return jnp.concatenate(rows, axis=0)


def split_left(matrix):
    hi, lo = halves(matrix)
    return jnp.concatenate([hi, hi, lo], axis=1).astype(bf16)


def parts(x):
    hi = x.astype(bf16)
    return hi, (x - hi.astype(f32)).astype(bf16)


def weight_factors(embed, radial, w_mix, w_latent, w_update, readout, geo, dense, radial_back, columns):
    elements, members, channels = embed.shape
    width = members * channels
    embed_t = jnp.concatenate([embed[:, m, :].T for m in range(members)], axis=0)
    embed_t = jnp.concatenate([embed_t, jnp.zeros((width, 8 - elements), f32)], axis=1)
    radial_t = jnp.concatenate([radial[m].T for m in range(members)], axis=0)
    r_hi, r_lo = halves(0.5 * radial_t)
    e_hi, e_lo = halves(embed_t)
    none = jnp.zeros_like(r_hi)
    geo[...] = jnp.concatenate(
        [
            jnp.concatenate([r_hi, r_hi, r_lo, none, none, none], axis=1),
            jnp.concatenate([none, none, none, e_hi, e_lo, none], axis=1),
        ],
        axis=0,
    ).astype(bf16)
    mix0 = block_diag([w_mix[m, 0] for m in range(members)])
    mix1 = block_diag([w_mix[m, 1] for m in range(members)])
    latent = block_diag([w_latent[m, 0] for m in range(members)])
    update0 = block_diag([w_update[m, 0] for m in range(members)])
    update1 = block_diag([w_update[m, 1] for m in range(members)])
    radial_back[...] = split_left(0.5 * block_diag([radial[m] for m in range(members)]))
    read_row = jnp.concatenate([readout[m : m + 1, :] for m in range(members)], axis=1)
    eye = (iota((width, width), 0) == iota((width, width), 1)).astype(f32)
    read = jnp.sum(eye * read_row, axis=1, keepdims=True)
    pull = jnp.sum(update1.T * read, axis=0, keepdims=True) * (energy_scale / NEIGH)
    columns[...] = jnp.broadcast_to(read * energy_scale, (width, LANES))
    factors = (
        0.5 * mix0.T, latent.T, 0.5 * mix1.T, 0.5 * mix1 * pull, latent, 0.5 * mix0,
        update0.T * (1.0 / NEIGH), update0 * (1.0 / NEIGH),
    )
    for at, matrix in enumerate(factors):
        dense[at] = split_left(matrix)


def lane_pick(table, lanes):
    return jnp.take_along_axis(table, jnp.broadcast_to(lanes, table.shape), axis=1, mode="promise_in_bounds")


def product(left, x):
    hi, lo = parts(x)
    return jnp.dot(left, jnp.concatenate([hi, lo, hi], axis=0), preferred_element_type=f32)


def sum_to(values, hot):
    hi, lo = parts(values)
    both = lax.dot_general(
        jnp.concatenate([hi, lo], axis=0), hot, (((1,), (1,)), ((), ())), preferred_element_type=f32
    )
    return both[: values.shape[0]] + both[values.shape[0] :]


def silu(h):
    return h + h * jnp.tanh(h)


def silu_and_slope(h):
    t = jnp.tanh(h)
    p = 1.0 + t
    return h * p, p + p * (h - h * t)


def sin_cos(x):
    turns = jnp.floor(x * 0.15915494309189535 + 0.5)
    r = (x - turns * 6.28125) - turns * 1.9353071795864769e-3
    h = 0.5 * r
    q = h * h
    s = h * (1.0 + q * (-1 / 6 + q * (1 / 120 + q * (-1 / 5040 + q * (1 / 362880 + q * (-1 / 39916800 + q * (1 / 6227020800)))))))
    c = 1.0 + q * (-1 / 2 + q * (1 / 24 + q * (-1 / 720 + q * (1 / 40320 + q * (-1 / 3628800 + q * (1 / 479001600 - q * (1 / 87178291200)))))))
    return 2.0 * s * c, 1.0 - 2.0 * s * s


def force_kernel(wx, wy, place, n_in, *refs):
    arrived = refs[:n_in]
    model_in, out = refs[n_in : n_in + 6], refs[n_in + 6]
    (raw, posb, lid_s, cl_s, spc, spn, unit, basis_s, slope_s, feats2, sums, grads, pulls,
     joined_s, lat_s, dpre_s, dz_s, back_s, total, tile_list, near_list,
     hold_a, hold_b, hold_hot, geo, dense, radial_back, columns, *model, sems) = refs[n_in + 7 :]
    tiles = 8
    n_dom = wx * wy
    nv = (wy + 1) // 2
    n_src = 3 * nv
    n_blk = wx * nv
    width = feats2.shape[1] // 2
    members = out.shape[0]
    own_a, own_b, slots = place()

    copies = [
        pltpu.make_async_copy(arrived[ref].at[pl.ds(at * PACK_ROWS, PACK_ROWS), :], raw.at[slot], sems.at[k])
        for k, (ref, at, slot) in enumerate(slots)
    ]
    later = [pltpu.make_async_copy(src, dst, sems.at[n_dom + k]) for k, (src, dst) in enumerate(zip(model_in, model))]
    for copy in copies + later:
        copy.start()
    none = n_dom * tiles
    lid_s[none : none + 8, :] = jnp.full((8, LANES), -1, i32)
    cl_s[none : none + 8, :] = jnp.full((8, LANES), -1, i32)
    for ref in (spc, spn):
        ref[none : none + 8, :] = jnp.zeros((8, LANES), i32)
    unit[:, none : none + 8, :] = jnp.zeros((3, 8, LANES), f32)
    basis_s[none * 8 : none * 8 + 16, :] = jnp.zeros((16, LANES), f32)
    slope_s[none * 8 : none * 8 + 16, :] = jnp.zeros((16, LANES), f32)
    for ref in (sums, grads):
        ref[...] = jnp.zeros(ref.shape, f32)
    for ref in (joined_s, lat_s, dpre_s, dz_s, back_s):
        ref[none : none + 2] = jnp.zeros((2, width, LANES), f32)
    total[...] = jnp.zeros(total.shape, f32)
    for copy in copies:
        copy.wait()

    pairs = CHUNK // 2
    count = jnp.int32(0)
    near = jnp.int32(0)
    for d in range(n_dom):
        a, b = d // wy, d % wy
        live = jnp.max(raw[d, 2 * tiles + 5 : 2 * tiles + 6, :]).astype(i32)
        live = lax.shift_right_logical(live + 1, 1)
        da = lax.rem(a - own_a + 1 + wx, wx)
        db = lax.rem(b - own_b + 1 + wy, wy)
        touches = jnp.logical_and(da < 3, db < 3)
        for t in range(tiles // 2):
            tile_list[count + t] = d * (tiles // 2) + t
            near_list[near + t] = d * (tiles // 2) + t
        count = count + live
        near = near + jnp.where(touches, live, 0)
    for t in range(pairs):
        tile_list[count + t] = none // 2
        near_list[near + t] = none // 2
    chunks = lax.div(count + (pairs - 1), pairs)
    near_chunks = lax.div(near + (pairs - 1), pairs)

    def tiles_of(ids, chunk):
        firsts = [ids[chunk * pairs + j] * 2 for j in range(pairs)]
        return [first + k for first in firsts for k in range(2)]

    def wide(p):
        return slice(p * 2 * LANES, (p + 1) * 2 * LANES)

    def cut(j):
        return slice(j * LANES, (j + 1) * LANES)

    lane = iota((8, LANES), 1)
    for a in range(wx):
        for v in range(nv):
            low = raw[a * wy + 2 * v, 2 * tiles : 2 * tiles + 8, :]
            high = raw[a * wy + min(2 * v + 1, wy - 1), 2 * tiles : 2 * tiles + 8, :]
            posb[a * nv + v] = jnp.where(lane < 64, low, high)

    row = lane[0:1]
    for d in range(n_dom):
        a, b = d // wy, d % wy

        def ids(u, v, start):
            src = ((a + u - 1) % wx) * wy + (b + v - 1) % wy
            base = u * nv * LANES + ((b + v - 1) % wy) * 64 + 8192 * v
            skin = raw[src, 2 * tiles + 4 : 2 * tiles + 5, :].astype(i32) + base
            return pltpu.roll(skin, start, 1) if start else skin

        first = row + (nv * LANES + b * 64 + 8192)
        first = jnp.where(row >= 64, ids(0, 1, 64), first)
        first = jnp.where(row >= 96, ids(1, 0, 96), first)
        second = ids(1, 2, 0)
        second = jnp.where(row >= 32, ids(2, 1, 32), second)
        for k, (u, v) in enumerate(((0, 0), (0, 2), (2, 0), (2, 2))):
            second = jnp.where(row >= 64 + 8 * k, ids(u, v, 64 + 8 * k), second)
        center = raw[d, 0:tiles, :].astype(i32)
        entry = raw[d, tiles : 2 * tiles, :].astype(i32)
        shape = (8, LANES)
        code = jnp.where(
            entry < LANES,
            lane_pick(jnp.broadcast_to(first, shape), entry & 127),
            lane_pick(jnp.broadcast_to(second, shape), entry & 127),
        )
        side_y = lax.shift_right_logical(code, 13)
        lid = code & 8191
        side_x = (lid >= nv * LANES).astype(f32) + (lid >= 2 * nv * LANES).astype(f32) - 1.0
        clid = center + b * 64
        block = lax.shift_right_logical(lid, 7)
        got_n, got_c = [], []
        for q in range(4):
            value = None
            for s in range(n_src):
                src = ((a + s // nv - 1) % wx) * nv + s % nv
                picked = lane_pick(jnp.broadcast_to(posb[src, q : q + 1, :], shape), lid & 127)
                value = picked if value is None else jnp.where(block == s, picked, value)
            got_n.append(value)
            got_c.append(lane_pick(jnp.broadcast_to(posb[a * nv + b // 2, q : q + 1, :], shape), clid & 127))
        dx = got_n[0] + box_edge * side_x - got_c[0]
        dy = got_n[1] + box_edge * (side_y.astype(f32) - 1.0) - got_c[1]
        dz = got_n[2] - got_c[2]
        distance = jnp.sqrt(dx * dx + dy * dy + dz * dz + 1.0)
        inverse = 1.0 / distance
        rows = slice(d * tiles, (d + 1) * tiles)
        for q, part in enumerate((dx, dy, dz)):
            unit[q, rows, :] = part * inverse
        spn[rows, :] = got_n[3].astype(i32)
        spc[rows, :] = got_c[3].astype(i32)
        live = iota(shape, 0).astype(f32) < raw[d, 2 * tiles + 5 : 2 * tiles + 6, :]
        lid_s[rows, :] = jnp.where(live, lid, -1)
        cl_s[rows, :] = jnp.where(live, clid, -1)
        s1, c1 = sin_cos(distance * 0.25)
        env = jnp.exp(distance * (-1.0 / 32.0))
        c_k, s_k = [jnp.ones_like(c1), c1], [jnp.zeros_like(s1), s1]
        for k in range(2, 8):
            c_k.append(2.0 * c1 * c_k[-1] - c_k[-2])
            s_k.append(2.0 * c1 * s_k[-1] - s_k[-2])
        for k in range(8):
            basis = c_k[k] * env
            basis_s[pl.ds(d * 64 + k, 8, stride=8), :] = basis
            slope_s[pl.ds(d * 64 + k, 8, stride=8), :] = s_k[k] * env * (-k / 4.0) - basis * (1.0 / 32.0)

    def spots(tau):
        d = lax.shift_right_logical(tau, 3)
        a, b = lax.div(d, wy), lax.rem(d, wy)
        sources = [lax.rem(a + (s // nv - 1 + wx), wx) * nv + s % nv for s in range(n_src)]
        home = lax.rem(a, wx) * nv + lax.div(b, 2)
        return sources, home, lax.div(b, 2)

    def ones_and_zeros(lanes):
        return iota((LANES, lanes), 0).astype(bf16), jnp.ones((LANES, lanes), bf16), jnp.zeros((LANES, lanes), bf16)

    def ids_of(ref, taus):
        return jnp.concatenate([ref[pl.ds(tau, 1), :] for tau in taus], axis=1)

    def hot(ids_row):
        atom, one, zero = ones_and_zeros(ids_row.shape[1])
        return jnp.where(atom == ids_row.astype(f32).astype(bf16), one, zero)

    def side(parts):
        return jnp.concatenate(parts, axis=1)

    def pipelined(step, ids, chunks):
        step(tiles_of(ids, 0), None)

        def both(chunk, carry):
            step(tiles_of(ids, chunk), tiles_of(ids, chunk - 1))
            return carry

        lax.fori_loop(1, chunks, both, 0)
        step(None, tiles_of(ids, chunks - 1))

    def forward(new, old):
        if old:
            old_latent = side([lat_s[tau] for tau in old])
            mixed = old_latent * side([joined_s[tau] for tau in old])
        if new:
            sub = iota((8, LANES), 0)
            rhs = []
            for tau in new:
                hi, lo = halves(basis_s[pl.ds(pl.multiple_of(tau * 8, 8), 8), :])
                kinds = (sub == spc[pl.ds(tau, 1), :]).astype(f32) + (sub == spn[pl.ds(tau, 1), :]).astype(f32)
                rhs.append(jnp.concatenate([hi, lo, hi, kinds, kinds, jnp.zeros_like(hi)], axis=0).astype(bf16))
        if old:
            homes, hots = [], []
            for p in range(pairs):
                _, home, half = spots(old[2 * p])
                homes.append(home)
                hots.append(hot(ids_of(cl_s, old[2 * p : 2 * p + 2]) - half * LANES))
            z = product(dense[0], mixed)
        if new:
            both = jnp.dot(geo[...], side(rhs), preferred_element_type=f32)
        if old:
            active, slope = silu_and_slope(z)
        if new:
            latent, latent_slope = silu_and_slope(both[:width])
        if old:
            added = [sum_to(active[:, wide(p)], hots[p]) for p in range(pairs)]
            old_latent = old_latent + product(dense[1], active)
        if new:
            for j, tau in enumerate(new):
                joined_s[tau] = both[width:, cut(j)]
                dpre_s[tau] = latent_slope[:, cut(j)]
                lat_s[tau] = latent[:, cut(j)]
        if old:
            for j, tau in enumerate(old):
                dz_s[tau] = slope[:, cut(j)]
                lat_s[tau] = old_latent[:, cut(j)]
            for p in range(pairs):
                sums[homes[p]] += added[p]

    for copy in later:
        copy.wait()
    weight_factors(*model, geo, dense, radial_back, columns)
    pipelined(forward, tile_list, chunks)

    sub = iota((8, n_blk * LANES), 0)
    kinds = (sub == side([posb[k, 3:4, :] for k in range(n_blk)]).astype(i32)).astype(f32)
    empty = jnp.zeros_like(kinds)
    rhs = jnp.concatenate([empty, empty, empty, kinds, kinds, empty], axis=0).astype(bf16)
    start = jnp.dot(geo[...], rhs, preferred_element_type=f32)[width:]
    features = start + product(dense[6], side([sums[k] for k in range(n_blk)]))
    features = jnp.concatenate(parts(features), axis=0)
    for k in range(n_blk):
        feats2[k] = features[:, cut(k)]

    def middle(new, old):
        if old:
            old_joined, old_slope = hold_a[...], hold_b[...]
            old_hots = [hold_hot[p] for p in range(pairs)]
            old_latent = side([lat_s[tau] for tau in old])
            old_sources = [spots(old[2 * p])[0] for p in range(pairs)]
        if new:
            latent = side([lat_s[tau] for tau in new])
            joined, hots = [], []
            for p in range(pairs):
                sources, _, half = spots(new[2 * p])
                lid = ids_of(lid_s, new[2 * p : 2 * p + 2])
                own = hot(ids_of(cl_s, new[2 * p : 2 * p + 2]) - half * LANES)
                rows = [hot(lid - s * LANES) for s in range(n_src)]
                for v in range(nv):
                    rows[nv + v] = rows[nv + v] + (own if nv == 1 else jnp.where(half == v, own, jnp.zeros_like(own)))
                hots.append(jnp.concatenate(rows, axis=0))
                both = jnp.dot(side([feats2[s] for s in sources]), hots[-1], preferred_element_type=f32)
                joined.append(both[:width] + both[width:])
        if old:
            dmix = product(dense[3], old_slope)
        if new:
            joined = side(joined)
            z = product(dense[2], latent * joined)
        if old:
            spread = dmix * old_latent
            added = [sum_to(spread[:, wide(p)], old_hots[p]) for p in range(pairs)]
            back = dmix * old_joined
        if new:
            _, slope = silu_and_slope(z)
            hold_a[...] = joined
            hold_b[...] = slope
            for p in range(pairs):
                hold_hot[p] = hots[p]
        if old:
            for j, tau in enumerate(old):
                back_s[tau] = back[:, cut(j)]
            for p in range(pairs):
                for s in range(n_src):
                    grads[old_sources[p][s]] += added[p][:, cut(s)]

    pipelined(middle, tile_list, chunks)

    pulled_all = product(dense[7], side([grads[k] + columns[...] for k in range(n_blk)]))
    for k in range(n_blk):
        pulls[k] = pulled_all[:, cut(k)]

    own_block = own_a * nv + lax.div(own_b, 2)

    def backward(new, old):
        if old:
            old_pre = hold_a[...]
            slopes = [slope_s[pl.ds(pl.multiple_of(tau * 8, 8), 8), :] for tau in old]
            units = [[unit[q, pl.ds(tau, 1), :] for q in range(3)] for tau in old]
        if new:
            back = side([back_s[tau] for tau in new])
            dz = side([dz_s[tau] for tau in new])
            joined = side([joined_s[tau] for tau in new])
            dpre = side([dpre_s[tau] for tau in new])
            pulled = []
            for tau in new:
                _, home, _ = spots(tau)
                pulled.append(lane_pick(pulls[home], cl_s[pl.ds(tau, 1), :] & 127))
        if old:
            hits, chits = [], []
            for p in range(pairs):
                sources, home, half = spots(old[2 * p])
                lid = ids_of(lid_s, old[2 * p : 2 * p + 2])
                hit = jnp.full(lid.shape, -1, i32)
                for s in range(n_src):
                    this = jnp.where(sources[s] == own_block, s, -2)
                    hit = jnp.where(lax.shift_right_arithmetic(lid, 7) == this, lid & 127, hit)
                hits.append(hit)
                chits.append(jnp.where(home == own_block, ids_of(cl_s, old[2 * p : 2 * p + 2]) - half * LANES, -1))
            many = hot(side(hits)) - hot(side(chits))
            dbasis = product(radial_back[...], old_pre)
        if new:
            active = side(pulled) + product(dense[4], back)
        if old:
            moves = []
            for j in range(CHUNK):
                rows = []
                for m in range(members):
                    along = jnp.sum(dbasis[m * 8 : (m + 1) * 8, cut(j)] * slopes[j], axis=0, keepdims=True)
                    rows += [along * units[j][q] for q in range(3)]
                rows.append(jnp.zeros((8 - 3 * members, LANES), f32))
                moves.append(jnp.concatenate(rows, axis=0))
            added = sum_to(side(moves), many)
        if new:
            dmix = product(dense[5], active * dz)
            hold_a[...] = (back + dmix * joined) * dpre
        if old:
            total[...] += added

    pipelined(backward, near_list, near_chunks)

    result = -total[...]
    result = jnp.where(lax.rem(own_b, 2) == 1, pltpu.roll(result, 64, 1), result)
    for m in range(members):
        for q in range(3):
            out[m, q, 0] = result[m * 3 + q : m * 3 + q + 1, 0:64]


def window(size):
    return min(size, 2 * REACH + 1)


def shift(value, axis, by):
    peers = lax.axis_size(axis)
    return lax.ppermute(value, axis, [(i, (i + by) % peers) for i in range(peers)])


def swap(value, by_core):
    sizes = [lax.axis_size(axis) for axis in ("gx", "gy", "gz")]
    pairs = []
    for a in range(sizes[0]):
        for b in range(sizes[1]):
            for c in range(sizes[2]):
                dx, dy, dz = by_core[c]
                pairs.append(((a * sizes[1] + b) * sizes[2] + c, ((a ^ dx) * sizes[1] + (b ^ dy)) * sizes[2] + (c ^ dz)))
    return lax.ppermute(value, ("gx", "gy", "gz"), pairs)


def gathered(own, gx, gy):
    if gx == 4 and gy == 2 and lax.axis_size("gz") == 2:
        fetch = (((0, 1), (2, 1)), ((1, 0), (3, 0)), ((1, 1), (3, 1)))
        far = swap(own, ((2, 0, 0), (2, 0, 0)))
        fetched = [swap(own, (low + (0,), high + (0,))) for low, high in fetch]
        handed = [swap(value, ((0, 0, 1), (0, 0, 1))) for value in fetched]

        def place():
            a, b, c = lax.axis_index("gx"), lax.axis_index("gy"), lax.axis_index("gz")
            slots = [(0, 0, a * 2 + b), (1, 0, (a ^ 2) * 2 + b)]
            for k, (low, high) in enumerate(fetch):
                mine = [jnp.where(c == 0, low[q], high[q]) for q in range(2)]
                other = [jnp.where(c == 0, high[q], low[q]) for q in range(2)]
                slots.append((2 + k, 0, (a ^ mine[0]) * 2 + (b ^ mine[1])))
                slots.append((5 + k, 0, (a ^ other[0]) * 2 + (b ^ other[1])))
            return a, b, slots

        return [own, far] + fetched + handed, place
    wx, wy = window(gx), window(gy)
    steps = list(range(wy // 2 + 1)) + list(range(wy // 2 + 1 - wy, 0))
    column = jnp.concatenate([own if s == 0 else shift(own, "gy", -s) for s in steps], axis=0)
    steps_x = list(range(wx // 2 + 1)) + list(range(wx // 2 + 1 - wx, 0))
    arrays = [column if s == 0 else shift(column, "gx", -s) for s in steps_x]

    def place():
        slots = [(k, at, k * wy + at) for k in range(wx) for at in range(wy)]
        return jnp.int32(0), jnp.int32(0), slots

    return arrays, place


def on_device(
    positions, species, centers, neighbours, masks, skin, embed, radial, w_mix, w_latent, w_update, readout
):
    gx, gy = lax.axis_size("gx"), lax.axis_size("gy")
    atoms = positions.shape[-1]
    members, _, channels = embed.shape
    width = members * channels
    raw = [pltpu.with_memory_space_constraint(x, pltpu.HBM) for x in (positions, species, centers, neighbours, masks, skin)]
    own = pl.pallas_call(
        pack_kernel,
        out_shape=jax.ShapeDtypeStruct((PACK_ROWS, LANES), f32),
        in_specs=[pl.BlockSpec(memory_space=pltpu.VMEM)] * len(raw),
        out_specs=pl.BlockSpec(memory_space=pl.ANY),
        scratch_shapes=[pltpu.VMEM((PACK_ROWS, LANES), f32), pltpu.SemaphoreType.DMA],
        compiler_params=pltpu.CompilerParams(vmem_limit_bytes=16 * 1024 * 1024),
        name="pack",
    )(*raw)
    model = (jnp.transpose(embed, (1, 0, 2)), radial, w_mix, w_latent, w_update, readout)
    model = tuple(pltpu.with_memory_space_constraint(part, pltpu.HBM) for part in model)
    arrays, place = gathered(own, gx, gy)
    wx, wy = window(gx), window(gy)
    n_dom = wx * wy
    n_tiles = n_dom * 8
    n_blk = wx * ((wy + 1) // 2)
    held = 5 * (n_tiles + 2) * width * LANES * 4 + 12 * 1024 * 1024
    per_tile = pltpu.VMEM((n_tiles + 2, width, LANES), f32)
    per_block = pltpu.VMEM((n_blk, width, LANES), f32)
    row_ids = pltpu.VMEM((n_tiles + 8, LANES), i32)

    def body(*refs):
        force_kernel(wx, wy, place, len(arrays), *refs)

    return pl.pallas_call(
        body,
        out_shape=jax.ShapeDtypeStruct((members, 3, 1, 1, atoms), f32),
        scratch_shapes=[
            pltpu.VMEM((n_dom, PACK_ROWS, LANES), f32),
            pltpu.VMEM((n_blk, 8, LANES), f32),
            row_ids,
            row_ids,
            row_ids,
            row_ids,
            pltpu.VMEM((3, n_tiles + 8, LANES), f32),
            pltpu.VMEM((n_tiles * 8 + 16, LANES), f32),
            pltpu.VMEM((n_tiles * 8 + 16, LANES), f32),
            pltpu.VMEM((n_blk, 2 * width, LANES), bf16),
            per_block,
            per_block,
            per_block,
            per_tile,
            per_tile,
            per_tile,
            per_tile,
            per_tile,
            pltpu.VMEM((8, LANES), f32),
            pltpu.SMEM((n_tiles // 2 + CHUNK // 2 + 4,), i32),
            pltpu.SMEM((n_tiles // 2 + CHUNK // 2 + 4,), i32),
            pltpu.VMEM((width, CHUNK * LANES), f32),
            pltpu.VMEM((width, CHUNK * LANES), f32),
            pltpu.VMEM((CHUNK // 2, 3 * n_blk // wx * LANES, 2 * LANES), bf16),
        ]
        + [
            pltpu.VMEM((2 * width, 48), bf16),
            pltpu.VMEM((8, width, 3 * width), bf16),
            pltpu.VMEM((members * 8, 3 * width), bf16),
            pltpu.VMEM((width, LANES), f32),
        ]
        + [pltpu.VMEM(part.shape, part.dtype) for part in model]
        + [pltpu.SemaphoreType.DMA((n_dom + len(model),))],
        in_specs=[pl.BlockSpec(memory_space=pl.ANY)] * len(arrays) + [pl.BlockSpec(memory_space=pltpu.HBM)] * len(model),
        compiler_params=pltpu.CompilerParams(vmem_limit_bytes=held),
        name="forces",
    )(*arrays, *model)


def solution(mesh):
    return jax.shard_map(
        on_device,
        mesh=mesh,
        in_specs=(
            P(None, ("groups", "gx"), "gy", None),
            P(("groups", "gx"), "gy", None),
            P(("groups", "gx"), "gy", None),
            P(("groups", "gx"), "gy", None),
            P(("groups", "gx"), "gy", None),
            P(("groups", "gx"), "gy", None),
            P("gz", None, None),
            P("gz", None, None),
            P("gz", None, None, None),
            P("gz", None, None, None),
            P("gz", None, None, None),
            P("gz", None),
        ),
        out_specs=P("gz", None, ("groups", "gx"), "gy", None),
        check_vma=False,
    )
```

```python
import jax
import jax.numpy as jnp
from jax import lax
from jax.experimental import pallas as pl
from jax.experimental.pallas import tpu as pltpu
from jax.sharding import PartitionSpec as P

NEIGH = 16
box_edge = 20.0
energy_scale = 16.0
REACH = 3
LANES = 128
CHUNK = 12
PACK_ROWS = 24
f32 = jnp.float32
bf16 = jnp.bfloat16
i32 = jnp.int32


def iota(shape, dim):
    return lax.broadcasted_iota(i32, shape, dim)


def halves(x):
    hi = x.astype(bf16).astype(f32)
    return hi, x - hi


def pack_kernel(pos, species, centers, neighbours, masks, skin, packed, out, sem):
    tiles = centers.shape[-1] // LANES
    atoms = pos.shape[-1]
    ghosts = skin.shape[-1]
    out[...] = jnp.zeros(out.shape, f32)
    live = jnp.zeros((1, LANES), f32)
    for t in range(tiles):
        cut = slice(t * LANES, (t + 1) * LANES)
        out[t : t + 1, :] = centers[0, :, cut].astype(f32)
        out[tiles + t : tiles + t + 1, :] = neighbours[0, :, cut].astype(f32)
        live = live + masks[0, :, cut].astype(f32)
    base = 2 * tiles
    for q in range(3):
        row = pos[q, 0]
        out[base + q : base + q + 1, :] = jnp.concatenate([row, row], axis=1)
    row = species[0].astype(f32)
    out[base + 3 : base + 4, :] = jnp.concatenate([row, row], axis=1)
    out[base + 4 : base + 5, 0:ghosts] = skin[0].astype(f32)
    out[base + 5 : base + 6, :] = live
    copy = pltpu.make_async_copy(out, packed, sem)
    copy.start()
    copy.wait()


def block_diag(blocks):
    rows = []
    for at, block in enumerate(blocks):
        parts = [block if k == at else jnp.zeros((block.shape[0], other.shape[1]), f32) for k, other in enumerate(blocks)]
        rows.append(jnp.concatenate(parts, axis=1))
    return jnp.concatenate(rows, axis=0)


def split_left(matrix):
    hi, lo = halves(matrix)
    return jnp.concatenate([hi, hi, lo], axis=1).astype(bf16)


def parts(x):
    hi = x.astype(bf16)
    return hi, (x - hi.astype(f32)).astype(bf16)


def weight_factors(embed, radial, w_mix, w_latent, w_update, readout, geo, dense, radial_back, columns):
    elements, members, channels = embed.shape
    width = members * channels
    embed_t = jnp.concatenate([embed[:, m, :].T for m in range(members)], axis=0)
    embed_t = jnp.concatenate([embed_t, jnp.zeros((width, 8 - elements), f32)], axis=1)
    radial_t = jnp.concatenate([radial[m].T for m in range(members)], axis=0)
    r_hi, r_lo = halves(0.5 * radial_t)
    e_hi, e_lo = halves(embed_t)
    none = jnp.zeros_like(r_hi)
    geo[...] = jnp.concatenate(
        [
            jnp.concatenate([r_hi, r_hi, r_lo, none, none, none], axis=1),
            jnp.concatenate([none, none, none, e_hi, e_lo, none], axis=1),
        ],
        axis=0,
    ).astype(bf16)
    mix0 = block_diag([w_mix[m, 0] for m in range(members)])
    mix1 = block_diag([w_mix[m, 1] for m in range(members)])
    latent = block_diag([w_latent[m, 0] for m in range(members)])
    update0 = block_diag([w_update[m, 0] for m in range(members)])
    update1 = block_diag([w_update[m, 1] for m in range(members)])
    radial_back[...] = split_left(0.5 * block_diag([radial[m] for m in range(members)]))
    read_row = jnp.concatenate([readout[m : m + 1, :] for m in range(members)], axis=1)
    eye = (iota((width, width), 0) == iota((width, width), 1)).astype(f32)
    read = jnp.sum(eye * read_row, axis=1, keepdims=True)
    pull = jnp.sum(update1.T * read, axis=0, keepdims=True) * (energy_scale / NEIGH)
    columns[...] = jnp.broadcast_to(read * energy_scale, (width, LANES))
    factors = (
        0.5 * mix0.T, latent.T, 0.5 * mix1.T, 0.5 * mix1 * pull, latent, 0.5 * mix0,
        update0.T * (1.0 / NEIGH), update0 * (1.0 / NEIGH),
    )
    for at, matrix in enumerate(factors):
        dense[at] = split_left(matrix)


def lane_pick(table, lanes):
    return jnp.take_along_axis(table, jnp.broadcast_to(lanes, table.shape), axis=1, mode="promise_in_bounds")


def product(left, x):
    hi, lo = parts(x)
    return jnp.dot(left, jnp.concatenate([hi, lo, hi], axis=0), preferred_element_type=f32)


def sum_to(values, hot):
    hi, lo = parts(values) if values.shape[0] % 16 == 0 else halves(values)
    both = lax.dot_general(
        jnp.concatenate([hi, lo], axis=0).astype(bf16), hot, (((1,), (1,)), ((), ())), preferred_element_type=f32
    )
    return both[: values.shape[0]] + both[values.shape[0] :]


def silu(h):
    return h + h * jnp.tanh(h)


def silu_and_slope(h):
    t = jnp.tanh(h)
    p = 1.0 + t
    return h * p, p + p * (h - h * t)


def sin_cos(x):
    turns = jnp.floor(x * 0.15915494309189535 + 0.5)
    r = (x - turns * 6.28125) - turns * 1.9353071795864769e-3
    h = 0.5 * r
    q = h * h
    s = h * (1.0 + q * (-1 / 6 + q * (1 / 120 + q * (-1 / 5040 + q * (1 / 362880 + q * (-1 / 39916800 + q * (1 / 6227020800)))))))
    c = 1.0 + q * (-1 / 2 + q * (1 / 24 + q * (-1 / 720 + q * (1 / 40320 + q * (-1 / 3628800 + q * (1 / 479001600 - q * (1 / 87178291200)))))))
    return 2.0 * s * c, 1.0 - 2.0 * s * s


def force_kernel(wx, wy, place, n_in, *refs):
    arrived = refs[:n_in]
    model_in, out = refs[n_in : n_in + 6], refs[n_in + 6]
    (raw, posb, lid_s, cl_s, spc, spn, unit, basis_s, slope_s, feats2, sums, grads, pulls,
     joined_s, lat_s, dpre_s, dz_s, back_s, total, tile_list, near_list,
     hold_a, hold_b, hold_hot, geo, dense, radial_back, columns, *model, sems) = refs[n_in + 7 :]
    tiles = 8
    n_dom = wx * wy
    nv = (wy + 1) // 2
    n_src = 3 * nv
    n_blk = wx * nv
    width = feats2.shape[1] // 2
    members = out.shape[0]
    own_a, own_b, slots = place()

    copies = [
        pltpu.make_async_copy(arrived[ref].at[pl.ds(at * PACK_ROWS, PACK_ROWS), :], raw.at[slot], sems.at[k])
        for k, (ref, at, slot) in enumerate(slots)
    ]
    later = [pltpu.make_async_copy(src, dst, sems.at[n_dom + k]) for k, (src, dst) in enumerate(zip(model_in, model))]
    for copy in copies + later:
        copy.start()
    none = n_dom * tiles
    lid_s[none : none + 8, :] = jnp.full((8, LANES), -1, i32)
    cl_s[none : none + 8, :] = jnp.full((8, LANES), -1, i32)
    for ref in (spc, spn):
        ref[none : none + 8, :] = jnp.zeros((8, LANES), i32)
    unit[:, none : none + 8, :] = jnp.zeros((3, 8, LANES), f32)
    basis_s[none * 8 : none * 8 + 16, :] = jnp.zeros((16, LANES), f32)
    slope_s[none * 8 : none * 8 + 16, :] = jnp.zeros((16, LANES), f32)
    for ref in (sums, grads):
        ref[...] = jnp.zeros(ref.shape, f32)
    for ref in (joined_s, lat_s, dpre_s, dz_s, back_s):
        ref[none : none + 2] = jnp.zeros((2, width, LANES), f32)
    total[...] = jnp.zeros(total.shape, f32)
    for copy in copies:
        copy.wait()

    pairs = CHUNK // 2
    count = jnp.int32(0)
    near = jnp.int32(0)
    for d in range(n_dom):
        a, b = d // wy, d % wy
        live = jnp.max(raw[d, 2 * tiles + 5 : 2 * tiles + 6, :]).astype(i32)
        live = lax.shift_right_logical(live + 1, 1)
        da = lax.rem(a - own_a + 1 + wx, wx)
        db = lax.rem(b - own_b + 1 + wy, wy)
        touches = jnp.logical_and(da < 3, db < 3)
        for t in range(tiles // 2):
            tile_list[count + t] = d * (tiles // 2) + t
            near_list[near + t] = d * (tiles // 2) + t
        count = count + live
        near = near + jnp.where(touches, live, 0)
    for t in range(pairs):
        tile_list[count + t] = none // 2
        near_list[near + t] = none // 2
    chunks = lax.div(count + (pairs - 1), pairs)
    near_chunks = lax.div(near + (pairs - 1), pairs)

    def tiles_of(ids, chunk):
        firsts = [ids[chunk * pairs + j] * 2 for j in range(pairs)]
        return [first + k for first in firsts for k in range(2)]

    def wide(p):
        return slice(p * 2 * LANES, (p + 1) * 2 * LANES)

    def cut(j):
        return slice(j * LANES, (j + 1) * LANES)

    lane = iota((8, LANES), 1)
    for a in range(wx):
        for v in range(nv):
            low = raw[a * wy + 2 * v, 2 * tiles : 2 * tiles + 8, :]
            high = raw[a * wy + min(2 * v + 1, wy - 1), 2 * tiles : 2 * tiles + 8, :]
            posb[a * nv + v] = jnp.where(lane < 64, low, high)

    row = lane[0:1]
    for d in range(n_dom):
        a, b = d // wy, d % wy

        def ids(u, v, start):
            src = ((a + u - 1) % wx) * wy + (b + v - 1) % wy
            base = u * nv * LANES + ((b + v - 1) % wy) * 64 + 8192 * v
            skin = raw[src, 2 * tiles + 4 : 2 * tiles + 5, :].astype(i32) + base
            return pltpu.roll(skin, start, 1) if start else skin

        first = row + (nv * LANES + b * 64 + 8192)
        first = jnp.where(row >= 64, ids(0, 1, 64), first)
        first = jnp.where(row >= 96, ids(1, 0, 96), first)
        second = ids(1, 2, 0)
        second = jnp.where(row >= 32, ids(2, 1, 32), second)
        for k, (u, v) in enumerate(((0, 0), (0, 2), (2, 0), (2, 2))):
            second = jnp.where(row >= 64 + 8 * k, ids(u, v, 64 + 8 * k), second)
        center = raw[d, 0:tiles, :].astype(i32)
        entry = raw[d, tiles : 2 * tiles, :].astype(i32)
        shape = (8, LANES)
        code = jnp.where(
            entry < LANES,
            lane_pick(jnp.broadcast_to(first, shape), entry & 127),
            lane_pick(jnp.broadcast_to(second, shape), entry & 127),
        )
        side_y = lax.shift_right_logical(code, 13)
        lid = code & 8191
        side_x = (lid >= nv * LANES).astype(f32) + (lid >= 2 * nv * LANES).astype(f32) - 1.0
        clid = center + b * 64
        block = lax.shift_right_logical(lid, 7)
        got_n, got_c = [], []
        for q in range(4):
            value = None
            for s in range(n_src):
                src = ((a + s // nv - 1) % wx) * nv + s % nv
                picked = lane_pick(jnp.broadcast_to(posb[src, q : q + 1, :], shape), lid & 127)
                value = picked if value is None else jnp.where(block == s, picked, value)
            got_n.append(value)
            got_c.append(lane_pick(jnp.broadcast_to(posb[a * nv + b // 2, q : q + 1, :], shape), clid & 127))
        dx = got_n[0] + box_edge * side_x - got_c[0]
        dy = got_n[1] + box_edge * (side_y.astype(f32) - 1.0) - got_c[1]
        dz = got_n[2] - got_c[2]
        distance = jnp.sqrt(dx * dx + dy * dy + dz * dz + 1.0)
        inverse = 1.0 / distance
        rows = slice(d * tiles, (d + 1) * tiles)
        for q, part in enumerate((dx, dy, dz)):
            unit[q, rows, :] = part * inverse
        spn[rows, :] = got_n[3].astype(i32)
        spc[rows, :] = got_c[3].astype(i32)
        live = iota(shape, 0).astype(f32) < raw[d, 2 * tiles + 5 : 2 * tiles + 6, :]
        lid_s[rows, :] = jnp.where(live, lid, -1)
        cl_s[rows, :] = jnp.where(live, clid, -1)
        s1, c1 = sin_cos(distance * 0.25)
        env = jnp.exp(distance * (-1.0 / 32.0))
        c_k, s_k = [jnp.ones_like(c1), c1], [jnp.zeros_like(s1), s1]
        for k in range(2, 8):
            c_k.append(2.0 * c1 * c_k[-1] - c_k[-2])
            s_k.append(2.0 * c1 * s_k[-1] - s_k[-2])
        for k in range(8):
            basis = c_k[k] * env
            basis_s[pl.ds(d * 64 + k, 8, stride=8), :] = basis
            slope_s[pl.ds(d * 64 + k, 8, stride=8), :] = s_k[k] * env * (-k / 4.0) - basis * (1.0 / 32.0)

    def spots(tau):
        d = lax.shift_right_logical(tau, 3)
        a, b = lax.div(d, wy), lax.rem(d, wy)
        sources = [lax.rem(a + (s // nv - 1 + wx), wx) * nv + s % nv for s in range(n_src)]
        home = lax.rem(a, wx) * nv + lax.div(b, 2)
        return sources, home, lax.div(b, 2)

    def ones_and_zeros(lanes):
        return iota((LANES, lanes), 0).astype(bf16), jnp.ones((LANES, lanes), bf16), jnp.zeros((LANES, lanes), bf16)

    def ids_of(ref, taus):
        return jnp.concatenate([ref[pl.ds(tau, 1), :] for tau in taus], axis=1)

    def hot(ids_row):
        atom, one, zero = ones_and_zeros(ids_row.shape[1])
        return jnp.where(atom == ids_row.astype(f32).astype(bf16), one, zero)

    def side(parts):
        return jnp.concatenate(parts, axis=1)

    def pipelined(step, ids, chunks):
        step(tiles_of(ids, 0), None)

        def both(chunk, carry):
            step(tiles_of(ids, chunk), tiles_of(ids, chunk - 1))
            return carry

        lax.fori_loop(1, chunks, both, 0)
        step(None, tiles_of(ids, chunks - 1))

    def forward(new, old):
        if old:
            old_latent = side([lat_s[tau] for tau in old])
            mixed = old_latent * side([joined_s[tau] for tau in old])
        if new:
            sub = iota((8, LANES), 0)
            rhs = []
            for tau in new:
                hi, lo = halves(basis_s[pl.ds(pl.multiple_of(tau * 8, 8), 8), :])
                kinds = (sub == spc[pl.ds(tau, 1), :]).astype(f32) + (sub == spn[pl.ds(tau, 1), :]).astype(f32)
                rhs.append(jnp.concatenate([hi, lo, hi, kinds, kinds, jnp.zeros_like(hi)], axis=0).astype(bf16))
        if old:
            homes, hots = [], []
            for p in range(pairs):
                _, home, half = spots(old[2 * p])
                homes.append(home)
                hots.append(hot(ids_of(cl_s, old[2 * p : 2 * p + 2]) - half * LANES))
            z = product(dense[0], mixed)
        if new:
            both = jnp.dot(geo[...], side(rhs), preferred_element_type=f32)
        if old:
            active, slope = silu_and_slope(z)
        if new:
            latent, latent_slope = silu_and_slope(both[:width])
        if old:
            added = [sum_to(active[:, wide(p)], hots[p]) for p in range(pairs)]
            old_latent = old_latent + product(dense[1], active)
        if new:
            for j, tau in enumerate(new):
                joined_s[tau] = both[width:, cut(j)]
                dpre_s[tau] = latent_slope[:, cut(j)]
                lat_s[tau] = latent[:, cut(j)]
        if old:
            for j, tau in enumerate(old):
                dz_s[tau] = slope[:, cut(j)]
                lat_s[tau] = old_latent[:, cut(j)]
            for p in range(pairs):
                sums[homes[p]] += added[p]

    for copy in later:
        copy.wait()
    weight_factors(*model, geo, dense, radial_back, columns)
    pipelined(forward, tile_list, chunks)

    sub = iota((8, n_blk * LANES), 0)
    kinds = (sub == side([posb[k, 3:4, :] for k in range(n_blk)]).astype(i32)).astype(f32)
    empty = jnp.zeros_like(kinds)
    rhs = jnp.concatenate([empty, empty, empty, kinds, kinds, empty], axis=0).astype(bf16)
    start = jnp.dot(geo[...], rhs, preferred_element_type=f32)[width:]
    features = start + product(dense[6], side([sums[k] for k in range(n_blk)]))
    features = jnp.concatenate(parts(features), axis=0)
    for k in range(n_blk):
        feats2[k] = features[:, cut(k)]

    def middle(new, old):
        if old:
            old_joined, old_slope = hold_a[...], hold_b[...]
            old_hots = [hold_hot[p] for p in range(pairs)]
            old_latent = side([lat_s[tau] for tau in old])
            old_sources = [spots(old[2 * p])[0] for p in range(pairs)]
        if new:
            latent = side([lat_s[tau] for tau in new])
            joined, hots = [], []
            for p in range(pairs):
                sources, _, half = spots(new[2 * p])
                lid = ids_of(lid_s, new[2 * p : 2 * p + 2])
                own = hot(ids_of(cl_s, new[2 * p : 2 * p + 2]) - half * LANES)
                rows = [hot(lid - s * LANES) for s in range(n_src)]
                for v in range(nv):
                    rows[nv + v] = rows[nv + v] + (own if nv == 1 else jnp.where(half == v, own, jnp.zeros_like(own)))
                hots.append(jnp.concatenate(rows, axis=0))
                both = jnp.dot(side([feats2[s] for s in sources]), hots[-1], preferred_element_type=f32)
                joined.append(both[:width] + both[width:])
        if old:
            dmix = product(dense[3], old_slope)
        if new:
            joined = side(joined)
            z = product(dense[2], latent * joined)
        if old:
            spread = dmix * old_latent
            added = [sum_to(spread[:, wide(p)], old_hots[p]) for p in range(pairs)]
            back = dmix * old_joined
        if new:
            _, slope = silu_and_slope(z)
            hold_a[...] = joined
            hold_b[...] = slope
            for p in range(pairs):
                hold_hot[p] = hots[p]
        if old:
            for j, tau in enumerate(old):
                back_s[tau] = back[:, cut(j)]
            for p in range(pairs):
                for s in range(n_src):
                    grads[old_sources[p][s]] += added[p][:, cut(s)]

    pipelined(middle, tile_list, chunks)

    pulled_all = product(dense[7], side([grads[k] + columns[...] for k in range(n_blk)]))
    for k in range(n_blk):
        pulls[k] = pulled_all[:, cut(k)]

    own_block = own_a * nv + lax.div(own_b, 2)

    def backward(new, old):
        if old:
            old_pre = hold_a[...]
            slopes = [slope_s[pl.ds(pl.multiple_of(tau * 8, 8), 8), :] for tau in old]
            units = [[unit[q, pl.ds(tau, 1), :] for q in range(3)] for tau in old]
        if new:
            back = side([back_s[tau] for tau in new])
            dz = side([dz_s[tau] for tau in new])
            joined = side([joined_s[tau] for tau in new])
            dpre = side([dpre_s[tau] for tau in new])
            pulled = []
            for tau in new:
                _, home, _ = spots(tau)
                pulled.append(lane_pick(pulls[home], cl_s[pl.ds(tau, 1), :] & 127))
        if old:
            hits, chits = [], []
            for p in range(pairs):
                sources, home, half = spots(old[2 * p])
                lid = ids_of(lid_s, old[2 * p : 2 * p + 2])
                hit = jnp.full(lid.shape, -1, i32)
                for s in range(n_src):
                    this = jnp.where(sources[s] == own_block, s, -2)
                    hit = jnp.where(lax.shift_right_arithmetic(lid, 7) == this, lid & 127, hit)
                hits.append(hit)
                chits.append(jnp.where(home == own_block, ids_of(cl_s, old[2 * p : 2 * p + 2]) - half * LANES, -1))
            many = hot(side(hits)) - hot(side(chits))
            dbasis = product(radial_back[...], old_pre)
        if new:
            active = side(pulled) + product(dense[4], back)
        if old:
            moves = []
            for j in range(CHUNK):
                rows = []
                for m in range(members):
                    along = jnp.sum(dbasis[m * 8 : (m + 1) * 8, cut(j)] * slopes[j], axis=0, keepdims=True)
                    rows += [along * units[j][q] for q in range(3)]
                rows.append(jnp.zeros((8 - 3 * members, LANES), f32))
                moves.append(jnp.concatenate(rows, axis=0))
            added = sum_to(side(moves), many)
        if new:
            dmix = product(dense[5], active * dz)
            hold_a[...] = (back + dmix * joined) * dpre
        if old:
            total[...] += added

    pipelined(backward, near_list, near_chunks)

    result = -total[...]
    result = jnp.where(lax.rem(own_b, 2) == 1, pltpu.roll(result, 64, 1), result)
    for m in range(members):
        for q in range(3):
            out[m, q, 0] = result[m * 3 + q : m * 3 + q + 1, 0:64]


def window(size):
    return min(size, 2 * REACH + 1)


def shift(value, axis, by):
    peers = lax.axis_size(axis)
    return lax.ppermute(value, axis, [(i, (i + by) % peers) for i in range(peers)])


def swap(value, by_core):
    sizes = [lax.axis_size(axis) for axis in ("gx", "gy", "gz")]
    pairs = []
    for a in range(sizes[0]):
        for b in range(sizes[1]):
            for c in range(sizes[2]):
                dx, dy, dz = by_core[c]
                pairs.append(((a * sizes[1] + b) * sizes[2] + c, ((a ^ dx) * sizes[1] + (b ^ dy)) * sizes[2] + (c ^ dz)))
    return lax.ppermute(value, ("gx", "gy", "gz"), pairs)


def gathered(own, gx, gy):
    if gx == 4 and gy == 2 and lax.axis_size("gz") == 2:
        fetch = (((0, 1), (2, 1)), ((1, 0), (3, 0)), ((1, 1), (3, 1)))
        far = swap(own, ((2, 0, 0), (2, 0, 0)))
        fetched = [swap(own, (low + (0,), high + (0,))) for low, high in fetch]
        handed = [swap(value, ((0, 0, 1), (0, 0, 1))) for value in fetched]

        def place():
            a, b, c = lax.axis_index("gx"), lax.axis_index("gy"), lax.axis_index("gz")
            slots = [(0, 0, a * 2 + b), (1, 0, (a ^ 2) * 2 + b)]
            for k, (low, high) in enumerate(fetch):
                mine = [jnp.where(c == 0, low[q], high[q]) for q in range(2)]
                other = [jnp.where(c == 0, high[q], low[q]) for q in range(2)]
                slots.append((2 + k, 0, (a ^ mine[0]) * 2 + (b ^ mine[1])))
                slots.append((5 + k, 0, (a ^ other[0]) * 2 + (b ^ other[1])))
            return a, b, slots

        return [own, far] + fetched + handed, place
    wx, wy = window(gx), window(gy)
    steps = list(range(wy // 2 + 1)) + list(range(wy // 2 + 1 - wy, 0))
    column = jnp.concatenate([own if s == 0 else shift(own, "gy", -s) for s in steps], axis=0)
    steps_x = list(range(wx // 2 + 1)) + list(range(wx // 2 + 1 - wx, 0))
    arrays = [column if s == 0 else shift(column, "gx", -s) for s in steps_x]

    def place():
        slots = [(k, at, k * wy + at) for k in range(wx) for at in range(wy)]
        return jnp.int32(0), jnp.int32(0), slots

    return arrays, place


def on_device(
    positions, species, centers, neighbours, masks, skin, embed, radial, w_mix, w_latent, w_update, readout
):
    gx, gy = lax.axis_size("gx"), lax.axis_size("gy")
    atoms = positions.shape[-1]
    members, _, channels = embed.shape
    width = members * channels
    raw = [pltpu.with_memory_space_constraint(x, pltpu.HBM) for x in (positions, species, centers, neighbours, masks, skin)]
    own = pl.pallas_call(
        pack_kernel,
        out_shape=jax.ShapeDtypeStruct((PACK_ROWS, LANES), f32),
        in_specs=[pl.BlockSpec(memory_space=pltpu.VMEM)] * len(raw),
        out_specs=pl.BlockSpec(memory_space=pl.ANY),
        scratch_shapes=[pltpu.VMEM((PACK_ROWS, LANES), f32), pltpu.SemaphoreType.DMA],
        compiler_params=pltpu.CompilerParams(vmem_limit_bytes=16 * 1024 * 1024),
        name="pack",
    )(*raw)
    model = (jnp.transpose(embed, (1, 0, 2)), radial, w_mix, w_latent, w_update, readout)
    model = tuple(pltpu.with_memory_space_constraint(part, pltpu.HBM) for part in model)
    arrays, place = gathered(own, gx, gy)
    wx, wy = window(gx), window(gy)
    n_dom = wx * wy
    n_tiles = n_dom * 8
    n_blk = wx * ((wy + 1) // 2)
    held = 5 * (n_tiles + 2) * width * LANES * 4 + 12 * 1024 * 1024
    per_tile = pltpu.VMEM((n_tiles + 2, width, LANES), f32)
    per_block = pltpu.VMEM((n_blk, width, LANES), f32)
    row_ids = pltpu.VMEM((n_tiles + 8, LANES), i32)

    def body(*refs):
        force_kernel(wx, wy, place, len(arrays), *refs)

    return pl.pallas_call(
        body,
        out_shape=jax.ShapeDtypeStruct((members, 3, 1, 1, atoms), f32),
        scratch_shapes=[
            pltpu.VMEM((n_dom, PACK_ROWS, LANES), f32),
            pltpu.VMEM((n_blk, 8, LANES), f32),
            row_ids,
            row_ids,
            row_ids,
            row_ids,
            pltpu.VMEM((3, n_tiles + 8, LANES), f32),
            pltpu.VMEM((n_tiles * 8 + 16, LANES), f32),
            pltpu.VMEM((n_tiles * 8 + 16, LANES), f32),
            pltpu.VMEM((n_blk, 2 * width, LANES), bf16),
            per_block,
            per_block,
            per_block,
            per_tile,
            per_tile,
            per_tile,
            per_tile,
            per_tile,
            pltpu.VMEM((8, LANES), f32),
            pltpu.SMEM((n_tiles // 2 + CHUNK // 2 + 4,), i32),
            pltpu.SMEM((n_tiles // 2 + CHUNK // 2 + 4,), i32),
            pltpu.VMEM((width, CHUNK * LANES), f32),
            pltpu.VMEM((width, CHUNK * LANES), f32),
            pltpu.VMEM((CHUNK // 2, 3 * n_blk // wx * LANES, 2 * LANES), bf16),
        ]
        + [
            pltpu.VMEM((2 * width, 48), bf16),
            pltpu.VMEM((8, width, 3 * width), bf16),
            pltpu.VMEM((members * 8, 3 * width), bf16),
            pltpu.VMEM((width, LANES), f32),
        ]
        + [pltpu.VMEM(part.shape, part.dtype) for part in model]
        + [pltpu.SemaphoreType.DMA((n_dom + len(model),))],
        in_specs=[pl.BlockSpec(memory_space=pl.ANY)] * len(arrays) + [pl.BlockSpec(memory_space=pltpu.HBM)] * len(model),
        compiler_params=pltpu.CompilerParams(vmem_limit_bytes=held),
        name="forces",
    )(*arrays, *model)


def solution(mesh):
    return jax.shard_map(
        on_device,
        mesh=mesh,
        in_specs=(
            P(None, ("groups", "gx"), "gy", None),
            P(("groups", "gx"), "gy", None),
            P(("groups", "gx"), "gy", None),
            P(("groups", "gx"), "gy", None),
            P(("groups", "gx"), "gy", None),
            P(("groups", "gx"), "gy", None),
            P("gz", None, None),
            P("gz", None, None),
            P("gz", None, None, None),
            P("gz", None, None, None),
            P("gz", None, None, None),
            P("gz", None),
        ),
        out_specs=P("gz", None, ("groups", "gx"), "gy", None),
        check_vma=False,
    )
```

```python
import jax
import jax.numpy as jnp
from jax import lax
from jax.experimental import pallas as pl
from jax.experimental.pallas import tpu as pltpu
from jax.sharding import PartitionSpec as P

NEIGH = 16
box_edge = 20.0
energy_scale = 16.0
REACH = 3
LANES = 128
CHUNK = 12
PACK_ROWS = 24
f32 = jnp.float32
bf16 = jnp.bfloat16
i32 = jnp.int32


def iota(shape, dim):
    return lax.broadcasted_iota(i32, shape, dim)


def halves(x):
    hi = x.astype(bf16).astype(f32)
    return hi, x - hi


def pack_kernel(pos, species, centers, neighbours, masks, skin, packed, out, sem):
    tiles = centers.shape[-1] // LANES
    atoms = pos.shape[-1]
    ghosts = skin.shape[-1]
    out[...] = jnp.zeros(out.shape, f32)
    live = jnp.zeros((1, LANES), f32)
    for t in range(tiles):
        cut = slice(t * LANES, (t + 1) * LANES)
        out[t : t + 1, :] = centers[0, :, cut].astype(f32)
        out[tiles + t : tiles + t + 1, :] = neighbours[0, :, cut].astype(f32)
        live = live + masks[0, :, cut].astype(f32)
    base = 2 * tiles
    for q in range(3):
        row = pos[q, 0]
        out[base + q : base + q + 1, :] = jnp.concatenate([row, row], axis=1)
    row = species[0].astype(f32)
    out[base + 3 : base + 4, :] = jnp.concatenate([row, row], axis=1)
    out[base + 4 : base + 5, 0:ghosts] = skin[0].astype(f32)
    out[base + 5 : base + 6, :] = live
    copy = pltpu.make_async_copy(out, packed, sem)
    copy.start()
    copy.wait()


def block_diag(blocks):
    rows = []
    for at, block in enumerate(blocks):
        parts = [block if k == at else jnp.zeros((block.shape[0], other.shape[1]), f32) for k, other in enumerate(blocks)]
        rows.append(jnp.concatenate(parts, axis=1))
    return jnp.concatenate(rows, axis=0)


def split_left(matrix):
    hi, lo = halves(matrix)
    return jnp.concatenate([hi, hi, lo], axis=1).astype(bf16)


def parts(x):
    hi = x.astype(bf16)
    return hi, (x - hi.astype(f32)).astype(bf16)


def weight_factors(embed, radial, w_mix, w_latent, w_update, readout, geo, dense, radial_back, columns):
    elements, members, channels = embed.shape
    width = members * channels
    embed_t = jnp.concatenate([embed[:, m, :].T for m in range(members)], axis=0)
    embed_t = jnp.concatenate([embed_t, jnp.zeros((width, 8 - elements), f32)], axis=1)
    radial_t = jnp.concatenate([radial[m].T for m in range(members)], axis=0)
    r_hi, r_lo = halves(0.5 * radial_t)
    e_hi, e_lo = halves(embed_t)
    none = jnp.zeros_like(r_hi)
    geo[...] = jnp.concatenate(
        [
            jnp.concatenate([r_hi, r_hi, r_lo, none, none, none], axis=1),
            jnp.concatenate([none, none, none, e_hi, e_lo, none], axis=1),
        ],
        axis=0,
    ).astype(bf16)
    mix0 = block_diag([w_mix[m, 0] for m in range(members)])
    mix1 = block_diag([w_mix[m, 1] for m in range(members)])
    latent = block_diag([w_latent[m, 0] for m in range(members)])
    update0 = block_diag([w_update[m, 0] for m in range(members)])
    update1 = block_diag([w_update[m, 1] for m in range(members)])
    radial_back[...] = split_left(0.5 * block_diag([radial[m] for m in range(members)]))
    read_row = jnp.concatenate([readout[m : m + 1, :] for m in range(members)], axis=1)
    eye = (iota((width, width), 0) == iota((width, width), 1)).astype(f32)
    read = jnp.sum(eye * read_row, axis=1, keepdims=True)
    pull = jnp.sum(update1.T * read, axis=0, keepdims=True) * (energy_scale / NEIGH)
    columns[...] = jnp.broadcast_to(read * energy_scale, (width, LANES))
    factors = (
        0.5 * mix0.T, latent.T, 0.5 * mix1.T, 0.5 * mix1 * pull, latent, 0.5 * mix0,
        update0.T * (1.0 / NEIGH), update0 * (1.0 / NEIGH),
    )
    for at, matrix in enumerate(factors):
        dense[at] = split_left(matrix)


def factors_kernel(*refs):
    outs, held, sems = refs[6:10], refs[10:14], refs[14]
    weight_factors(*refs[:6], *held)
    copies = [pltpu.make_async_copy(src, dst, sems.at[k]) for k, (src, dst) in enumerate(zip(held, outs))]
    for copy in copies:
        copy.start()
    for copy in copies:
        copy.wait()


def lane_pick(table, lanes):
    return jnp.take_along_axis(table, jnp.broadcast_to(lanes, table.shape), axis=1, mode="promise_in_bounds")


def product(left, x):
    hi, lo = parts(x)
    return jnp.dot(left, jnp.concatenate([hi, lo, hi], axis=0), preferred_element_type=f32)


def sum_to(values, hot):
    hi, lo = parts(values) if values.shape[0] % 16 == 0 else halves(values)
    both = lax.dot_general(
        jnp.concatenate([hi, lo], axis=0).astype(bf16), hot, (((1,), (1,)), ((), ())), preferred_element_type=f32
    )
    return both[: values.shape[0]] + both[values.shape[0] :]


def silu(h):
    return h + h * jnp.tanh(h)


def silu_and_slope(h):
    t = jnp.tanh(h)
    p = 1.0 + t
    return h * p, p + p * (h - h * t)


def sin_cos(x):
    turns = jnp.floor(x * 0.15915494309189535 + 0.5)
    r = (x - turns * 6.28125) - turns * 1.9353071795864769e-3
    h = 0.5 * r
    q = h * h
    s = h * (1.0 + q * (-1 / 6 + q * (1 / 120 + q * (-1 / 5040 + q * (1 / 362880 + q * (-1 / 39916800 + q * (1 / 6227020800)))))))
    c = 1.0 + q * (-1 / 2 + q * (1 / 24 + q * (-1 / 720 + q * (1 / 40320 + q * (-1 / 3628800 + q * (1 / 479001600 - q * (1 / 87178291200)))))))
    return 2.0 * s * c, 1.0 - 2.0 * s * s


def force_kernel(wx, wy, place, n_in, *refs):
    arrived = refs[:n_in]
    factors_in, out = refs[n_in : n_in + 4], refs[n_in + 4]
    (raw, posb, lid_s, cl_s, spc, spn, unit, basis_s, slope_s, feats2, sums, grads, pulls,
     joined_s, lat_s, dpre_s, dz_s, back_s, total, tile_list, near_list,
     hold_a, hold_b, hold_hot, geo, dense, radial_back, columns, sems) = refs[n_in + 5 :]
    tiles = 8
    n_dom = wx * wy
    nv = (wy + 1) // 2
    n_src = 3 * nv
    n_blk = wx * nv
    width = feats2.shape[1] // 2
    members = out.shape[0]
    own_a, own_b, slots = place()

    copies = [
        pltpu.make_async_copy(arrived[ref].at[pl.ds(at * PACK_ROWS, PACK_ROWS), :], raw.at[slot], sems.at[k])
        for k, (ref, at, slot) in enumerate(slots)
    ]
    later = [pltpu.make_async_copy(src, dst, sems.at[n_dom + k]) for k, (src, dst) in enumerate(zip(factors_in, (geo, dense, radial_back, columns)))]
    for copy in copies + later:
        copy.start()
    none = n_dom * tiles
    lid_s[none : none + 8, :] = jnp.full((8, LANES), -1, i32)
    cl_s[none : none + 8, :] = jnp.full((8, LANES), -1, i32)
    for ref in (spc, spn):
        ref[none : none + 8, :] = jnp.zeros((8, LANES), i32)
    unit[:, none : none + 8, :] = jnp.zeros((3, 8, LANES), f32)
    basis_s[none * 8 : none * 8 + 16, :] = jnp.zeros((16, LANES), f32)
    slope_s[none * 8 : none * 8 + 16, :] = jnp.zeros((16, LANES), f32)
    for ref in (sums, grads):
        ref[...] = jnp.zeros(ref.shape, f32)
    for ref in (joined_s, lat_s, dpre_s, dz_s, back_s):
        ref[none : none + 2] = jnp.zeros((2, width, LANES), f32)
    total[...] = jnp.zeros(total.shape, f32)
    for copy in copies:
        copy.wait()

    pairs = CHUNK // 2
    count = jnp.int32(0)
    near = jnp.int32(0)
    for d in range(n_dom):
        a, b = d // wy, d % wy
        live = jnp.max(raw[d, 2 * tiles + 5 : 2 * tiles + 6, :]).astype(i32)
        live = lax.shift_right_logical(live + 1, 1)
        da = lax.rem(a - own_a + 1 + wx, wx)
        db = lax.rem(b - own_b + 1 + wy, wy)
        touches = jnp.logical_and(da < 3, db < 3)
        for t in range(tiles // 2):
            tile_list[count + t] = d * (tiles // 2) + t
            near_list[near + t] = d * (tiles // 2) + t
        count = count + live
        near = near + jnp.where(touches, live, 0)
    for t in range(pairs):
        tile_list[count + t] = none // 2
        near_list[near + t] = none // 2
    chunks = lax.div(count + (pairs - 1), pairs)
    near_chunks = lax.div(near + (pairs - 1), pairs)

    def tiles_of(ids, chunk):
        firsts = [ids[chunk * pairs + j] * 2 for j in range(pairs)]
        return [first + k for first in firsts for k in range(2)]

    def wide(p):
        return slice(p * 2 * LANES, (p + 1) * 2 * LANES)

    def cut(j):
        return slice(j * LANES, (j + 1) * LANES)

    lane = iota((8, LANES), 1)
    for a in range(wx):
        for v in range(nv):
            low = raw[a * wy + 2 * v, 2 * tiles : 2 * tiles + 8, :]
            high = raw[a * wy + min(2 * v + 1, wy - 1), 2 * tiles : 2 * tiles + 8, :]
            posb[a * nv + v] = jnp.where(lane < 64, low, high)

    row = lane[0:1]
    for d in range(n_dom):
        a, b = d // wy, d % wy

        def ids(u, v, start):
            src = ((a + u - 1) % wx) * wy + (b + v - 1) % wy
            base = u * nv * LANES + ((b + v - 1) % wy) * 64 + 8192 * v
            skin = raw[src, 2 * tiles + 4 : 2 * tiles + 5, :].astype(i32) + base
            return pltpu.roll(skin, start, 1) if start else skin

        first = row + (nv * LANES + b * 64 + 8192)
        first = jnp.where(row >= 64, ids(0, 1, 64), first)
        first = jnp.where(row >= 96, ids(1, 0, 96), first)
        second = ids(1, 2, 0)
        second = jnp.where(row >= 32, ids(2, 1, 32), second)
        for k, (u, v) in enumerate(((0, 0), (0, 2), (2, 0), (2, 2))):
            second = jnp.where(row >= 64 + 8 * k, ids(u, v, 64 + 8 * k), second)
        center = raw[d, 0:tiles, :].astype(i32)
        entry = raw[d, tiles : 2 * tiles, :].astype(i32)
        shape = (8, LANES)
        code = jnp.where(
            entry < LANES,
            lane_pick(jnp.broadcast_to(first, shape), entry & 127),
            lane_pick(jnp.broadcast_to(second, shape), entry & 127),
        )
        side_y = lax.shift_right_logical(code, 13)
        lid = code & 8191
        side_x = (lid >= nv * LANES).astype(f32) + (lid >= 2 * nv * LANES).astype(f32) - 1.0
        clid = center + b * 64
        block = lax.shift_right_logical(lid, 7)
        got_n, got_c = [], []
        for q in range(4):
            value = None
            for s in range(n_src):
                src = ((a + s // nv - 1) % wx) * nv + s % nv
                picked = lane_pick(jnp.broadcast_to(posb[src, q : q + 1, :], shape), lid & 127)
                value = picked if value is None else jnp.where(block == s, picked, value)
            got_n.append(value)
            got_c.append(lane_pick(jnp.broadcast_to(posb[a * nv + b // 2, q : q + 1, :], shape), clid & 127))
        dx = got_n[0] + box_edge * side_x - got_c[0]
        dy = got_n[1] + box_edge * (side_y.astype(f32) - 1.0) - got_c[1]
        dz = got_n[2] - got_c[2]
        distance = jnp.sqrt(dx * dx + dy * dy + dz * dz + 1.0)
        inverse = 1.0 / distance
        rows = slice(d * tiles, (d + 1) * tiles)
        for q, part in enumerate((dx, dy, dz)):
            unit[q, rows, :] = part * inverse
        spn[rows, :] = got_n[3].astype(i32)
        spc[rows, :] = got_c[3].astype(i32)
        live = iota(shape, 0).astype(f32) < raw[d, 2 * tiles + 5 : 2 * tiles + 6, :]
        lid_s[rows, :] = jnp.where(live, lid, -1)
        cl_s[rows, :] = jnp.where(live, clid, -1)
        s1, c1 = sin_cos(distance * 0.25)
        env = jnp.exp(distance * (-1.0 / 32.0))
        c_k, s_k = [jnp.ones_like(c1), c1], [jnp.zeros_like(s1), s1]
        for k in range(2, 8):
            c_k.append(2.0 * c1 * c_k[-1] - c_k[-2])
            s_k.append(2.0 * c1 * s_k[-1] - s_k[-2])
        for k in range(8):
            basis = c_k[k] * env
            basis_s[pl.ds(d * 64 + k, 8, stride=8), :] = basis
            slope_s[pl.ds(d * 64 + k, 8, stride=8), :] = s_k[k] * env * (-k / 4.0) - basis * (1.0 / 32.0)

    def spots(tau):
        d = lax.shift_right_logical(tau, 3)
        a, b = lax.div(d, wy), lax.rem(d, wy)
        sources = [lax.rem(a + (s // nv - 1 + wx), wx) * nv + s % nv for s in range(n_src)]
        home = lax.rem(a, wx) * nv + lax.div(b, 2)
        return sources, home, lax.div(b, 2)

    def ones_and_zeros(lanes):
        return iota((LANES, lanes), 0).astype(bf16), jnp.ones((LANES, lanes), bf16), jnp.zeros((LANES, lanes), bf16)

    def ids_of(ref, taus):
        return jnp.concatenate([ref[pl.ds(tau, 1), :] for tau in taus], axis=1)

    def hot(ids_row):
        atom, one, zero = ones_and_zeros(ids_row.shape[1])
        return jnp.where(atom == ids_row.astype(f32).astype(bf16), one, zero)

    def side(parts):
        return jnp.concatenate(parts, axis=1)

    def pipelined(step, ids, chunks):
        step(tiles_of(ids, 0), None)

        def both(chunk, carry):
            step(tiles_of(ids, chunk), tiles_of(ids, chunk - 1))
            return carry

        lax.fori_loop(1, chunks, both, 0)
        step(None, tiles_of(ids, chunks - 1))

    def forward(new, old):
        if old:
            old_latent = side([lat_s[tau] for tau in old])
            mixed = old_latent * side([joined_s[tau] for tau in old])
        if new:
            sub = iota((8, LANES), 0)
            rhs = []
            for tau in new:
                hi, lo = halves(basis_s[pl.ds(pl.multiple_of(tau * 8, 8), 8), :])
                kinds = (sub == spc[pl.ds(tau, 1), :]).astype(f32) + (sub == spn[pl.ds(tau, 1), :]).astype(f32)
                rhs.append(jnp.concatenate([hi, lo, hi, kinds, kinds, jnp.zeros_like(hi)], axis=0).astype(bf16))
        if old:
            homes, hots = [], []
            for p in range(pairs):
                _, home, half = spots(old[2 * p])
                homes.append(home)
                hots.append(hot(ids_of(cl_s, old[2 * p : 2 * p + 2]) - half * LANES))
            z = product(dense[0], mixed)
        if new:
            both = jnp.dot(geo[...], side(rhs), preferred_element_type=f32)
        if old:
            active, slope = silu_and_slope(z)
        if new:
            latent, latent_slope = silu_and_slope(both[:width])
        if old:
            added = [sum_to(active[:, wide(p)], hots[p]) for p in range(pairs)]
            old_latent = old_latent + product(dense[1], active)
        if new:
            for j, tau in enumerate(new):
                joined_s[tau] = both[width:, cut(j)]
                dpre_s[tau] = latent_slope[:, cut(j)]
                lat_s[tau] = latent[:, cut(j)]
        if old:
            for j, tau in enumerate(old):
                dz_s[tau] = slope[:, cut(j)]
                lat_s[tau] = old_latent[:, cut(j)]
            for p in range(pairs):
                sums[homes[p]] += added[p]

    for copy in later:
        copy.wait()
    pipelined(forward, tile_list, chunks)

    sub = iota((8, n_blk * LANES), 0)
    kinds = (sub == side([posb[k, 3:4, :] for k in range(n_blk)]).astype(i32)).astype(f32)
    empty = jnp.zeros_like(kinds)
    rhs = jnp.concatenate([empty, empty, empty, kinds, kinds, empty], axis=0).astype(bf16)
    start = jnp.dot(geo[...], rhs, preferred_element_type=f32)[width:]
    features = start + product(dense[6], side([sums[k] for k in range(n_blk)]))
    features = jnp.concatenate(parts(features), axis=0)
    for k in range(n_blk):
        feats2[k] = features[:, cut(k)]

    def middle(new, old):
        if old:
            old_joined, old_slope = hold_a[...], hold_b[...]
            old_hots = [hold_hot[p] for p in range(pairs)]
            old_latent = side([lat_s[tau] for tau in old])
            old_sources = [spots(old[2 * p])[0] for p in range(pairs)]
        if new:
            latent = side([lat_s[tau] for tau in new])
            joined, hots = [], []
            for p in range(pairs):
                sources, _, half = spots(new[2 * p])
                lid = ids_of(lid_s, new[2 * p : 2 * p + 2])
                own = hot(ids_of(cl_s, new[2 * p : 2 * p + 2]) - half * LANES)
                rows = [hot(lid - s * LANES) for s in range(n_src)]
                for v in range(nv):
                    rows[nv + v] = rows[nv + v] + (own if nv == 1 else jnp.where(half == v, own, jnp.zeros_like(own)))
                hots.append(jnp.concatenate(rows, axis=0))
                both = jnp.dot(side([feats2[s] for s in sources]), hots[-1], preferred_element_type=f32)
                joined.append(both[:width] + both[width:])
        if old:
            dmix = product(dense[3], old_slope)
        if new:
            joined = side(joined)
            z = product(dense[2], latent * joined)
        if old:
            spread = dmix * old_latent
            added = [sum_to(spread[:, wide(p)], old_hots[p]) for p in range(pairs)]
            back = dmix * old_joined
        if new:
            _, slope = silu_and_slope(z)
            hold_a[...] = joined
            hold_b[...] = slope
            for p in range(pairs):
                hold_hot[p] = hots[p]
        if old:
            for j, tau in enumerate(old):
                back_s[tau] = back[:, cut(j)]
            for p in range(pairs):
                for s in range(n_src):
                    grads[old_sources[p][s]] += added[p][:, cut(s)]

    pipelined(middle, tile_list, chunks)

    pulled_all = product(dense[7], side([grads[k] + columns[...] for k in range(n_blk)]))
    for k in range(n_blk):
        pulls[k] = pulled_all[:, cut(k)]

    own_block = own_a * nv + lax.div(own_b, 2)

    def backward(new, old):
        if old:
            old_pre = hold_a[...]
            slopes = [slope_s[pl.ds(pl.multiple_of(tau * 8, 8), 8), :] for tau in old]
            units = [[unit[q, pl.ds(tau, 1), :] for q in range(3)] for tau in old]
        if new:
            back = side([back_s[tau] for tau in new])
            dz = side([dz_s[tau] for tau in new])
            joined = side([joined_s[tau] for tau in new])
            dpre = side([dpre_s[tau] for tau in new])
            pulled = []
            for tau in new:
                _, home, _ = spots(tau)
                pulled.append(lane_pick(pulls[home], cl_s[pl.ds(tau, 1), :] & 127))
        if old:
            hits, chits = [], []
            for p in range(pairs):
                sources, home, half = spots(old[2 * p])
                lid = ids_of(lid_s, old[2 * p : 2 * p + 2])
                hit = jnp.full(lid.shape, -1, i32)
                for s in range(n_src):
                    this = jnp.where(sources[s] == own_block, s, -2)
                    hit = jnp.where(lax.shift_right_arithmetic(lid, 7) == this, lid & 127, hit)
                hits.append(hit)
                chits.append(jnp.where(home == own_block, ids_of(cl_s, old[2 * p : 2 * p + 2]) - half * LANES, -1))
            many = hot(side(hits)) - hot(side(chits))
            dbasis = product(radial_back[...], old_pre)
        if new:
            active = side(pulled) + product(dense[4], back)
        if old:
            moves = []
            for j in range(CHUNK):
                rows = []
                for m in range(members):
                    along = jnp.sum(dbasis[m * 8 : (m + 1) * 8, cut(j)] * slopes[j], axis=0, keepdims=True)
                    rows += [along * units[j][q] for q in range(3)]
                rows.append(jnp.zeros((8 - 3 * members, LANES), f32))
                moves.append(jnp.concatenate(rows, axis=0))
            added = sum_to(side(moves), many)
        if new:
            dmix = product(dense[5], active * dz)
            hold_a[...] = (back + dmix * joined) * dpre
        if old:
            total[...] += added

    pipelined(backward, near_list, near_chunks)

    result = -total[...]
    result = jnp.where(lax.rem(own_b, 2) == 1, pltpu.roll(result, 64, 1), result)
    for m in range(members):
        for q in range(3):
            out[m, q, 0] = result[m * 3 + q : m * 3 + q + 1, 0:64]


def window(size):
    return min(size, 2 * REACH + 1)


def shift(value, axis, by):
    peers = lax.axis_size(axis)
    return lax.ppermute(value, axis, [(i, (i + by) % peers) for i in range(peers)])


def swap(value, by_core):
    sizes = [lax.axis_size(axis) for axis in ("gx", "gy", "gz")]
    pairs = []
    for a in range(sizes[0]):
        for b in range(sizes[1]):
            for c in range(sizes[2]):
                dx, dy, dz = by_core[c]
                pairs.append(((a * sizes[1] + b) * sizes[2] + c, ((a ^ dx) * sizes[1] + (b ^ dy)) * sizes[2] + (c ^ dz)))
    return lax.ppermute(value, ("gx", "gy", "gz"), pairs)


def gathered(own, gx, gy):
    if gx == 4 and gy == 2 and lax.axis_size("gz") == 2:
        fetch = (((0, 1), (2, 1)), ((1, 0), (3, 0)), ((1, 1), (3, 1)))
        far = swap(own, ((2, 0, 0), (2, 0, 0)))
        fetched = [swap(own, (low + (0,), high + (0,))) for low, high in fetch]
        handed = [swap(value, ((0, 0, 1), (0, 0, 1))) for value in fetched]

        def place():
            a, b, c = lax.axis_index("gx"), lax.axis_index("gy"), lax.axis_index("gz")
            slots = [(0, 0, a * 2 + b), (1, 0, (a ^ 2) * 2 + b)]
            for k, (low, high) in enumerate(fetch):
                mine = [jnp.where(c == 0, low[q], high[q]) for q in range(2)]
                other = [jnp.where(c == 0, high[q], low[q]) for q in range(2)]
                slots.append((2 + k, 0, (a ^ mine[0]) * 2 + (b ^ mine[1])))
                slots.append((5 + k, 0, (a ^ other[0]) * 2 + (b ^ other[1])))
            return a, b, slots

        return [own, far] + fetched + handed, place
    wx, wy = window(gx), window(gy)
    steps = list(range(wy // 2 + 1)) + list(range(wy // 2 + 1 - wy, 0))
    column = jnp.concatenate([own if s == 0 else shift(own, "gy", -s) for s in steps], axis=0)
    steps_x = list(range(wx // 2 + 1)) + list(range(wx // 2 + 1 - wx, 0))
    arrays = [column if s == 0 else shift(column, "gx", -s) for s in steps_x]

    def place():
        slots = [(k, at, k * wy + at) for k in range(wx) for at in range(wy)]
        return jnp.int32(0), jnp.int32(0), slots

    return arrays, place


def on_device(
    positions, species, centers, neighbours, masks, skin, embed, radial, w_mix, w_latent, w_update, readout
):
    gx, gy = lax.axis_size("gx"), lax.axis_size("gy")
    atoms = positions.shape[-1]
    members, _, channels = embed.shape
    width = members * channels
    raw = [pltpu.with_memory_space_constraint(x, pltpu.HBM) for x in (positions, species, centers, neighbours, masks, skin)]
    own = pl.pallas_call(
        pack_kernel,
        out_shape=jax.ShapeDtypeStruct((PACK_ROWS, LANES), f32),
        in_specs=[pl.BlockSpec(memory_space=pltpu.VMEM)] * len(raw),
        out_specs=pl.BlockSpec(memory_space=pl.ANY),
        scratch_shapes=[pltpu.VMEM((PACK_ROWS, LANES), f32), pltpu.SemaphoreType.DMA],
        compiler_params=pltpu.CompilerParams(vmem_limit_bytes=16 * 1024 * 1024),
        name="pack",
    )(*raw)
    model = (jnp.transpose(embed, (1, 0, 2)), radial, w_mix, w_latent, w_update, readout)
    model = tuple(pltpu.with_memory_space_constraint(part, pltpu.HBM) for part in model)
    factors = (
        jax.ShapeDtypeStruct((2 * width, 48), bf16),
        jax.ShapeDtypeStruct((8, width, 3 * width), bf16),
        jax.ShapeDtypeStruct((members * 8, 3 * width), bf16),
        jax.ShapeDtypeStruct((width, LANES), f32),
    )
    factors = pl.pallas_call(
        factors_kernel,
        out_shape=factors,
        in_specs=[pl.BlockSpec(memory_space=pltpu.VMEM)] * len(model),
        out_specs=tuple([pl.BlockSpec(memory_space=pl.ANY)] * len(factors)),
        scratch_shapes=[pltpu.VMEM(part.shape, part.dtype) for part in factors] + [pltpu.SemaphoreType.DMA((len(factors),))],
        compiler_params=pltpu.CompilerParams(vmem_limit_bytes=16 * 1024 * 1024),
        cost_estimate=pl.CostEstimate(flops=2000000, bytes_accessed=500000, transcendentals=0),
        name="weights",
    )(*model)
    arrays, place = gathered(own, gx, gy)
    wx, wy = window(gx), window(gy)
    n_dom = wx * wy
    n_tiles = n_dom * 8
    n_blk = wx * ((wy + 1) // 2)
    held = 5 * (n_tiles + 2) * width * LANES * 4 + 12 * 1024 * 1024
    per_tile = pltpu.VMEM((n_tiles + 2, width, LANES), f32)
    per_block = pltpu.VMEM((n_blk, width, LANES), f32)
    row_ids = pltpu.VMEM((n_tiles + 8, LANES), i32)

    def body(*refs):
        force_kernel(wx, wy, place, len(arrays), *refs)

    return pl.pallas_call(
        body,
        out_shape=jax.ShapeDtypeStruct((members, 3, 1, 1, atoms), f32),
        scratch_shapes=[
            pltpu.VMEM((n_dom, PACK_ROWS, LANES), f32),
            pltpu.VMEM((n_blk, 8, LANES), f32),
            row_ids,
            row_ids,
            row_ids,
            row_ids,
            pltpu.VMEM((3, n_tiles + 8, LANES), f32),
            pltpu.VMEM((n_tiles * 8 + 16, LANES), f32),
            pltpu.VMEM((n_tiles * 8 + 16, LANES), f32),
            pltpu.VMEM((n_blk, 2 * width, LANES), bf16),
            per_block,
            per_block,
            per_block,
            per_tile,
            per_tile,
            per_tile,
            per_tile,
            per_tile,
            pltpu.VMEM((8, LANES), f32),
            pltpu.SMEM((n_tiles // 2 + CHUNK // 2 + 4,), i32),
            pltpu.SMEM((n_tiles // 2 + CHUNK // 2 + 4,), i32),
            pltpu.VMEM((width, CHUNK * LANES), f32),
            pltpu.VMEM((width, CHUNK * LANES), f32),
            pltpu.VMEM((CHUNK // 2, 3 * n_blk // wx * LANES, 2 * LANES), bf16),
        ]
        + [
            pltpu.VMEM((2 * width, 48), bf16),
            pltpu.VMEM((8, width, 3 * width), bf16),
            pltpu.VMEM((members * 8, 3 * width), bf16),
            pltpu.VMEM((width, LANES), f32),
        ]
        + [pltpu.SemaphoreType.DMA((n_dom + len(factors),))],
        in_specs=[pl.BlockSpec(memory_space=pl.ANY)] * (len(arrays) + len(factors)),
        compiler_params=pltpu.CompilerParams(vmem_limit_bytes=held),
        name="forces",
    )(*arrays, *factors)


def solution(mesh):
    return jax.shard_map(
        on_device,
        mesh=mesh,
        in_specs=(
            P(None, ("groups", "gx"), "gy", None),
            P(("groups", "gx"), "gy", None),
            P(("groups", "gx"), "gy", None),
            P(("groups", "gx"), "gy", None),
            P(("groups", "gx"), "gy", None),
            P(("groups", "gx"), "gy", None),
            P("gz", None, None),
            P("gz", None, None),
            P("gz", None, None, None),
            P("gz", None, None, None),
            P("gz", None, None, None),
            P("gz", None),
        ),
        out_specs=P("gz", None, ("groups", "gx"), "gy", None),
        check_vma=False,
    )
```
